128 devices in a mesh: dp: 32 (over x, y, core), seq: 4 (over z).
Axes of the slice: x: 4, y: 4, z: 4, core: 2. Of those that a mesh axis runs over, the one named last changes fastest.
Arguments:
- inputs: bfloat16 [2, 32, 512, 1024], P(None, 'dp', 'seq'), may hold values from -6 to 6
- starts: int32 [2, 32, 512], P(None, 'dp', 'seq'), may hold values from 0 to 511, as said below
- w_query: bfloat16 [1024, 1024], P('dp'), may hold values from -0.1875 to 0.1875
- key_weight: bfloat16 [1024, 512], P('dp'), may hold values from -0.1875 to 0.1875
- value_weight: bfloat16 [1024, 512], P('dp'), may hold values from -0.1875 to 0.1875
- w_out: bfloat16 [1024, 1024], P('dp'), may hold values from -0.75 to 0.75
- w_gate: bfloat16 [1024, 4608], P('dp'), may hold values from -0.1875 to 0.1875
- w_up: bfloat16 [1024, 4608], P('dp'), may hold values from -0.1875 to 0.1875
- w_down: bfloat16 [4608, 1024], P('dp'), may hold values from -0.09375 to 0.09375
- prenorm: bfloat16 [1024], P('dp'), may hold values from 0.5 to 1.5
- midnorm: bfloat16 [1024], P('dp'), may hold values from 0.5 to 1.5
- querynorm: bfloat16 [64], P('dp'), may hold values from 1 to 2
- keynorm: bfloat16 [64], P('dp'), may hold values from 1 to 2
- cotangent: bfloat16 [2, 32, 512, 1024], P(None, 'dp', 'seq'), may hold values from -6 to 6
Outputs:
- outputs: bfloat16 [2, 32, 512, 1024], P(None, 'dp', 'seq')
- grad_inputs: float32 [2, 32, 512, 1024], P(None, 'dp', 'seq')
- dw_query: float32 [1024, 1024], P('dp')
- dw_key: float32 [1024, 512], P('dp')
- dw_value: float32 [1024, 512], P('dp')
- dw_out: float32 [1024, 1024], P('dp')
- dw_gate: float32 [1024, 4608], P('dp')
- dw_up: float32 [1024, 4608], P('dp')
- dw_down: float32 [4608, 1024], P('dp')
- grad_prenorm: float32 [1024], P('dp')
- grad_midnorm: float32 [1024], P('dp')
- grad_querynorm: float32 [64], P('dp')
- grad_keynorm: float32 [64], P('dp')
The draws below stay inside these ranges and needn't reach their ends.
Inputs may be any that keep to these rules, and one draw needn't show every extreme that they name: Documents are contiguous: in each row a value is the first position that holds it and values never fall. One document of each row starts before position 64 and covers position 448; at most one short document precedes it and one short document follows it, ending the row.
All inputs are finite; a program needn't handle non-finite values.
Results may differ from the reference program's by a relative error of at most 0.04.
Values may be sent and summed in bfloat16 or wider, within the bound.
A program may use at most 192 MiB of HBM per device.

```python
import math
import jax
import jax.numpy as jnp
from jax import lax

MODEL_WIDTH = 1024
QUERY_HEADS = 16
KEY_VALUE_HEADS = 8
HEAD_SIZE = 64
FF = 4608
TOK_DEV = 128
MICRO = 2
ROW = 512
BATCH = 32


def draw_starts(key, part):
    key = jax.random.fold_in(key, 7)
    key_front, key_back = jax.random.split(key)
    half_tok = TOK_DEV // 2
    opening = jax.random.randint(key_front, (MICRO, BATCH, 1), 0, half_tok)
    closing = jax.random.randint(key_back, (MICRO, BATCH, 1), ROW - half_tok + 1, ROW)
    closing = closing.at[0, 0, 0].set(ROW - 1)
    positions = jnp.arange(ROW, dtype=jnp.int32)[None, None, :]
    return jnp.where(positions < opening, 0, jnp.where(positions < closing, opening, closing)).astype(jnp.int32)


def strengthened(entries, rng, source, target, blocks, factor):
    owner, partner = [(jnp.arange(entries.shape[position]) // (entries.shape[position] // blocks)).reshape([-1 if axis == position else 1 for axis in range(entries.ndim)]) for position in (source, target)]
    chosen = jax.random.permutation(rng, blocks)[partner]
    strong = (owner == chosen) | (owner == (partner + blocks // 2) % blocks)
    return jnp.where(strong, factor * entries, entries)


def block_levels(rng, extent, cuts, smallest, high):
    factor_of = 1.0
    for dim, blocks in cuts:
        steps = jax.random.uniform(jax.random.fold_in(jax.random.fold_in(rng, 6), dim), (blocks,), jnp.float32, smallest / len(cuts), high / len(cuts))
        factor_of = factor_of * jnp.repeat(jnp.exp(steps), extent[dim] // blocks).reshape((-1,) + (1,) * (len(extent) - 1 - dim))
    return factor_of


def centred(stream_key, shape, deviation, most, shards=(), kind=jnp.bfloat16):
    drawn = jax.random.normal(stream_key, shape, jnp.float32) * deviation
    if len(shards) > 0:
        drawn = block_levels(stream_key, shape, shards, -0.22, 0.18) * drawn
    return jnp.clip(drawn, min=-most, max=most).astype(kind)


def bell_draw_with(stream_key, dims, width, most, cuts, heavy, held_as=jnp.bfloat16):
    array = width * jax.random.normal(stream_key, dims, jnp.float32)
    if cuts:
        array = array * block_levels(stream_key, dims, cuts, -0.22, 0.18)
    return jnp.clip(strengthened(array, jax.random.fold_in(stream_key, 3), *heavy), -most, most).astype(held_as)


def setup_inputs(seed: int = 0) -> dict:
    keys = jax.random.split(jax.random.key(seed), 15)
    inputs = bell_draw_with(keys[0], (MICRO, BATCH, ROW, MODEL_WIDTH), 1.0, 6.0, ((1, 32), (2, 4)), (1, 3, 32, 2.75))
    starts = draw_starts(jax.random.fold_in(keys[14], 71), 0)
    w_query = centred(keys[2], (MODEL_WIDTH, QUERY_HEADS * HEAD_SIZE), MODEL_WIDTH ** -0.5, 0.1875, ((0, 32),))
    key_weight = centred(keys[3], (MODEL_WIDTH, KEY_VALUE_HEADS * HEAD_SIZE), MODEL_WIDTH ** -0.5, 0.1875, ((0, 32),))
    value_weight = centred(keys[4], (MODEL_WIDTH, KEY_VALUE_HEADS * HEAD_SIZE), MODEL_WIDTH ** -0.5, 0.1875, ((0, 32),))
    w_out = centred(keys[5], (QUERY_HEADS * HEAD_SIZE, MODEL_WIDTH), 64 ** -0.5, 0.75, ((0, 32),))
    w_gate = centred(keys[6], (MODEL_WIDTH, FF), MODEL_WIDTH ** -0.5, 0.1875, ((0, 32),))
    w_up = centred(keys[7], (MODEL_WIDTH, FF), MODEL_WIDTH ** -0.5, 0.1875, ((0, 32),))
    w_down = centred(keys[8], (FF, MODEL_WIDTH), FF ** -0.5, 0.09375, ((0, 32),))
    prenorm = jnp.clip(1.0 + 0.1 * jax.random.normal(keys[9], (MODEL_WIDTH,), jnp.float32), 0.5, 1.5).astype(jnp.bfloat16)
    midnorm = jnp.clip(1.0 + 0.1 * jax.random.normal(keys[10], (MODEL_WIDTH,), jnp.float32), 0.5, 1.5).astype(jnp.bfloat16)
    querynorm = jnp.clip(1.0 + 1.0 * jax.random.uniform(keys[11], (HEAD_SIZE,), jnp.float32) ** block_levels(keys[11], (HEAD_SIZE,), ((0, 32),), -0.2, 0.2), 1.0, 2.0).astype(jnp.bfloat16)
    keynorm = jnp.clip(1.0 + 1.0 * jax.random.uniform(keys[12], (HEAD_SIZE,), jnp.float32) ** block_levels(keys[12], (HEAD_SIZE,), ((0, 32),), -0.2, 0.2), 1.0, 2.0).astype(jnp.bfloat16)
    cotangent = centred(keys[13], (MICRO, BATCH, ROW, MODEL_WIDTH), 1.0, 6.0, ((1, 32), (2, 4)))
    return dict(inputs=inputs, starts=starts, w_query=w_query, key_weight=key_weight, value_weight=value_weight, w_out=w_out, w_gate=w_gate, w_up=w_up, w_down=w_down, prenorm=prenorm, midnorm=midnorm, querynorm=querynorm, keynorm=keynorm, cotangent=cotangent)


EPS = 1e-05
ROPE_BASE = 1000000.0
HIGH = lax.Precision.HIGHEST

@jax.custom_vjp
def low(v):
    return lax.optimization_barrier(v.astype(jnp.bfloat16)).astype(jnp.float32)

@jax.custom_vjp
def lower_backward(v):
    return v

def low_keep(v):
    return (low(v), None)

def low_pass(kept, grad):
    return (grad,)

def back_keep(v):
    return (v, None)

def back_low(kept, grad):
    return (low(grad),)
low.defvjp(low_keep, low_pass)
lower_backward.defvjp(back_keep, back_low)

def root_mean_norm(source, gain_vector):
    return source * lax.rsqrt(lax.optimization_barrier(jnp.mean(source * source, axis=-1, keepdims=True)) + EPS) * gain_vector

def rotary_apply(source, inside_document):
    half_dim = source.shape[-1] // 2
    frequency = ROPE_BASE ** (-(jnp.arange(half_dim, dtype=jnp.float32) * 2.0 / source.shape[-1]))
    angles = inside_document.astype(jnp.float32)[:, None] * frequency[None, :]
    cosine = jnp.cos(angles)[:, None, :]
    sine = jnp.sin(angles)[:, None, :]
    leading = source[..., :half_dim]
    trailing = source[..., half_dim:]
    return jnp.concatenate([leading * cosine - trailing * sine, trailing * cosine + leading * sine], axis=-1)

def product_exact(left, right):
    return jnp.dot(left, right, precision=HIGH, preferred_element_type=jnp.float32)

def attend(query_rows, key_rows, value_matrix, starts):
    sequence_length = query_rows.shape[0]
    token_extent = min(512, sequence_length)
    grouped_rows = query_rows.reshape(sequence_length // token_extent, token_extent, KEY_VALUE_HEADS, QUERY_HEADS // KEY_VALUE_HEADS, HEAD_SIZE)
    positions = jnp.arange(sequence_length, dtype=jnp.int32)

    @jax.checkpoint
    def attend_block(pieces):
        query_block, query_pos, query_start = pieces
        scores = jnp.einsum('bkgd,tkd->kgbt', query_block, key_rows, precision=HIGH)
        scores = lower_backward(scores)
        allowed = (positions[None, :] <= query_pos[:, None]) & (positions[None, :] >= query_start[:, None])
        scores = jnp.where(allowed, scores, -1e+30)
        largest = lax.optimization_barrier(jnp.max(scores, axis=-1, keepdims=True))
        raised = jnp.exp(scores - largest)
        chances = low(raised / lax.optimization_barrier(jnp.sum(raised, axis=-1, keepdims=True)))
        return jnp.einsum('kgbt,tkd->bkgd', chances, value_matrix, precision=HIGH)
    mixed = lax.map(attend_block, (grouped_rows, positions.reshape(-1, token_extent), starts.reshape(-1, token_extent)))
    return mixed.reshape(sequence_length, QUERY_HEADS * HEAD_SIZE)

def layer_row(params, inputs, starts):
    w_query, key_weight, value_weight, w_out, w_gate, w_up, w_down, prenorm, midnorm, querynorm, keynorm = params
    sequence_length = inputs.shape[0]
    inside_document = jnp.arange(sequence_length, dtype=jnp.int32) - starts
    normalized = low(root_mean_norm(inputs, prenorm))
    lin_query = lower_backward(product_exact(normalized, w_query)).reshape(sequence_length, QUERY_HEADS, HEAD_SIZE)
    linear_key = lower_backward(product_exact(normalized, key_weight)).reshape(sequence_length, KEY_VALUE_HEADS, HEAD_SIZE)
    linear_value = lower_backward(product_exact(normalized, value_weight)).reshape(sequence_length, KEY_VALUE_HEADS, HEAD_SIZE)
    query_rows = low(rotary_apply(root_mean_norm(lin_query, querynorm), inside_document) * HEAD_SIZE ** (-0.5))
    key_rows = low(rotary_apply(root_mean_norm(linear_key, keynorm), inside_document))
    value_matrix = low(linear_value)
    mixed = low(lower_backward(attend(query_rows, key_rows, value_matrix, starts)))
    middle = inputs + lower_backward(product_exact(mixed, w_out))
    normed_ffn = low(root_mean_norm(middle, midnorm))
    gated = lower_backward(product_exact(normed_ffn, w_gate))
    upward = lower_backward(product_exact(normed_ffn, w_up))
    hidden = low(jax.nn.silu(gated) * upward)
    return middle + product_exact(hidden, w_down)

def reference(inputs, starts, w_query, key_weight, value_weight, w_out, w_gate, w_up, w_down, prenorm, midnorm, querynorm, keynorm, cotangent):
    params = tuple((p.astype(jnp.float32) for p in (w_query, key_weight, value_weight, w_out, w_gate, w_up, w_down, prenorm, midnorm, querynorm, keynorm)))
    rows_all = MICRO * BATCH
    group_rows = math.gcd(rows_all, max(1, 4096 // ROW))
    flat_in = inputs.astype(jnp.float32).reshape(rows_all // group_rows, group_rows, ROW, MODEL_WIDTH)
    flat_start = starts.reshape(rows_all // group_rows, group_rows, ROW)
    flat_cot = cotangent.astype(jnp.float32).reshape(rows_all // group_rows, group_rows, ROW, MODEL_WIDTH)

    def scan_step(totals, pieces):
        source, begin, upstream = pieces

        def forward(params_in, source_in):
            return jax.vmap(layer_row, (None, 0, 0))(params_in, source_in, begin)
        result, pull = jax.vjp(forward, params, source)
        grads, grad_source = pull(upstream)
        return (jax.tree.map(jnp.add, totals, grads), (result, grad_source))
    zeros = tuple((jnp.zeros(p.shape, jnp.float32) for p in params))
    totals, (results, grad_sources) = lax.scan(scan_step, zeros, (flat_in, flat_start, flat_cot))
    outputs = results.reshape(MICRO, BATCH, ROW, MODEL_WIDTH).astype(jnp.bfloat16)
    grad_inputs = grad_sources.reshape(MICRO, BATCH, ROW, MODEL_WIDTH)
    return (outputs, grad_inputs, totals[0], totals[1], totals[2], totals[3], totals[4], totals[5], totals[6], totals[7], totals[8], totals[9], totals[10])
```

```python
from functools import partial

import jax
import jax.numpy as jnp
from jax import lax
from jax.experimental import pallas as pl
from jax.experimental.pallas import tpu as pltpu
from jax.sharding import PartitionSpec as P

QUERY_HEADS = 16
KEY_VALUE_HEADS = 8
HEAD_SIZE = 64
EPS = 1e-05
ROPE_BASE = 1000000.0

MESH = pl.DeviceIdType.MESH
BF = jnp.bfloat16
F32 = jnp.float32
WA = 3200
GU = 2304
DN = 144


class Links:
    def __init__(self, send, recv, local):
        dp = lax.axis_index("dp")
        self.z = lax.axis_index("seq")
        self.x, self.y, self.c = dp // 8, (dp // 2) % 4, dp % 2
        self.send, self.recv, self.local = send, recv, local
        self.n = self.m = 0
        self.out = []

    def dev(self, x, y, c, z):
        return ((x * 4 + y) * 2 + c, z)

    def nbr(self, axis, step):
        x, y, c, z = self.x, self.y, self.c, self.z
        if axis == "x":
            x = (x + step + 4) % 4
        elif axis == "y":
            y = (y + step + 4) % 4
        elif axis == "z":
            z = (z + step + 4) % 4
        else:
            c = 1 - c
        return self.dev(x, y, c, z)

    def sides(self, axis):
        return self.nbr(axis, 1), self.nbr(axis, -1)

    def barrier(self, axes):
        sem = pltpu.get_barrier_semaphore()
        count = 0
        for axis in axes:
            for step in (1,) if axis == "c" else (1, -1):
                pl.semaphore_signal(sem, inc=1, device_id=self.nbr(axis, step), device_id_type=MESH)
                count += 1
        pl.semaphore_wait(sem, count)

    def make(self, src, dst, to):
        copy = pltpu.make_async_remote_copy(
            src_ref=src,
            dst_ref=dst,
            send_sem=self.send.at[self.n],
            recv_sem=self.recv.at[self.n],
            device_id=to,
            device_id_type=MESH,
        )
        self.n += 1
        return copy

    def put(self, src, dst, to):
        copy = self.make(src, dst, to)
        copy.start()
        self.out.append(copy)
        return copy

    def keep(self, src, dst):
        copy = pltpu.make_async_copy(src, dst, self.local.at[self.m])
        self.m += 1
        copy.start()
        return copy

    def flush(self):
        for copy in self.out:
            copy.wait_send()
        self.out = []


def drive(*steps):
    steps = list(steps)
    while steps:
        steps = [s for s in steps if next(s, "end") != "end"]


def ring_gather(lk, own, slot, part, axis, me, ready=None):
    right, left = lk.sides(axis)
    before, after, far = (me + 3) % 4, (me + 1) % 4, (me + 2) % 4
    a = lk.put(own, slot(me), right)
    b = lk.put(own, slot(me), left)
    yield 1
    a.wait_recv()
    c = lk.put(part(before, 0), part(before, 0), right)
    if ready:
        ready(before)
    b.wait_recv()
    d = lk.put(part(after, 1), part(after, 1), left)
    if ready:
        ready(after)
    yield 1
    c.wait_recv()
    d.wait_recv()
    if ready:
        ready(far)


def plane_gather(lk, own, out, first, lo, hi):
    cols = pl.ds(lo, hi - lo)
    x, y, c = lk.x, lk.y, lk.c
    kept = lk.keep(own.at[:, cols], out.at[x, y, c, :, cols])
    crossing = []

    def cross(ref):
        crossing.append(lk.put(ref, ref, lk.nbr("c", 1)))

    def rows(k):
        return pl.ds(16 * k, 16)

    def two(k):
        return pl.ds(2 * k, 2)

    if first == "x":
        yield from ring_gather(
            lk, own.at[:, cols], lambda i: out.at[i, y, c, :, cols],
            lambda i, k: out.at[i, y, c, rows(k), cols], "x", x,
        )
        kept.wait()
        whole = out.at[:, y, c, :, cols]
        cross(whole)
        yield from ring_gather(
            lk, whole, lambda j: out.at[:, j, c, :, cols],
            lambda j, k: out.at[two(k), j, c, :, cols], "y", y,
            lambda j: cross(out.at[:, j, c, :, cols]),
        )
    else:
        yield from ring_gather(
            lk, own.at[:, cols], lambda j: out.at[x, j, c, :, cols],
            lambda j, k: out.at[x, j, c, rows(k), cols], "y", y,
        )
        kept.wait()
        whole = out.at[x, :, c, :, cols]
        cross(whole)
        yield from ring_gather(
            lk, whole, lambda i: out.at[i, :, c, :, cols],
            lambda i, k: out.at[i, two(k), c, :, cols], "x", x,
            lambda i: cross(out.at[i, :, c, :, cols]),
        )
    yield 1
    for copy in crossing:
        copy.wait_recv()


def ring_spread(lk, own, dst, part, axis, place):
    right, left = lk.sides(axis)
    a, b = lk.make(own, dst, right), lk.make(own, dst, left)
    c, d = lk.make(part(0), part(0), right), lk.make(part(1), part(1), left)
    kept = pltpu.make_async_copy(own, dst, lk.local.at[lk.m])
    lk.m += 1

    @pl.when(place == 0)
    def _():
        a.start()
        b.start()
        kept.start()

    yield 1

    @pl.when(place == 1)
    def _():
        a.wait_recv()
        c.start()

    @pl.when(place == 3)
    def _():
        b.wait_recv()
        d.start()

    yield 1

    @pl.when(place == 2)
    def _():
        c.wait_recv()
        d.wait_recv()

    @pl.when(place == 0)
    def _():
        kept.wait()
        a.wait_send()
        b.wait_send()

    @pl.when(place == 1)
    def _():
        c.wait_send()

    @pl.when(place == 3)
    def _():
        d.wait_send()


def down_part(k):
    return pl.ds(0, 80) if k == 0 else pl.ds(80, 64)


def down_gather(lk, own, out):
    y, c = lk.y, lk.c
    yield from ring_spread(
        lk, own, out.at[y, c], lambda k: out.at[y, c, down_part(k)], "x", (lk.x - lk.z + 4) % 4
    )
    crossing = []

    def cross(j):
        crossing.append(lk.put(out.at[j, c], out.at[j, c], lk.nbr("c", 1)))

    cross(y)
    yield from ring_gather(
        lk, out.at[y, c], lambda j: out.at[j, c], lambda j, k: out.at[j, c, down_part(k)], "y", y, cross
    )
    yield 1
    for copy in crossing:
        copy.wait_recv()


def line_gather(lk, own, out, cut):
    z, rows = lk.z, own.shape[0]
    kept = lk.keep(own, out.at[z])

    def part(i, k):
        return out.at[i, pl.ds(0, cut)] if k == 0 else out.at[i, pl.ds(cut, rows - cut)]

    yield from ring_gather(lk, own, lambda i: out.at[i], part, "z", z)
    kept.wait()


def add_into(dst, src):
    if len(dst.shape) == 2:
        dst[...] = (dst[...].astype(F32) + src[...].astype(F32)).astype(BF)
    else:
        for i in range(dst.shape[0]):
            dst[i] = (dst[i].astype(F32) + src[i].astype(F32)).astype(BF)


def ring_reduce(lk, p, part, bufs, axis, me):
    right, left = lk.sides(axis)
    r0, r1, ra, rb = bufs
    before, after, far = (me + 3) % 4, (me + 1) % 4, (me + 2) % 4
    a = lk.put(part(far, 0), r0, right)
    b = lk.put(part(far, 1), r1, left)
    yield 1
    a.wait_recv()
    add_into(part(after, 0), r0)
    c = lk.put(p(after), ra, right)
    b.wait_recv()
    add_into(part(before, 1), r1)
    d = lk.put(p(before), rb, left)
    yield 1
    c.wait_recv()
    add_into(p(me), ra)
    d.wait_recv()
    add_into(p(me), rb)


def plane_reduce(lk, part_hbm, acc, sib, bufs, out, first, lo, hi):
    cols = pl.ds(lo, hi - lo)
    x, y, c = lk.x, lk.y, lk.c
    one, two = bufs
    kept = lk.keep(part_hbm.at[:, :, c, :, cols], acc)
    got = lk.put(part_hbm.at[:, :, 1 - c, :, cols], sib, lk.nbr("c", 1))
    yield 1
    kept.wait()
    got.wait_recv()

    def step(i, _):
        acc[i // 4, i % 4] = (acc[i // 4, i % 4].astype(F32) + sib[i // 4, i % 4].astype(F32)).astype(BF)
        return 0

    lax.fori_loop(0, 16, step, 0)

    def pair(k):
        return pl.ds(2 * k, 2)

    def rows(k):
        return pl.ds(16 * k, 16)

    if first == "y":
        yield from ring_reduce(
            lk, lambda j: acc.at[:, j], lambda j, k: acc.at[pair(k), j], one, "y", y
        )
        yield from ring_reduce(
            lk, lambda i: acc.at[i, y], lambda i, k: acc.at[i, y, rows(k)], two, "x", x
        )
    else:
        yield from ring_reduce(
            lk, lambda i: acc.at[i], lambda i, k: acc.at[i, pair(k)], one, "x", x
        )
        yield from ring_reduce(
            lk, lambda j: acc.at[x, j], lambda j, k: acc.at[x, j, rows(k)], two, "y", y
        )
    done = lk.keep(acc.at[x, y], out.at[:, cols])
    yield 1
    done.wait()


def plane_scratch(cols):
    return [
        pltpu.VMEM((4, 4, 32, cols), BF),
        pltpu.VMEM((4, 4, 32, cols), BF),
        pltpu.VMEM((2, 32, cols), BF),
        pltpu.VMEM((2, 32, cols), BF),
        pltpu.VMEM((4, 32, cols), BF),
        pltpu.VMEM((4, 32, cols), BF),
        pltpu.VMEM((16, cols), BF),
        pltpu.VMEM((16, cols), BF),
        pltpu.VMEM((32, cols), BF),
        pltpu.VMEM((32, cols), BF),
    ]


def plane_pick(s):
    return s[0], s[1], (s[2:6], s[6:10])


def down_scratch():
    return [
        pltpu.VMEM((4, DN, 1024), BF),
        pltpu.VMEM((4, DN, 1024), BF),
        pltpu.VMEM((80, 1024), BF),
        pltpu.VMEM((64, 1024), BF),
        pltpu.VMEM((DN, 1024), BF),
        pltpu.VMEM((DN, 1024), BF),
        pltpu.VMEM((80, 1024), BF),
        pltpu.VMEM((64, 1024), BF),
        pltpu.VMEM((DN, 1024), BF),
        pltpu.VMEM((DN, 1024), BF),
    ]


def down_reduce(lk, part_hbm, s, out):
    acc, sib, one, (x0, x1, xa, xb) = s[0], s[1], s[2:6], s[6:10]
    y, c = lk.y, lk.c
    kept = lk.keep(part_hbm.at[:, c], acc)
    got = lk.put(part_hbm.at[:, 1 - c], sib, lk.nbr("c", 1))
    yield 1
    kept.wait()
    got.wait_recv()
    add_into(acc, sib)
    yield from ring_reduce(
        lk, lambda j: acc.at[j], lambda j, k: acc.at[j, down_part(k)], one, "y", y
    )
    mine = acc.at[y]
    right, left = lk.sides("x")
    place = (lk.x - lk.z + 4) % 4
    a = lk.make(acc.at[y, down_part(0)], x0, left)
    b = lk.make(acc.at[y, down_part(1)], x1, right)
    e = lk.make(mine, xa, left)
    f = lk.make(mine, xb, right)

    @pl.when(place == 2)
    def _():
        a.start()
        b.start()

    yield 1

    @pl.when(place == 1)
    def _():
        a.wait_recv()
        add_into(acc.at[y, down_part(0)], x0)
        e.start()

    @pl.when(place == 3)
    def _():
        b.wait_recv()
        add_into(acc.at[y, down_part(1)], x1)
        f.start()

    yield 1

    @pl.when(place == 0)
    def _():
        e.wait_recv()
        add_into(mine, xa)
        f.wait_recv()
        add_into(mine, xb)

    @pl.when(place == 1)
    def _():
        e.wait_send()

    @pl.when(place == 3)
    def _():
        f.wait_send()

    @pl.when(place == 2)
    def _():
        a.wait_send()
        b.wait_send()

    yield from ring_spread(
        lk, mine, out, lambda k: out.at[down_part(k)], "z", (lk.z - lk.x + 4) % 4
    )


ANY = pl.BlockSpec(memory_space=pl.ANY)


def sems(n):
    return [pltpu.SemaphoreType.DMA((n,)), pltpu.SemaphoreType.DMA((n,)), pltpu.SemaphoreType.DMA((16,))]


def params(number):
    return pltpu.CompilerParams(collective_id=number, has_side_effects=True, vmem_limit_bytes=56 * 2**20)


def shape(*dims, dtype=BF):
    return jax.ShapeDtypeStruct(dims, dtype)


def gather_kernel(wa, gu, dn, x, cot, st, WAo, GUo, DNo, Xo, COTo, STo, send, recv, local):
    lk = Links(send, recv, local)
    lk.barrier("xyzc")
    drive(
        plane_gather(lk, wa, WAo, "x", 0, 1536),
        plane_gather(lk, wa, WAo, "y", 1536, WA),
        line_gather(lk, st, STo, 8),
        line_gather(lk, x, Xo, 128),
    )
    drive(
        plane_gather(lk, gu, GUo, "x", 0, 1152),
        plane_gather(lk, gu, GUo, "y", 1152, GU),
        down_gather(lk, dn, DNo),
        line_gather(lk, cot, COTo, 128),
    )
    lk.flush()


def gather_all(wa, gu, dn, x, cot, st):
    return pl.pallas_call(
        gather_kernel,
        out_shape=(
            shape(4, 4, 2, 32, WA), shape(4, 4, 2, 32, GU), shape(4, 2, DN, 1024),
            shape(4, 256, 1024), shape(4, 256, 1024), shape(4, 16, 128, dtype=F32),
        ),
        in_specs=[ANY] * 6,
        out_specs=[ANY] * 6,
        scratch_shapes=sems(96),
        compiler_params=params(0),
    )(wa, gu, dn, x, cot, st)


def line_kernel(a, out, send, recv, local):
    lk = Links(send, recv, local)
    lk.barrier("z")
    drive(line_gather(lk, a, out, 128))
    lk.flush()


def gather_line(a):
    return pl.pallas_call(
        line_kernel,
        out_shape=shape(4, *a.shape),
        in_specs=[ANY],
        out_specs=ANY,
        scratch_shapes=sems(8),
        compiler_params=params(1),
    )(a)


def line_reduce(lk, part_hbm, s, out):
    acc, bufs = s[0], s[1:5]
    z = lk.z
    kept = lk.keep(part_hbm, acc)
    kept.wait()

    def part(i, k):
        return acc.at[i, pl.ds(128 * k, 128)]

    yield from ring_reduce(lk, lambda i: acc.at[i], part, bufs, "z", z)
    done = lk.keep(acc.at[z], out)
    yield 1
    done.wait()


def line_scratch():
    return [
        pltpu.VMEM((4, 256, 1024), BF),
        pltpu.VMEM((128, 1024), BF),
        pltpu.VMEM((128, 1024), BF),
        pltpu.VMEM((256, 1024), BF),
        pltpu.VMEM((256, 1024), BF),
    ]


def line_reduce_kernel(number, *refs):
    ins, outs, refs = refs[:number], refs[number : 2 * number], refs[2 * number :]
    send, recv, local = refs[:3]
    lk = Links(send, recv, local)
    lk.barrier("z")
    drive(*[line_reduce(lk, ins[i], refs[3 + 5 * i : 8 + 5 * i], outs[i]) for i in range(number)])
    lk.flush()


def reduce_line(cid, *arrays):
    n = len(arrays)
    return pl.pallas_call(
        partial(line_reduce_kernel, n),
        out_shape=[shape(256, 1024) for _ in arrays],
        in_specs=[ANY] * n,
        out_specs=[ANY] * n,
        scratch_shapes=sems(8 * n) + line_scratch() * n,
        compiler_params=params(cid),
    )(*arrays)


def reduce_kernel(ga, ggu, gdn, aw, guw, dnw, a_own, gu_own, *refs):
    send, recv, local = refs[:3]
    lk = Links(send, recv, local)
    lk.barrier("xyzc")
    s = refs[3:]
    q = [s[10 * i : 10 * i + 10] for i in range(5)]

    def plane(src, k, own, first, lo, hi):
        acc, sib, bufs = plane_pick(q[k])
        return plane_reduce(lk, src, acc, sib, bufs, own, first, lo, hi)

    drive(
        plane(ggu, 0, gu_own, "y", 0, 1152),
        plane(ggu, 1, gu_own, "x", 1152, GU),
        down_reduce(lk, gdn, q[4], dnw),
    )
    drive(
        plane(ga, 2, a_own, "y", 0, 1536),
        plane(ga, 3, a_own, "x", 1536, WA),
        line_gather(lk, gu_own, guw, 16),
    )
    drive(line_gather(lk, a_own, aw, 16))
    lk.flush()


def reduce_all(ga, ggu, gdn):
    out = pl.pallas_call(
        reduce_kernel,
        out_shape=(
            shape(4, 32, WA), shape(4, 32, GU), shape(DN, 1024), shape(32, WA), shape(32, GU),
        ),
        in_specs=[ANY] * 3,
        out_specs=[ANY] * 5,
        scratch_shapes=sems(96)
        + plane_scratch(1152) + plane_scratch(1152) + plane_scratch(1536) + plane_scratch(WA - 1536)
        + down_scratch(),
        compiler_params=params(2),
    )(ga, ggu, gdn)
    return out[:3]


def root_mean_norm(source, gain_vector):
    return source * lax.rsqrt(jnp.mean(source * source, axis=-1, keepdims=True) + EPS) * gain_vector


def rotary_apply(source, inside_document):
    half_dim = source.shape[-1] // 2
    frequency = ROPE_BASE ** (-(jnp.arange(half_dim, dtype=jnp.float32) * 2.0 / source.shape[-1]))
    angles = inside_document.astype(jnp.float32)[..., None] * frequency
    cosine = jnp.cos(angles)[..., None, :]
    sine = jnp.sin(angles)[..., None, :]
    leading = source[..., :half_dim]
    trailing = source[..., half_dim:]
    return jnp.concatenate(
        [leading * cosine - trailing * sine, trailing * cosine + leading * sine], axis=-1
    )


def query_piece(linear, gain_vector, inside_document):
    linear = linear.reshape(2, -1, QUERY_HEADS, HEAD_SIZE)
    return rotary_apply(root_mean_norm(linear, gain_vector), inside_document) * HEAD_SIZE ** (-0.5)


def key_piece(linear, gain_vector, inside_document):
    linear = linear.reshape(2, -1, KEY_VALUE_HEADS, HEAD_SIZE)
    return rotary_apply(root_mean_norm(linear, gain_vector), inside_document)


def dot(left, right, dims=((1,), (0,)), kind=F32):
    return lax.dot_general(left, right, (dims, ((), ())), preferred_element_type=F32).astype(kind)


TOKENS = ((0,), (0,))
ROWS = ((1,), (1,))


def body(
    inputs, starts, w_query, key_weight, value_weight, w_out, w_gate, w_up, w_down,
    prenorm, midnorm, querynorm, keynorm, cotangent,
):
    z = lax.axis_index("seq")
    gains = jnp.zeros((32, 128), BF)
    gains = gains.at[:, 0].set(prenorm).at[:, 1].set(midnorm)
    gains = gains.at[:2, 2].set(querynorm).at[:2, 3].set(keynorm)
    wa = jnp.concatenate([w_query, key_weight, value_weight, w_out, gains], axis=1)
    gu = jnp.concatenate(
        [lax.dynamic_slice(w, (0, z * 1152), (32, 1152)) for w in (w_gate, w_up)], axis=1
    )
    begin = jnp.pad(starts[:, 0].astype(F32), ((0, 14), (0, 0)))
    source = inputs.reshape(256, 1024)
    upstream = cotangent.reshape(256, 1024)
    whole, gate_up, down, sources, cots, begins = gather_all(wa, gu, w_down, source, upstream, begin)
    whole = whole.reshape(1024, WA)
    gate_up = gate_up.reshape(1024, GU)
    down = down.reshape(1152, 1024)
    cots = cots.reshape(1024, 1024)
    wqkv, wo = whole[:, :2048], whole[:, 2048:3072]
    gain = whole[:, 3072:3076].astype(F32)
    pre, mid = gain[:, 0], gain[:, 1]
    qn, kn = [gain[:, i].reshape(32, 32)[:, :2].reshape(64) for i in (2, 3)]

    begins = begins[:, :2].astype(jnp.int32).transpose(1, 0, 2).reshape(2, 512)
    inside_all = jnp.arange(512, dtype=jnp.int32) - begins
    pos = z * 128 + jnp.arange(128, dtype=jnp.int32)
    inside = pos - starts[:, 0]
    rows = sources.reshape(4, 2, 128, 1024).transpose(1, 0, 2, 3).reshape(1024, 1024)
    normed_all = root_mean_norm(rows.astype(F32), pre).astype(BF)
    source32 = source.astype(F32)
    normed = root_mean_norm(source32, pre).astype(BF)
    lin = dot(normed, wqkv)
    lin_query, lin_key = lin[:, :1024], lin[:, 1024:1536]
    lin_kv = dot(normed_all, wqkv[:, 1024:])
    queries = query_piece(lin_query, qn, inside).astype(BF)
    keys = key_piece(lin_kv[:, :512], kn, inside_all).astype(BF)
    values = lin_kv[:, 512:].reshape(2, 512, KEY_VALUE_HEADS, HEAD_SIZE).astype(BF)
    grouped = queries.reshape(2, 128, KEY_VALUE_HEADS, 2, HEAD_SIZE)
    key_pos = jnp.arange(512, dtype=jnp.int32)
    allowed = (key_pos <= pos[None, :, None]) & (key_pos >= starts[:, 0][:, :, None])
    allowed = allowed[:, None, None]
    scores = jnp.einsum("mbkgd,mtkd->mkgbt", grouped, keys, preferred_element_type=F32)
    scores = jnp.where(allowed, scores, -1e30)
    raised = jnp.exp(scores - jnp.max(scores, axis=-1, keepdims=True))
    chances = raised / jnp.sum(raised, axis=-1, keepdims=True)
    chances_low = chances.astype(BF)
    mixed = jnp.einsum("mkgbt,mtkd->mbkgd", chances_low, values, preferred_element_type=F32)
    mixed = mixed.reshape(256, 1024).astype(BF)
    middle = source32 + dot(mixed, wo)
    normed_ffn = root_mean_norm(middle, mid).astype(BF)

    ffn_all = gather_line(normed_ffn).reshape(1024, 1024)
    lin_ffn = dot(ffn_all, gate_up)
    gated, upward = lin_ffn[:, :1152], lin_ffn[:, 1152:]
    sigma = jax.nn.sigmoid(gated)
    hidden = (gated * sigma * upward).astype(BF)
    out_part = dot(hidden, down, kind=BF).reshape(4, 256, 1024)
    grad_down = dot(hidden, cots, TOKENS, BF).reshape(4, 2, DN, 1024)
    grad_hidden = dot(cots, down, ROWS)
    grad_gated = (grad_hidden * upward * sigma * (1.0 + gated * (1.0 - sigma))).astype(BF)
    grad_upward = (grad_hidden * gated * sigma).astype(BF)
    grad_both = jnp.concatenate([grad_gated, grad_upward], axis=1)
    grad_gu = dot(ffn_all, grad_both, TOKENS, BF).reshape(4, 4, 2, 32, GU)
    grad_ffn_part = dot(grad_both, gate_up, ROWS, BF).reshape(4, 256, 1024)
    out_sum, grad_ffn = reduce_line(3, out_part, grad_ffn_part)
    outputs = (middle + out_sum.astype(F32)).astype(BF)

    unused, pull_ffn = jax.vjp(root_mean_norm, middle, mid)
    grad_middle, grad_mid = pull_ffn(grad_ffn.astype(F32))
    grad_middle = grad_middle + upstream.astype(F32)
    grad_branch = grad_middle.astype(BF)
    grad_out = dot(mixed, grad_branch, TOKENS, BF)
    grad_mixed = dot(grad_branch, wo, ROWS, BF).reshape(2, 128, KEY_VALUE_HEADS, 2, HEAD_SIZE)
    grad_chances = jnp.einsum("mbkgd,mtkd->mkgbt", grad_mixed, values, preferred_element_type=F32)
    inner = jnp.sum(chances * grad_chances, axis=-1, keepdims=True)
    grad_scores = (chances * (grad_chances - inner)).astype(BF)
    grad_queries = jnp.einsum("mkgbt,mtkd->mbkgd", grad_scores, keys, preferred_element_type=F32)
    grad_keys = jnp.einsum("mkgbt,mbkgd->mtkd", grad_scores, grouped, preferred_element_type=F32)
    grad_values = jnp.einsum("mkgbt,mbkgd->mtkd", chances_low, grad_mixed, preferred_element_type=F32)
    grad_kv = jnp.concatenate([grad_keys.reshape(2, 512, 512), grad_values.reshape(2, 512, 512)], axis=-1)
    grad_kv = grad_kv.astype(BF).reshape(2, 4, 128, 1024).transpose(1, 0, 2, 3).reshape(4, 256, 1024)
    (grad_kv,) = reduce_line(4, grad_kv)
    grad_keys = grad_kv[:, :512].astype(F32).reshape(2, 128, KEY_VALUE_HEADS, HEAD_SIZE)
    unused_q, pull_query = jax.vjp(partial(query_piece, inside_document=inside), lin_query, qn)
    grad_lin_query, grad_qn = pull_query(grad_queries.reshape(2, 128, QUERY_HEADS, HEAD_SIZE))
    unused_k, pull_key = jax.vjp(partial(key_piece, inside_document=inside), lin_key, kn)
    grad_lin_key, grad_kn = pull_key(grad_keys)
    grad_lin = jnp.concatenate([grad_lin_query.astype(BF), grad_lin_key.astype(BF), grad_kv[:, 512:]], axis=1)
    grad_qkv = dot(normed, grad_lin, TOKENS, BF)
    grad_normed = dot(grad_lin, wqkv, ROWS)
    unused_a, pull_attn = jax.vjp(root_mean_norm, source32, pre)
    grad_source, grad_pre = pull_attn(grad_normed)
    grad_inputs = grad_middle + grad_source

    small = jnp.stack(
        [grad_pre, grad_mid]
        + [jnp.pad(g.reshape(32, 2), ((0, 0), (0, 30))).reshape(1024) for g in (grad_qn, grad_kn)],
        axis=1,
    )
    grad_gains = jnp.pad(small, ((0, 0), (0, 124))).astype(BF)
    grad_whole = jnp.concatenate([grad_qkv, grad_out, grad_gains], axis=1).reshape(4, 4, 2, 32, WA)
    own_whole, own_gu, own_down = reduce_all(grad_whole, grad_gu, grad_down)
    own = jnp.sum(own_whole.astype(F32), axis=0)
    own_gu = own_gu.astype(F32).transpose(1, 0, 2)
    return (
        outputs.reshape(2, 1, 128, 1024),
        grad_inputs.reshape(2, 1, 128, 1024),
        own[:, :1024],
        own[:, 1024:1536],
        own[:, 1536:2048],
        own[:, 2048:3072],
        own_gu[:, :, :1152].reshape(32, 4608),
        own_gu[:, :, 1152:].reshape(32, 4608),
        own_down.astype(F32),
        own[:, 3072],
        own[:, 3073],
        own[:2, 3074],
        own[:2, 3075],
    )


def solution(mesh):
    tokens, matrix, vector = P(None, "dp", "seq", None), P("dp", None), P("dp")
    return jax.shard_map(
        body,
        mesh=mesh,
        in_specs=(tokens, P(None, "dp", "seq")) + (matrix,) * 7 + (vector,) * 4 + (tokens,),
        out_specs=(tokens, tokens) + (matrix,) * 7 + (vector,) * 4,
        check_vma=False,
    )
```

```python
from functools import partial

import jax
import jax.numpy as jnp
from jax import lax
from jax.experimental import pallas as pl
from jax.experimental.pallas import tpu as pltpu
from jax.sharding import PartitionSpec as P

QUERY_HEADS = 16
KEY_VALUE_HEADS = 8
HEAD_SIZE = 64
EPS = 1e-05
ROPE_BASE = 1000000.0

MESH = pl.DeviceIdType.MESH
BF = jnp.bfloat16
F32 = jnp.float32
WA = 3200
GU = 2304
DN = 144


class Links:
    def __init__(self, send, recv, local):
        dp = lax.axis_index("dp")
        self.z = lax.axis_index("seq")
        self.x, self.y, self.c = dp // 8, (dp // 2) % 4, dp % 2
        self.send, self.recv, self.local = send, recv, local
        self.n = self.m = 0
        self.out = []
        self.other = 1 - self.c
        place = {"x": self.x, "y": self.y, "z": self.z}
        self.ring = {k: ((v + 3) % 4, (v + 1) % 4, (v + 2) % 4) for k, v in place.items()}
        self.past_x = (self.x - self.z + 4) % 4
        self.past_z = (self.z - self.x + 4) % 4
        self.near = {("c", 1): self.dev(self.x, self.y, self.other, self.z)}
        for k, (before, after, far) in self.ring.items():
            for step, v in ((-1, before), (1, after)):
                spot = dict(place, **{k: v})
                self.near[k, step] = self.dev(spot["x"], spot["y"], self.c, spot["z"])

    def dev(self, x, y, c, z):
        return ((x * 4 + y) * 2 + c, z)

    def nbr(self, axis, step):
        return self.near[axis, step]

    def sides(self, axis):
        return self.nbr(axis, 1), self.nbr(axis, -1)

    def barrier(self, axes):
        sem = pltpu.get_barrier_semaphore()
        count = 0
        for axis in axes:
            for step in (1,) if axis == "c" else (1, -1):
                pl.semaphore_signal(sem, inc=1, device_id=self.nbr(axis, step), device_id_type=MESH)
                count += 1
        pl.semaphore_wait(sem, count)

    def make(self, src, dst, to):
        copy = pltpu.make_async_remote_copy(
            src_ref=src,
            dst_ref=dst,
            send_sem=self.send.at[self.n],
            recv_sem=self.recv.at[self.n],
            device_id=to,
            device_id_type=MESH,
        )
        self.n += 1
        return copy

    def put(self, src, dst, to):
        copy = self.make(src, dst, to)
        copy.start()
        self.out.append(copy)
        return copy

    def keep(self, src, dst):
        copy = pltpu.make_async_copy(src, dst, self.local.at[self.m])
        self.m += 1
        copy.start()
        return copy

    def flush(self):
        for copy in self.out:
            copy.wait_send()
        self.out = []


def drive(*steps):
    steps = list(steps)
    while steps:
        steps = [s for s in steps if next(s, "end") != "end"]


def ring_gather(lk, own, slot, part, axis, me, ready=None):
    right, left = lk.sides(axis)
    before, after, far = lk.ring[axis]
    a = lk.put(own, slot(me), right)
    b = lk.put(own, slot(me), left)
    yield 1
    a.wait_recv()
    c = lk.put(part(before, 0), part(before, 0), right)
    if ready:
        ready(before)
    b.wait_recv()
    d = lk.put(part(after, 1), part(after, 1), left)
    if ready:
        ready(after)
    yield 1
    c.wait_recv()
    d.wait_recv()
    if ready:
        ready(far)


def plane_gather(lk, own, out, first, lo, hi):
    cols = pl.ds(lo, hi - lo)
    x, y, c = lk.x, lk.y, lk.c
    kept = lk.keep(own.at[:, cols], out.at[x, y, c, :, cols])
    crossing = []

    def cross(ref):
        crossing.append(lk.put(ref, ref, lk.nbr("c", 1)))

    def rows(k):
        return pl.ds(16 * k, 16)

    def two(k):
        return pl.ds(2 * k, 2)

    if first == "x":
        yield from ring_gather(
            lk, own.at[:, cols], lambda i: out.at[i, y, c, :, cols],
            lambda i, k: out.at[i, y, c, rows(k), cols], "x", x,
        )
        kept.wait()
        whole = out.at[:, y, c, :, cols]
        cross(whole)
        yield from ring_gather(
            lk, whole, lambda j: out.at[:, j, c, :, cols],
            lambda j, k: out.at[two(k), j, c, :, cols], "y", y,
            lambda j: cross(out.at[:, j, c, :, cols]),
        )
    else:
        yield from ring_gather(
            lk, own.at[:, cols], lambda j: out.at[x, j, c, :, cols],
            lambda j, k: out.at[x, j, c, rows(k), cols], "y", y,
        )
        kept.wait()
        whole = out.at[x, :, c, :, cols]
        cross(whole)
        yield from ring_gather(
            lk, whole, lambda i: out.at[i, :, c, :, cols],
            lambda i, k: out.at[i, two(k), c, :, cols], "x", x,
            lambda i: cross(out.at[i, :, c, :, cols]),
        )
    yield 1
    for copy in crossing:
        copy.wait_recv()


def ring_spread(lk, own, dst, part, axis, place):
    right, left = lk.sides(axis)
    a, b = lk.make(own, dst, right), lk.make(own, dst, left)
    c, d = lk.make(part(0), part(0), right), lk.make(part(1), part(1), left)
    kept = pltpu.make_async_copy(own, dst, lk.local.at[lk.m])
    lk.m += 1

    @pl.when(place == 0)
    def _():
        a.start()
        b.start()
        kept.start()

    yield 1

    @pl.when(place == 1)
    def _():
        a.wait_recv()
        c.start()

    @pl.when(place == 3)
    def _():
        b.wait_recv()
        d.start()

    yield 1

    @pl.when(place == 2)
    def _():
        c.wait_recv()
        d.wait_recv()

    @pl.when(place == 0)
    def _():
        kept.wait()
        a.wait_send()
        b.wait_send()

    @pl.when(place == 1)
    def _():
        c.wait_send()

    @pl.when(place == 3)
    def _():
        d.wait_send()


def down_part(k):
    return pl.ds(0, 80) if k == 0 else pl.ds(80, 64)


def down_gather(lk, own, out):
    y, c = lk.y, lk.c
    yield from ring_spread(
        lk, own, out.at[y, c], lambda k: out.at[y, c, down_part(k)], "x", lk.past_x
    )
    crossing = []

    def cross(j):
        crossing.append(lk.put(out.at[j, c], out.at[j, c], lk.nbr("c", 1)))

    cross(y)
    yield from ring_gather(
        lk, out.at[y, c], lambda j: out.at[j, c], lambda j, k: out.at[j, c, down_part(k)], "y", y, cross
    )
    yield 1
    for copy in crossing:
        copy.wait_recv()


def line_gather(lk, own, out, cut):
    z, rows = lk.z, own.shape[0]
    kept = lk.keep(own, out.at[z])

    def part(i, k):
        return out.at[i, pl.ds(0, cut)] if k == 0 else out.at[i, pl.ds(cut, rows - cut)]

    yield from ring_gather(lk, own, lambda i: out.at[i], part, "z", z)
    kept.wait()


def add_into(dst, src):
    if len(dst.shape) == 2:
        dst[...] = (dst[...].astype(F32) + src[...].astype(F32)).astype(BF)
    else:
        for i in range(dst.shape[0]):
            dst[i] = (dst[i].astype(F32) + src[i].astype(F32)).astype(BF)


def ring_reduce(lk, p, part, bufs, axis, me):
    right, left = lk.sides(axis)
    r0, r1, ra, rb = bufs
    before, after, far = lk.ring[axis]
    a = lk.put(part(far, 0), r0, right)
    b = lk.put(part(far, 1), r1, left)
    yield 1
    a.wait_recv()
    add_into(part(after, 0), r0)
    c = lk.put(p(after), ra, right)
    b.wait_recv()
    add_into(part(before, 1), r1)
    d = lk.put(p(before), rb, left)
    yield 1
    c.wait_recv()
    add_into(p(me), ra)
    d.wait_recv()
    add_into(p(me), rb)


def plane_reduce(lk, spot, sib_src, sib, bufs, out, first, kept=None):
    x, y, c = lk.x, lk.y, lk.c
    one, two = bufs
    got = lk.put(sib_src, sib, lk.nbr("c", 1))
    yield 1
    if kept is not None:
        kept.wait()
    got.wait_recv()

    def step(i, _):
        ref = spot(i // 4, i % 4)
        ref[...] = (ref[...].astype(F32) + sib[i // 4, i % 4].astype(F32)).astype(BF)
        return 0

    lax.fori_loop(0, 16, step, 0)
    every = slice(None)

    def pair(k):
        return pl.ds(2 * k, 2)

    def rows(ref, k):
        return ref.at[pl.ds(16 * k, 16)]

    if first == "y":
        yield from ring_reduce(lk, lambda j: spot(every, j), lambda j, k: spot(pair(k), j), one, "y", y)
        yield from ring_reduce(lk, lambda i: spot(i, y), lambda i, k: rows(spot(i, y), k), two, "x", x)
    else:
        yield from ring_reduce(lk, lambda i: spot(i, every), lambda i, k: spot(i, pair(k)), one, "x", x)
        yield from ring_reduce(lk, lambda j: spot(x, j), lambda j, k: rows(spot(x, j), k), two, "y", y)
    done = lk.keep(spot(x, y), out)
    yield 1
    done.wait()


def ring_scratch(cols):
    return [
        pltpu.VMEM((4, 4, 32, cols), BF),
        pltpu.VMEM((2, 32, cols), BF),
        pltpu.VMEM((2, 32, cols), BF),
        pltpu.VMEM((4, 32, cols), BF),
        pltpu.VMEM((4, 32, cols), BF),
        pltpu.VMEM((16, cols), BF),
        pltpu.VMEM((16, cols), BF),
        pltpu.VMEM((32, cols), BF),
        pltpu.VMEM((32, cols), BF),
    ]


def down_scratch():
    return [
        pltpu.VMEM((4, DN, 1024), BF),
        pltpu.VMEM((4, DN, 1024), BF),
        pltpu.VMEM((80, 1024), BF),
        pltpu.VMEM((64, 1024), BF),
        pltpu.VMEM((DN, 1024), BF),
        pltpu.VMEM((DN, 1024), BF),
        pltpu.VMEM((80, 1024), BF),
        pltpu.VMEM((64, 1024), BF),
        pltpu.VMEM((DN, 1024), BF),
        pltpu.VMEM((DN, 1024), BF),
    ]


def down_reduce(lk, part_hbm, s, out):
    acc, sib, one, (x0, x1, xa, xb) = s[0], s[1], s[2:6], s[6:10]
    y, c = lk.y, lk.c
    kept = lk.keep(part_hbm.at[:, c], acc)
    got = lk.put(part_hbm.at[:, 1 - c], sib, lk.nbr("c", 1))
    yield 1
    kept.wait()
    got.wait_recv()
    add_into(acc, sib)
    yield from ring_reduce(
        lk, lambda j: acc.at[j], lambda j, k: acc.at[j, down_part(k)], one, "y", y
    )
    mine = acc.at[y]
    right, left = lk.sides("x")
    place = lk.past_x
    a = lk.make(acc.at[y, down_part(0)], x0, left)
    b = lk.make(acc.at[y, down_part(1)], x1, right)
    e = lk.make(mine, xa, left)
    f = lk.make(mine, xb, right)

    @pl.when(place == 2)
    def _():
        a.start()
        b.start()

    yield 1

    @pl.when(place == 1)
    def _():
        a.wait_recv()
        add_into(acc.at[y, down_part(0)], x0)
        e.start()

    @pl.when(place == 3)
    def _():
        b.wait_recv()
        add_into(acc.at[y, down_part(1)], x1)
        f.start()

    yield 1

    @pl.when(place == 0)
    def _():
        e.wait_recv()
        add_into(mine, xa)
        f.wait_recv()
        add_into(mine, xb)

    @pl.when(place == 1)
    def _():
        e.wait_send()

    @pl.when(place == 3)
    def _():
        f.wait_send()

    @pl.when(place == 2)
    def _():
        a.wait_send()
        b.wait_send()

    yield from ring_spread(
        lk, mine, out, lambda k: out.at[down_part(k)], "z", lk.past_z
    )


ANY = pl.BlockSpec(memory_space=pl.ANY)


def sems(n):
    return [pltpu.SemaphoreType.DMA((n,)), pltpu.SemaphoreType.DMA((n,)), pltpu.SemaphoreType.DMA((40,))]


def params(number):
    return pltpu.CompilerParams(collective_id=number, has_side_effects=True, vmem_limit_bytes=56 * 2**20)


def shape(*dims, dtype=BF):
    return jax.ShapeDtypeStruct(dims, dtype)


def lanes_of(shape):
    return lax.broadcasted_iota(jnp.int32, shape, len(shape) - 1)


def dot(left, right, dims=((1,), (0,)), kind=F32):
    return lax.dot_general(left, right, (dims, ((), ())), preferred_element_type=F32).astype(kind)


TOKENS = ((0,), (0,))
ROWS = ((1,), (1,))


def flat(value):
    return value.reshape(-1, value.shape[-1])


def head_ones():
    row = lax.broadcasted_iota(jnp.int32, (256, 256), 0) // 64
    col = lax.broadcasted_iota(jnp.int32, (256, 256), 1) // 64
    return jnp.where(row == col, 1.0 / 64, 0.0).astype(BF)


def head_mean(v, ones):
    high = v.astype(BF)
    low = (v - high.astype(F32)).astype(BF)
    return dot(high, ones) + dot(low, ones)


def halves_swapped(v):
    lane = lanes_of(v.shape)
    return jnp.where(lane % 64 < 32, pltpu.roll(v, 96, 1), pltpu.roll(v, 32, 1))


def angle_tables(tab):
    lane = lanes_of(tab.shape)
    other = pltpu.roll(tab, 64, 1)
    return jnp.where(lane < 64, tab, other), jnp.where(lane < 64, other, tab)


def row_scale(v):
    return lax.rsqrt(jnp.mean(v * v, axis=-1, keepdims=True) + EPS)


def gain_rows(whole, gain):
    def step(i, total):
        return total + whole[i // 8, (i // 2) % 4, i % 2, :, pl.ds(2048, 128)].astype(F32)

    total = lax.fori_loop(0, 32, step, jnp.zeros((32, 128), F32))
    for k in range(8):
        gain[0:1, pl.ds(128 * k, 128)] = total[8 + k : 9 + k]
        gain[1:2, pl.ds(128 * k, 128)] = total[16 + k : 17 + k]
        gain[2:3, pl.ds(128 * k, 128)] = total[0:1]
        gain[3:4, pl.ds(128 * k, 128)] = total[1:2]


def keys_values(whole, sources, tables, gain, normed, keys, values, lin_key, own):
    ones = head_ones()

    def step(q, _):
        src = sources[q].astype(F32)
        normed[q] = (src * row_scale(src) * gain[0:1]).astype(BF)
        cosine, sine = angle_tables(tables[q])
        kn = gain[3:4, 0:128]
        lane = lanes_of((256, 128))

        def put(ref, tile, r):
            turned = pltpu.roll(r, 64, 1)
            even = jnp.where(lane < 64, r, turned).astype(BF)
            odd = jnp.where(lane < 64, turned, r).astype(BF)
            for m in range(2):
                ref[m, 2 * tile, pl.ds(q * 128, 128)] = even[128 * m : 128 * m + 128]
                ref[m, 2 * tile + 1, pl.ds(q * 128, 128)] = odd[128 * m : 128 * m + 128]

        for j in range(4):
            lin = dot(normed[q], flat(whole[:, :, :, :, pl.ds(1024 + 256 * j, 256)]))
            if j < 2:
                scale = lax.rsqrt(head_mean(lin * lin, ones) + EPS)

                @pl.when(q == own)
                def _():
                    lin_key[:, pl.ds(256 * j, 256)] = lin

                for h in range(2):
                    cut = slice(128 * h, 128 * h + 128)
                    v = lin[:, cut] * scale[:, cut] * kn
                    put(keys, 2 * j + h, v * cosine + halves_swapped(v) * sine)
            else:
                for h in range(2):
                    put(values, 2 * (j - 2) + h, lin[:, 128 * h : 128 * h + 128])
        return 0

    lax.fori_loop(0, 4, step, 0)


def own_queries(whole, tables, gain, normed, lin_query, queries, own):
    ones = head_ones()
    cosine, sine = angle_tables(tables[own])
    qn = gain[2:3, 0:128]
    lane = lanes_of((256, 128))

    def step(j, _):
        lin = dot(normed[own], flat(whole[:, :, :, :, pl.ds(pl.multiple_of(256 * j, 256), 256)]))
        lin_query[:, pl.ds(pl.multiple_of(256 * j, 256), 256)] = lin
        scale = lax.rsqrt(head_mean(lin * lin, ones) + EPS)
        for h in range(2):
            cut = slice(128 * h, 128 * h + 128)
            v = lin[:, cut] * scale[:, cut] * qn
            r = (v * cosine + halves_swapped(v) * sine) * HEAD_SIZE ** (-0.5)
            first = jnp.where(lane < 64, r, 0.0).astype(BF)
            second = jnp.where(lane < 64, 0.0, r).astype(BF)
            for m in range(2):
                queries[m, 2 * j + h, 0:128] = first[128 * m : 128 * m + 128]
                queries[m, 2 * j + h, 128:256] = second[128 * m : 128 * m + 128]
        return 0

    lax.fori_loop(0, 4, step, 0)


def attend(queries, keys, values, starts, probs, mixed, own):
    key_pos = lax.broadcasted_iota(jnp.int32, (512, 256), 0)
    query_pos = own * 128 + lax.broadcasted_iota(jnp.int32, (1, 256), 1) % 128
    lane = lanes_of((128, 128))

    def step(i, _):
        m, k = i // 8, i % 8
        row = starts[pl.ds(m, 1)]
        begin = jnp.concatenate([row, row], axis=1)
        scores = dot(keys[m, k], queries[m, k], ROWS)
        scores = jnp.where((key_pos <= query_pos) & (key_pos >= begin), scores, -1e30)
        raised = jnp.exp(scores - jnp.max(scores, axis=0, keepdims=True))
        chance = (raised * (1.0 / jnp.sum(raised, axis=0, keepdims=True))).astype(BF)
        probs[i] = chance
        got = dot(values[m, k], chance, TOKENS).T
        both = jnp.where(lane < 64, got[0:128], got[128:256]).astype(BF)
        mixed[pl.ds(pl.multiple_of(m * 128, 128), 128), pl.ds(pl.multiple_of(k * 128, 128), 128)] = both
        return 0

    lax.fori_loop(0, 16, step, 0)


def out_project(whole, source, gain, mixed, middle, normed_ffn, own):
    def step(j, _):
        cut = pl.ds(pl.multiple_of(256 * j, 256), 256)
        w = flat(whole[:, :, :, :, pl.ds(pl.multiple_of(2176 + 256 * j, 128), 256)])
        middle[:, cut] = source[:, cut].astype(F32) + dot(mixed[...], w)
        return 0

    lax.fori_loop(0, 4, step, 0)
    mid = middle[...]
    normed_ffn[own] = (mid * row_scale(mid) * gain[1:2]).astype(BF)


def feed_back_in(cots, down, grad_hidden):
    def step(i, _):
        grad_hidden[i] = dot(cots[i], flat(down[...]), ROWS, BF)
        return 0

    lax.fori_loop(0, 4, step, 0)


def feed_chunk(i, ffn, gate_up, down, grad_hidden, hidden, turned, ffn_turned, grad_both, grad_ffn, out_part):
    def step(j, _):
        cut = pl.ds(pl.multiple_of(384 * j, 128), 384)
        cut_up = pl.ds(pl.multiple_of(1152 + 384 * j, 128), 384)
        gated = dot(ffn[i], flat(gate_up[:, :, :, :, cut]))
        upward = dot(ffn[i], flat(gate_up[:, :, :, :, cut_up]))
        sigma = 1.0 / (1.0 + jnp.exp(-gated))
        silu = gated * sigma
        made = (silu * upward).astype(BF)
        hidden[:, cut] = made
        turned[i, cut] = made.T
        back = grad_hidden[i, :, cut].astype(F32)
        grad_both[i, :, cut] = (back * upward * sigma * (1.0 + gated * (1.0 - sigma))).astype(BF)
        grad_both[i, :, cut_up] = (back * silu).astype(BF)
        return 0

    lax.fori_loop(0, 3, step, 0)

    def last(j, _):
        cut = pl.ds(pl.multiple_of(256 * j, 256), 256)
        grad_ffn[i, :, cut] = dot(grad_both[i], flat(gate_up[j]), ROWS, BF)
        out_part[i, :, cut] = dot(hidden[...], flat(down[:, :, :, cut]), kind=BF)
        ffn_turned[i, cut] = ffn[i, :, cut].T
        return 0

    lax.fori_loop(0, 4, last, 0)


def feed_grads(left, right, out, tiles):
    def step(j, _):
        cut = pl.ds(pl.multiple_of(256 * j, 256), 256)
        got = dot(left[0], right[0, :, cut])
        for i in range(1, 4):
            got = got + dot(left[i], right[i, :, cut])
        lead = out.shape[:-1]
        out[(slice(None),) * len(lead) + (cut,)] = got.astype(BF).reshape(*lead, 256)
        return 0

    lax.fori_loop(0, tiles, step, 0)


FWD_SCRATCH = [
    pltpu.VMEM((4, 4, 2, 32, WA), BF),
    pltpu.VMEM((4, 4, 2, 32, GU), BF),
    pltpu.VMEM((4, 2, DN, 1024), BF),
    pltpu.VMEM((4, 256, 1024), BF),
    pltpu.VMEM((4, 256, 128), F32),
    pltpu.VMEM((4, 256, 1024), BF),
    pltpu.VMEM((4, 256, 1024), BF),
    pltpu.VMEM((4, 256, 1024), BF),
    pltpu.VMEM((256, 1024), F32),
    pltpu.VMEM((256, 512), F32),
    pltpu.VMEM((2, 8, 512, 128), BF),
    pltpu.VMEM((2, 8, 512, 128), BF),
    pltpu.VMEM((2, 8, 256, 128), BF),
    pltpu.VMEM((16, 512, 256), BF),
    pltpu.VMEM((256, 1024), BF),
    pltpu.VMEM((256, 1024), F32),
    pltpu.VMEM((8, 1024), F32),
    pltpu.VMEM((4, 256, 1152), BF),
    pltpu.VMEM((256, 1152), BF),
    pltpu.VMEM((4, 1152, 256), BF),
    pltpu.VMEM((4, 1024, 256), BF),
    pltpu.VMEM((4, 256, GU), BF),
    pltpu.VMEM((4, 256, 1024), BF),
    pltpu.VMEM((4, 256, 1024), BF),
    pltpu.VMEM((256, 1024), BF),
    pltpu.VMEM((256, 1024), BF),
    pltpu.VMEM((2, 128, 1024), BF),
    pltpu.VMEM((2, 128, 1024), BF),
    pltpu.VMEM((2, 128), jnp.int32),
]

FWD_OUT = (
    shape(4, 4, 2, 32, WA),
    shape(256, 1024),
    shape(256, 1024, dtype=F32),
    shape(256, 512, dtype=F32),
    shape(2, 8, 512, 128),
    shape(2, 8, 512, 128),
    shape(2, 8, 256, 128),
    shape(16, 512, 256),
    shape(256, 1024),
    shape(256, 1024, dtype=F32),
    shape(8, 1024, dtype=F32),
    shape(4, 4, 2, 32, GU),
    shape(4, 2, DN, 1024),
    shape(4, 256, 1024),
    shape(256, 1024, dtype=F32),
)


def fwd_kernel(wa, gu, dn, x, cot, tab, starts_hbm, *refs):
    outs, refs = refs[: len(FWD_OUT)], refs[len(FWD_OUT) :]
    lk = Links(*refs[:3])
    (
        whole, gate_up, down, sources, tables, cots, ffn, normed, lin_query, lin_key, keys, values, queries,
        probs, mixed, middle, gain, grad_hidden, hidden, turned, ffn_turned, grad_both, grad_ffn, out_part,
        from_right, from_left, passing, from_far, starts,
    ) = refs[3:]
    own = lk.z
    before, after, far = (own + 3) % 4, (own + 1) % 4, (own + 2) % 4
    lk.barrier("xyzc")
    first = [
        plane_gather(lk, wa, whole, "x", 0, 1536),
        plane_gather(lk, wa, whole, "y", 1536, WA),
        line_gather(lk, tab, tables, 128),
        line_gather(lk, x, sources, 128),
    ]
    later = [
        plane_gather(lk, gu, gate_up, "x", 0, 1152),
        plane_gather(lk, gu, gate_up, "y", 1152, GU),
        down_gather(lk, dn, down),
        line_gather(lk, cot, cots, 128),
    ]
    for s in first + later[:3]:
        next(s)
    saved = [lk.keep(starts_hbm, starts)]
    saved[0].wait()
    saved = []
    drive(*first)

    def tick():
        for s in later:
            next(s, None)

    tick()
    gain_rows(whole, gain)
    saved.append(lk.keep(whole, outs[0]))
    keys_values(whole, sources, tables, gain, normed, keys, values, lin_key, own)
    tick()
    own_queries(whole, tables, gain, normed, lin_query, queries, own)
    for k, ref in enumerate((normed.at[own], lin_query, lin_key, keys, values, queries)):
        saved.append(lk.keep(ref, outs[1 + k]))
    tick()
    attend(queries, keys, values, starts, probs, mixed, own)
    tick()
    out_project(whole, sources.at[own], gain, mixed, middle, ffn, own)
    for k, ref in enumerate((probs, mixed, middle, gain)):
        saved.append(lk.keep(ref, outs[7 + k]))
    passed = ring_gather(
        lk, ffn.at[own], lambda i: ffn.at[i], lambda i, k: ffn.at[i, pl.ds(128 * k, 128)], "z", own
    )
    next(passed)
    drive(*later)
    feed_back_in(cots, down, grad_hidden)

    def chunk(i):
        feed_chunk(
            i, ffn, gate_up, down, grad_hidden, hidden, turned, ffn_turned, grad_both, grad_ffn, out_part
        )

    right, left = lk.sides("z")
    chunk(own)
    lk.flush()
    next(passed)
    chunk(before)
    one = lk.put(grad_ffn.at[before], from_right, left)
    chunk(after)
    two = lk.put(grad_ffn.at[after], from_left, right)
    next(passed, None)
    chunk(far)
    saved.append(lk.keep(out_part, outs[13]))
    three = lk.put(grad_ffn.at[far, pl.ds(0, 128)], passing.at[0], right)
    four = lk.put(grad_ffn.at[far, pl.ds(128, 128)], passing.at[1], left)
    feed_grads(ffn_turned, grad_both, gate_up, 9)
    saved.append(lk.keep(gate_up, outs[11]))
    three.wait_recv()
    five = lk.put(passing.at[0], from_far.at[0], right)
    four.wait_recv()
    six = lk.put(passing.at[1], from_far.at[1], left)
    feed_grads(turned, cots, down, 4)
    saved.append(lk.keep(down, outs[12]))
    for copy in (one, two, five, six):
        copy.wait_recv()
    for copy in saved:
        copy.wait()
    total = grad_ffn[own].astype(F32) + from_right[...].astype(F32) + from_left[...].astype(F32)
    lin_query[...] = total + flat(from_far[...]).astype(F32)
    lk.keep(lin_query, outs[14]).wait()
    lk.flush()


def forward(*args):
    return pl.pallas_call(
        fwd_kernel,
        out_shape=FWD_OUT,
        in_specs=[ANY] * 7,
        out_specs=[ANY] * len(FWD_OUT),
        scratch_shapes=sems(96) + FWD_SCRATCH,
        compiler_params=pltpu.CompilerParams(
            collective_id=0, has_side_effects=True, vmem_limit_bytes=60 * 2**20
        ),
    )(*args)


BWD_IN = 18
PIECES = (1152, 1152, 512, 512, 512, 512, 512, 640)
BWD_OUT = (
    shape(256, 1024),
    shape(256, 1024, dtype=F32),
    shape(4, 32, WA),
    shape(4, 32, GU),
    shape(DN, 1024),
    shape(32, WA),
    shape(32, GU),
)
BWD_SCRATCH = [
    pltpu.VMEM((4, 4, 2, 32, WA), BF),
    pltpu.VMEM((256, 1024), BF),
    pltpu.VMEM((256, 1024), F32),
    pltpu.VMEM((256, 512), F32),
    pltpu.VMEM((2, 8, 512, 128), BF),
    pltpu.VMEM((2, 8, 512, 128), BF),
    pltpu.VMEM((2, 8, 256, 128), BF),
    pltpu.VMEM((16, 512, 256), BF),
    pltpu.VMEM((256, 1024), BF),
    pltpu.VMEM((256, 1024), F32),
    pltpu.VMEM((8, 1024), F32),
    pltpu.VMEM((4, 256, 1024), BF),
    pltpu.VMEM((256, 1024), F32),
    pltpu.VMEM((256, 1024), BF),
    pltpu.VMEM((256, 1024), BF),
    pltpu.VMEM((256, 128), F32),
]
BWD_WORK = [
    pltpu.VMEM((256, 1024), BF),
    pltpu.VMEM((2, 8, 256, 128), BF),
    pltpu.VMEM((256, 1024), F32),
    pltpu.VMEM((4, 256, 1024), BF),
    pltpu.VMEM((256, 2048), BF),
    pltpu.VMEM((1024, 256), BF),
    pltpu.VMEM((256, 1024), F32),
    pltpu.VMEM((8, 1024), F32),
    pltpu.VMEM((4, 4, 2, 32, WA), BF),
    pltpu.VMEM((4, 4, 32, 1152), BF),
    pltpu.VMEM((4, 4, 32, 1152), BF),
    pltpu.VMEM((256, 1024), BF),
]
Z_RING = [
    pltpu.VMEM((128, 1024), BF),
    pltpu.VMEM((128, 1024), BF),
    pltpu.VMEM((256, 1024), BF),
    pltpu.VMEM((256, 1024), BF),
]


def norm_back(v, g, dy):
    r = row_scale(v)
    gdy = g * dy
    back = r * gdy - v * (r * r * r * jnp.mean(v * gdy, axis=-1, keepdims=True))
    return back, jnp.sum(v * r * dy, axis=0, keepdims=True)


def heads_back(lin, grad, gain, cosine, sine, ones):
    parts = []
    for h in range(2):
        part = grad[:, 128 * h : 128 * h + 128]
        parts.append(part * cosine + halves_swapped(part * sine))
    dy = jnp.concatenate(parts, axis=1)
    r = lax.rsqrt(head_mean(lin * lin, ones) + EPS)
    gdy = dy * gain
    back = r * gdy - lin * (r * r * r * head_mean(lin * gdy, ones))
    return back, jnp.sum(lin * r * dy, axis=0, keepdims=True)


def turned_grads(turned, right, out, start, tiles, base=0):
    def step(j, _):
        got = dot(turned[...], right[:, pl.ds(pl.multiple_of(base + 256 * j, 256), 256)], kind=BF)
        out[:, :, :, :, pl.ds(pl.multiple_of(start + 256 * j, 128), 256)] = got.reshape(4, 4, 2, 32, 256)
        return 0

    lax.fori_loop(0, tiles, step, 0)


def attend_back(queries, keys, values, probs, grad_mixed, grad_queries, grad_kv, tick):
    lane = lanes_of((128, 128))
    lane_keys = lanes_of((512, 128))

    def step(n, _):
        m, j = n // 4, n % 4
        folded = []
        for e in range(2):
            k = 2 * j + e
            i = m * 8 + k
            chance = probs[i]
            back = dot(values[m, k], grad_mixed[m, k], ROWS)
            p = chance.astype(F32)
            p_back = p * back
            grad_scores = (p_back - p * jnp.sum(p_back, axis=0, keepdims=True)).astype(BF)
            got = dot(keys[m, k], grad_scores, TOKENS).T
            cut = pl.ds(pl.multiple_of(128 * k, 128), 128)
            grad_queries[pl.ds(pl.multiple_of(m * 128, 128), 128), cut] = jnp.where(
                lane < 64, got[0:128], got[128:256]
            )
            for v in (dot(grad_scores, queries[m, k]), dot(chance, grad_mixed[m, k])):
                folded.append(v + pltpu.roll(v, 64, 1))
        for s in range(2):
            tile = jnp.where(lane_keys < 64, folded[s], folded[2 + s]).astype(BF)
            cut = pl.ds(pl.multiple_of(512 * s + 128 * j, 128), 128)
            for q in range(4):
                grad_kv[q, pl.ds(pl.multiple_of(m * 128, 128), 128), cut] = tile[128 * q : 128 * q + 128]

        return 0

    lax.fori_loop(0, 4, step, 0)
    tick()
    lax.fori_loop(4, 8, step, 0)


def bwd_kernel(*refs):
    ins, refs = refs[:BWD_IN], refs[BWD_IN:]
    outs, refs = refs[: len(BWD_OUT)], refs[len(BWD_OUT) :]
    lk = Links(*refs[:3])
    refs = refs[3:]
    n = len(BWD_SCRATCH)
    held, refs = refs[:n], refs[n:]
    (
        whole, normed, lin_query, lin_key, keys, values, queries, probs, mixed, middle, gain, out_part, grad_middle,
        upstream, source, table,
    ) = held
    grad_gu, grad_down = ins[16:]
    n = len(BWD_WORK)
    work, refs = refs[:n], refs[n:]
    (
        grad_branch, grad_mixed, grad_queries, grad_kv, grad_lin, turned, grad_normed, gains_back, grad_whole, acc_a,
        acc_b, made,
    ) = work
    z_out, z_kv, refs = refs[:4], refs[4:8], refs[8:]
    down_refs, refs = refs[:10], refs[10:]
    rings = [refs[9 * i : 9 * i + 9] for i in range(len(PIECES))]
    outputs, grad_inputs, a_all, gu_all, down_own, a_own, gu_own = outs
    own, c = lk.z, lk.c

    order = [12, 9, 13, 10, 0, 8, 5, 7, 6, 4, 11, 2, 15, 1, 3, 14]
    loads = {}
    for k in order[:6]:
        loads[k] = lk.keep(ins[k], held[k])
    lk.barrier("xyzc")

    def piece(k, spot, src, out, first, kept=None):
        ring = rings[k]
        return plane_reduce(lk, spot, src, ring[0], (ring[1:5], ring[5:9]), out, first, kept)

    def feed_piece(k, acc, lo, first):
        cols = pl.ds(lo, 1152)
        kept = lk.keep(grad_gu.at[:, :, c, :, cols], acc)
        return piece(
            k, lambda i, j: acc.at[i, j], grad_gu.at[:, :, lk.other, :, cols], gu_own.at[:, cols], first, kept
        )

    def whole_piece(k, lo, first):
        cols = pl.ds(lo, PIECES[k])
        return piece(
            k, lambda i, j: grad_whole.at[i, j, c, :, cols], grad_whole.at[:, :, lk.other, :, cols],
            a_own.at[:, cols], first,
        )

    def feed_chain():
        parts = [feed_piece(0, acc_a, 0, "y"), feed_piece(1, acc_b, 1152, "x")]
        while parts:
            parts = [s for s in parts if next(s, "end") != "end"]
            yield 1
        yield from line_gather(lk, gu_own, gu_all, 16)

    def out_chain():
        yield from ring_reduce(
            lk, lambda i: out_part.at[i], lambda i, k: out_part.at[i, pl.ds(128 * k, 128)], z_out, "z", own
        )
        made[...] = (middle[...] + out_part[own].astype(F32)).astype(BF)
        done = lk.keep(made, outputs)
        yield 1
        done.wait()

    behind = [feed_chain(), down_reduce(lk, grad_down, down_refs, down_own)]

    def tick():
        for s in list(behind):
            if next(s, "end") == "end":
                behind.remove(s)

    tick()
    for k in order[6:]:
        loads[k] = lk.keep(ins[k], held[k])

    def need(*names):
        for k in names:
            loads.pop(k).wait()

    need(12, 9, 13, 10)
    back, row = norm_back(middle[...], gain[1:2], grad_middle[...])
    total = upstream[...].astype(F32) + back
    grad_middle[...] = total
    grad_branch[...] = total.astype(BF)
    gains_back[1:2] = row
    need(0, 8)
    tick()
    turned[...] = mixed[...].T
    turned_grads(turned, grad_branch, grad_whole, 2176, 4)
    behind += [whole_piece(2, 2176, "y"), whole_piece(3, 2688, "x")]
    tick()
    lane = lanes_of((256, 128))

    def back_mixed(j, _):
        got = dot(grad_branch[...], flat(whole[j, :, :, :, pl.ds(2176, 1024)]), ROWS)
        for h in range(2):
            r = got[:, 128 * h : 128 * h + 128]
            first = jnp.where(lane < 64, r, 0.0).astype(BF)
            second = jnp.where(lane < 64, 0.0, r).astype(BF)
            for m in range(2):
                grad_mixed[m, 2 * j + h, 0:128] = first[128 * m : 128 * m + 128]
                grad_mixed[m, 2 * j + h, 128:256] = second[128 * m : 128 * m + 128]
        return 0

    lax.fori_loop(0, 4, back_mixed, 0)
    need(5, 7, 6, 4, 11)
    behind.append(out_chain())
    tick()
    attend_back(queries, keys, values, probs, grad_mixed, grad_queries, grad_kv, tick)
    kv_sum = ring_reduce(
        lk, lambda i: grad_kv.at[i], lambda i, k: grad_kv.at[i, pl.ds(128 * k, 128)], z_kv, "z", own
    )
    next(kv_sum)
    tick()
    need(2, 15, 1)
    ones = head_ones()
    cosine, sine = angle_tables(table[...])

    def back_query(j, _):
        cut = pl.ds(pl.multiple_of(256 * j, 256), 256)
        grad = grad_queries[:, cut] * HEAD_SIZE ** (-0.5)
        got, line = heads_back(lin_query[:, cut], grad, gain[2:3, 0:256], cosine, sine, ones)
        grad_lin[:, cut] = got.astype(BF)
        gains_back[2:3, cut] = line
        return 0

    lax.fori_loop(0, 4, back_query, 0)
    turned[...] = normed[...].T
    turned_grads(turned, grad_lin, grad_whole, 0, 4)
    behind += [whole_piece(4, 0, "y"), whole_piece(5, 512, "x")]
    tick()
    next(kv_sum)

    def back_normed(j, _):
        grad_normed[:, pl.ds(pl.multiple_of(256 * j, 256), 256)] = dot(
            grad_lin[:, 0:1024], flat(whole[j, :, :, :, pl.ds(0, 1024)]), ROWS
        )
        return 0

    lax.fori_loop(0, 4, back_normed, 0)
    need(3, 14)
    tick()
    next(kv_sum, None)

    def back_key(j, _):
        cut = pl.ds(pl.multiple_of(256 * j, 256), 256)
        grad = grad_kv[own, :, cut].astype(F32)
        got, line = heads_back(lin_key[:, cut], grad, gain[3:4, 0:256], cosine, sine, ones)
        grad_lin[:, pl.ds(pl.multiple_of(1024 + 256 * j, 256), 256)] = got.astype(BF)
        gains_back[3:4, cut] = line
        return 0

    lax.fori_loop(0, 2, back_key, 0)
    grad_lin[:, 1536:2048] = grad_kv[own, :, 512:1024]
    turned_grads(turned, grad_lin, grad_whole, 1024, 4, 1024)

    def more_normed(j, _):
        cut = pl.ds(pl.multiple_of(256 * j, 256), 256)
        grad_normed[:, cut] = grad_normed[:, cut] + dot(
            grad_lin[:, 1024:2048], flat(whole[j, :, :, :, pl.ds(1024, 1024)]), ROWS
        )
        return 0

    lax.fori_loop(0, 4, more_normed, 0)
    back, row = norm_back(source[...].astype(F32), gain[0:1], grad_normed[...])
    gains_back[0:1] = row
    grad_normed[...] = grad_middle[...] + back

    small = [jnp.zeros((1, 128), F32)] * 2
    for s, tiles in ((0, 8), (1, 4)):
        for k in range(tiles):
            small[s] = small[s] + gains_back[2 + s : 3 + s, 128 * k : 128 * k + 128]
        small[s] = small[s] + pltpu.roll(jnp.broadcast_to(small[s], (8, 128)), 64, 1)[0:1]
    heads = jnp.where(lanes_of((1, 128)) < 64, small[0], small[1])
    line = lax.broadcasted_iota(jnp.int32, (32, 128), 0)
    for k in range(8):
        cut = slice(128 * k, 128 * k + 128)
        block = jnp.where(line == 8, gains_back[0:1, cut], 0.0)
        block = jnp.where(line == 16, gains_back[1:2, cut], block)
        block = jnp.where(line == 0, heads, block).astype(BF)
        for d in range(4 * k, 4 * k + 4):
            grad_whole[d // 8, (d // 2) % 4, d % 2, :, 2048:2176] = block
    behind += [whole_piece(6, 1024, "y"), whole_piece(7, 1536, "x")]
    drive(*behind)
    final = lk.keep(grad_normed, grad_inputs)
    drive(line_gather(lk, a_own, a_all, 16))
    final.wait()
    lk.flush()


def backward(*args):
    return pl.pallas_call(
        bwd_kernel,
        out_shape=BWD_OUT,
        in_specs=[ANY] * BWD_IN,
        out_specs=[ANY] * len(BWD_OUT),
        scratch_shapes=sems(128) + BWD_SCRATCH + BWD_WORK + Z_RING * 2 + down_scratch()
        + [v for cols in PIECES for v in ring_scratch(cols)],
        compiler_params=pltpu.CompilerParams(
            collective_id=1, has_side_effects=True, vmem_limit_bytes=62 * 2**20
        ),
    )(*args)


def body(
    inputs, starts, w_query, key_weight, value_weight, w_out, w_gate, w_up, w_down,
    prenorm, midnorm, querynorm, keynorm, cotangent,
):
    z = lax.axis_index("seq")
    dp = lax.axis_index("dp")
    lane = jnp.arange(128)[None, :]
    line = jnp.arange(32)[:, None]

    def spread(v, row, start):
        here = jnp.pad(v, (0, 128 - v.shape[0]))
        return jnp.where(line == row, jnp.roll(here, start)[None, :], 0)

    both = dp % 4 * 32
    gains = spread(prenorm, 8 + dp // 4, both) + spread(midnorm, 16 + dp // 4, both)
    for row, v in ((0, querynorm), (1, keynorm)):
        gains = gains + spread(v, row, 2 * dp) + spread(v, row, 2 * dp + 64)
    wa = jnp.concatenate([w_query, key_weight, value_weight, gains, w_out], axis=1)
    gu = jnp.concatenate(
        [lax.dynamic_slice(w, (0, z * 1152), (32, 1152)) for w in (w_gate, w_up)], axis=1
    )
    pos = z * 128 + jnp.arange(128, dtype=jnp.int32)
    inside = pos - starts[:, 0]
    frequency = ROPE_BASE ** (-(jnp.arange(32, dtype=F32) * 2.0 / 64))
    angle = inside.reshape(256, 1).astype(F32) * frequency[None, :]
    cosine, sine = jnp.cos(angle), jnp.sin(angle)
    tab = jnp.concatenate([cosine, cosine, -sine, sine], axis=1)
    source = inputs.reshape(256, 1024)
    upstream = cotangent.reshape(256, 1024)
    (
        whole, normed, lin_query, lin_key, keys, values, queries, probs, mixed, middle, gain, grad_gu, grad_down,
        out_part, grad_ffn,
    ) = forward(wa, gu, w_down, source, upstream, tab, starts[:, 0])
    outputs, grad_inputs, own_whole, own_gu, own_down, _, _ = backward(
        whole, normed, lin_query, lin_key, keys, values, queries, probs, mixed, middle, gain, out_part, grad_ffn,
        upstream, source, tab, grad_gu, grad_down,
    )
    own = jnp.sum(own_whole.astype(F32), axis=0)
    own_gu = own_gu.astype(F32).transpose(1, 0, 2)
    grad_gains = own[:, 2048:2176]
    return (
        outputs.reshape(2, 1, 128, 1024),
        grad_inputs.reshape(2, 1, 128, 1024),
        own[:, :1024],
        own[:, 1024:1536],
        own[:, 1536:2048],
        own[:, 2176:],
        own_gu[:, :, :1152].reshape(32, 4608),
        own_gu[:, :, 1152:].reshape(32, 4608),
        own_down.astype(F32),
        lax.dynamic_slice(grad_gains, (8, both), (1, 32))[0],
        lax.dynamic_slice(grad_gains, (16, both), (1, 32))[0],
        lax.dynamic_slice(grad_gains, (0, 2 * dp), (1, 2))[0],
        lax.dynamic_slice(grad_gains, (0, 64 + 2 * dp), (1, 2))[0],
    )


def solution(mesh):
    tokens, matrix, vector = P(None, "dp", "seq", None), P("dp", None), P("dp")
    return jax.shard_map(
        body,
        mesh=mesh,
        in_specs=(tokens, P(None, "dp", "seq")) + (matrix,) * 7 + (vector,) * 4 + (tokens,),
        out_specs=(tokens, tokens) + (matrix,) * 7 + (vector,) * 4,
        check_vma=False,
    )
```

```python
from functools import partial

import jax
import jax.numpy as jnp
from jax import lax
from jax.experimental import pallas as pl
from jax.experimental.pallas import tpu as pltpu
from jax.sharding import PartitionSpec as P

QUERY_HEADS = 16
KEY_VALUE_HEADS = 8
HEAD_SIZE = 64
EPS = 1e-05
ROPE_BASE = 1000000.0

MESH = pl.DeviceIdType.MESH
BF = jnp.bfloat16
F32 = jnp.float32
WA = 3200
GU = 2304
DN = 144


class Links:
    def __init__(self, send, recv, local):
        dp = lax.axis_index("dp")
        self.z = lax.axis_index("seq")
        self.x, self.y, self.c = dp // 8, (dp // 2) % 4, dp % 2
        self.send, self.recv, self.local = send, recv, local
        self.n = self.m = 0
        self.out = []
        self.other = 1 - self.c
        place = {"x": self.x, "y": self.y, "z": self.z}
        self.ring = {k: ((v + 3) % 4, (v + 1) % 4, (v + 2) % 4) for k, v in place.items()}
        self.past_x = (self.x - self.z + 4) % 4
        self.past_z = (self.z - self.x + 4) % 4
        self.near = {("c", 1): self.dev(self.x, self.y, self.other, self.z)}
        for k, (before, after, far) in self.ring.items():
            for step, v in ((-1, before), (1, after)):
                spot = dict(place, **{k: v})
                self.near[k, step] = self.dev(spot["x"], spot["y"], self.c, spot["z"])

    def dev(self, x, y, c, z):
        return ((x * 4 + y) * 2 + c, z)

    def nbr(self, axis, step):
        return self.near[axis, step]

    def sides(self, axis):
        return self.nbr(axis, 1), self.nbr(axis, -1)

    def barrier(self, axes):
        sem = pltpu.get_barrier_semaphore()
        count = 0
        for axis in axes:
            for step in (1,) if axis == "c" else (1, -1):
                pl.semaphore_signal(sem, inc=1, device_id=self.nbr(axis, step), device_id_type=MESH)
                count += 1
        pl.semaphore_wait(sem, count)

    def make(self, src, dst, to):
        copy = pltpu.make_async_remote_copy(
            src_ref=src,
            dst_ref=dst,
            send_sem=self.send.at[self.n],
            recv_sem=self.recv.at[self.n],
            device_id=to,
            device_id_type=MESH,
        )
        self.n += 1
        assert self.n <= self.send.shape[0]
        return copy

    def put(self, src, dst, to):
        copy = self.make(src, dst, to)
        copy.start()
        self.out.append(copy)
        return copy

    def keep(self, src, dst):
        copy = pltpu.make_async_copy(src, dst, self.local.at[self.m])
        self.m += 1
        assert self.m <= self.local.shape[0]
        copy.start()
        return copy

    def flush(self):
        for copy in self.out:
            copy.wait_send()
        self.out = []


def drive(*steps):
    steps = list(steps)
    while steps:
        steps = [s for s in steps if next(s, "end") != "end"]


def ring_gather(lk, own, slot, part, axis, me, ready=None):
    right, left = lk.sides(axis)
    before, after, far = lk.ring[axis]
    a = lk.put(own, slot(me), right)
    b = lk.put(own, slot(me), left)
    yield 1
    a.wait_recv()
    c = lk.put(part(before, 0), part(before, 0), right)
    if ready:
        ready(before)
    b.wait_recv()
    d = lk.put(part(after, 1), part(after, 1), left)
    if ready:
        ready(after)
    yield 1
    c.wait_recv()
    d.wait_recv()
    if ready:
        ready(far)


def plane_gather(lk, own, out, first, lo, hi):
    cols = pl.ds(lo, hi - lo)
    x, y, c = lk.x, lk.y, lk.c
    kept = lk.keep(own.at[:, cols], out.at[x, y, c, :, cols])
    crossing = []

    def cross(ref):
        crossing.append(lk.put(ref, ref, lk.nbr("c", 1)))

    def rows(k):
        return pl.ds(16 * k, 16)

    def two(k):
        return pl.ds(2 * k, 2)

    if first == "x":
        yield from ring_gather(
            lk, own.at[:, cols], lambda i: out.at[i, y, c, :, cols],
            lambda i, k: out.at[i, y, c, rows(k), cols], "x", x,
        )
        kept.wait()
        whole = out.at[:, y, c, :, cols]
        cross(whole)
        yield from ring_gather(
            lk, whole, lambda j: out.at[:, j, c, :, cols],
            lambda j, k: out.at[two(k), j, c, :, cols], "y", y,
            lambda j: cross(out.at[:, j, c, :, cols]),
        )
    else:
        yield from ring_gather(
            lk, own.at[:, cols], lambda j: out.at[x, j, c, :, cols],
            lambda j, k: out.at[x, j, c, rows(k), cols], "y", y,
        )
        kept.wait()
        whole = out.at[x, :, c, :, cols]
        cross(whole)
        yield from ring_gather(
            lk, whole, lambda i: out.at[i, :, c, :, cols],
            lambda i, k: out.at[i, two(k), c, :, cols], "x", x,
            lambda i: cross(out.at[i, :, c, :, cols]),
        )
    yield 1
    for copy in crossing:
        copy.wait_recv()


def ring_spread(lk, own, dst, part, axis, place):
    right, left = lk.sides(axis)
    a, b = lk.make(own, dst, right), lk.make(own, dst, left)
    c, d = lk.make(part(0), part(0), right), lk.make(part(1), part(1), left)
    kept = pltpu.make_async_copy(own, dst, lk.local.at[lk.m])
    lk.m += 1

    @pl.when(place == 0)
    def _():
        a.start()
        b.start()
        kept.start()

    yield 1

    @pl.when(place == 1)
    def _():
        a.wait_recv()
        c.start()

    @pl.when(place == 3)
    def _():
        b.wait_recv()
        d.start()

    yield 1

    @pl.when(place == 2)
    def _():
        c.wait_recv()
        d.wait_recv()

    @pl.when(place == 0)
    def _():
        kept.wait()
        a.wait_send()
        b.wait_send()

    @pl.when(place == 1)
    def _():
        c.wait_send()

    @pl.when(place == 3)
    def _():
        d.wait_send()


def down_part(k):
    return pl.ds(0, 80) if k == 0 else pl.ds(80, 64)


def down_gather(lk, own, out):
    y, c = lk.y, lk.c
    yield from ring_spread(
        lk, own, out.at[y, c], lambda k: out.at[y, c, down_part(k)], "x", lk.past_x
    )
    crossing = []

    def cross(j):
        crossing.append(lk.put(out.at[j, c], out.at[j, c], lk.nbr("c", 1)))

    cross(y)
    yield from ring_gather(
        lk, out.at[y, c], lambda j: out.at[j, c], lambda j, k: out.at[j, c, down_part(k)], "y", y, cross
    )
    yield 1
    for copy in crossing:
        copy.wait_recv()


def line_gather(lk, own, out, cut):
    z, rows = lk.z, own.shape[0]
    kept = lk.keep(own, out.at[z])

    def part(i, k):
        return out.at[i, pl.ds(0, cut)] if k == 0 else out.at[i, pl.ds(cut, rows - cut)]

    yield from ring_gather(lk, own, lambda i: out.at[i], part, "z", z)
    kept.wait()


def add_into(dst, src):
    if len(dst.shape) == 2:
        dst[...] = (dst[...].astype(F32) + src[...].astype(F32)).astype(BF)
    else:
        for i in range(dst.shape[0]):
            dst[i] = (dst[i].astype(F32) + src[i].astype(F32)).astype(BF)


def ring_reduce(lk, p, part, bufs, axis, me):
    right, left = lk.sides(axis)
    r0, r1, ra, rb = bufs
    before, after, far = lk.ring[axis]
    a = lk.put(part(far, 0), r0, right)
    b = lk.put(part(far, 1), r1, left)
    yield 1
    a.wait_recv()
    add_into(part(after, 0), r0)
    c = lk.put(p(after), ra, right)
    b.wait_recv()
    add_into(part(before, 1), r1)
    d = lk.put(p(before), rb, left)
    yield 1
    c.wait_recv()
    add_into(p(me), ra)
    d.wait_recv()
    add_into(p(me), rb)


def plane_reduce(lk, spot, sib_src, sib, bufs, out, first, kept=None):
    x, y, c = lk.x, lk.y, lk.c
    one, two = bufs
    got = lk.put(sib_src, sib, lk.nbr("c", 1))
    yield 1
    if kept is not None:
        kept.wait()
    got.wait_recv()

    def step(i, _):
        ref = spot(i // 4, i % 4)
        ref[...] = (ref[...].astype(F32) + sib[i // 4, i % 4].astype(F32)).astype(BF)
        return 0

    lax.fori_loop(0, 16, step, 0)
    every = slice(None)

    def pair(k):
        return pl.ds(2 * k, 2)

    def rows(ref, k):
        return ref.at[pl.ds(16 * k, 16)]

    if first == "y":
        yield from ring_reduce(lk, lambda j: spot(every, j), lambda j, k: spot(pair(k), j), one, "y", y)
        yield from ring_reduce(lk, lambda i: spot(i, y), lambda i, k: rows(spot(i, y), k), two, "x", x)
    else:
        yield from ring_reduce(lk, lambda i: spot(i, every), lambda i, k: spot(i, pair(k)), one, "x", x)
        yield from ring_reduce(lk, lambda j: spot(x, j), lambda j, k: rows(spot(x, j), k), two, "y", y)
    yield 1
    yield from line_gather(lk, spot(x, y), out, 16)


def ring_scratch(cols):
    return [
        pltpu.VMEM((4, 4, 32, cols), BF),
        pltpu.VMEM((2, 32, cols), BF),
        pltpu.VMEM((2, 32, cols), BF),
        pltpu.VMEM((4, 32, cols), BF),
        pltpu.VMEM((4, 32, cols), BF),
        pltpu.VMEM((16, cols), BF),
        pltpu.VMEM((16, cols), BF),
        pltpu.VMEM((32, cols), BF),
        pltpu.VMEM((32, cols), BF),
    ]


def down_scratch():
    return [
        pltpu.VMEM((4, DN, 1024), BF),
        pltpu.VMEM((4, DN, 1024), BF),
        pltpu.VMEM((80, 1024), BF),
        pltpu.VMEM((64, 1024), BF),
        pltpu.VMEM((DN, 1024), BF),
        pltpu.VMEM((DN, 1024), BF),
        pltpu.VMEM((80, 1024), BF),
        pltpu.VMEM((64, 1024), BF),
        pltpu.VMEM((DN, 1024), BF),
        pltpu.VMEM((DN, 1024), BF),
    ]


def down_reduce(lk, part_hbm, s, out):
    acc, sib, one, (x0, x1, xa, xb) = s[0], s[1], s[2:6], s[6:10]
    y, c = lk.y, lk.c
    kept = lk.keep(part_hbm.at[:, c], acc)
    got = lk.put(part_hbm.at[:, 1 - c], sib, lk.nbr("c", 1))
    yield 1
    kept.wait()
    got.wait_recv()
    add_into(acc, sib)
    yield from ring_reduce(
        lk, lambda j: acc.at[j], lambda j, k: acc.at[j, down_part(k)], one, "y", y
    )
    mine = acc.at[y]
    right, left = lk.sides("x")
    place = lk.past_x
    a = lk.make(acc.at[y, down_part(0)], x0, left)
    b = lk.make(acc.at[y, down_part(1)], x1, right)
    e = lk.make(mine, xa, left)
    f = lk.make(mine, xb, right)

    @pl.when(place == 2)
    def _():
        a.start()
        b.start()

    yield 1

    @pl.when(place == 1)
    def _():
        a.wait_recv()
        add_into(acc.at[y, down_part(0)], x0)
        e.start()

    @pl.when(place == 3)
    def _():
        b.wait_recv()
        add_into(acc.at[y, down_part(1)], x1)
        f.start()

    yield 1

    @pl.when(place == 0)
    def _():
        e.wait_recv()
        add_into(mine, xa)
        f.wait_recv()
        add_into(mine, xb)

    @pl.when(place == 1)
    def _():
        e.wait_send()

    @pl.when(place == 3)
    def _():
        f.wait_send()

    @pl.when(place == 2)
    def _():
        a.wait_send()
        b.wait_send()

    yield from ring_spread(
        lk, mine, out, lambda k: out.at[down_part(k)], "z", lk.past_z
    )


ANY = pl.BlockSpec(memory_space=pl.ANY)


def sems(n):
    return [pltpu.SemaphoreType.DMA((n,)), pltpu.SemaphoreType.DMA((n,)), pltpu.SemaphoreType.DMA((40,))]


def params(number):
    return pltpu.CompilerParams(collective_id=number, has_side_effects=True, vmem_limit_bytes=56 * 2**20)


def shape(*dims, dtype=BF):
    return jax.ShapeDtypeStruct(dims, dtype)


def lanes_of(shape):
    return lax.broadcasted_iota(jnp.int32, shape, len(shape) - 1)


def dot(left, right, dims=((1,), (0,)), kind=F32):
    return lax.dot_general(left, right, (dims, ((), ())), preferred_element_type=F32).astype(kind)


TOKENS = ((0,), (0,))
ROWS = ((1,), (1,))


def flat(value):
    return value.reshape(-1, value.shape[-1])


def head_ones():
    row = lax.broadcasted_iota(jnp.int32, (256, 256), 0) // 64
    col = lax.broadcasted_iota(jnp.int32, (256, 256), 1) // 64
    return jnp.where(row == col, 1.0 / 64, 0.0).astype(BF)


def head_mean(v, ones):
    high = v.astype(BF)
    low = (v - high.astype(F32)).astype(BF)
    return dot(high, ones) + dot(low, ones)


def halves_swapped(v):
    lane = lanes_of(v.shape)
    return jnp.where(lane % 64 < 32, pltpu.roll(v, 96, 1), pltpu.roll(v, 32, 1))


def angle_tables(tab):
    lane = lanes_of(tab.shape)
    other = pltpu.roll(tab, 64, 1)
    return jnp.where(lane < 64, tab, other), jnp.where(lane < 64, other, tab)


def row_scale(v):
    return lax.rsqrt(jnp.mean(v * v, axis=-1, keepdims=True) + EPS)


def gain_rows(whole, gain):
    def step(i, total):
        return total + whole[i // 8, (i // 2) % 4, i % 2, :, pl.ds(2048, 128)].astype(F32)

    total = lax.fori_loop(0, 32, step, jnp.zeros((32, 128), F32))
    for k in range(8):
        gain[0:1, pl.ds(128 * k, 128)] = total[8 + k : 9 + k]
        gain[1:2, pl.ds(128 * k, 128)] = total[16 + k : 17 + k]
        gain[2:3, pl.ds(128 * k, 128)] = total[0:1]
        gain[3:4, pl.ds(128 * k, 128)] = total[1:2]


def keys_values(whole, sources, tables, gain, normed, keys, values, lin_key, own):
    ones = head_ones()

    def step(q, _):
        src = sources[q].astype(F32)
        normed[q] = (src * row_scale(src) * gain[0:1]).astype(BF)
        cosine, sine = angle_tables(tables[q])
        kn = gain[3:4, 0:128]
        lane = lanes_of((256, 128))

        def put(ref, tile, r):
            turned = pltpu.roll(r, 64, 1)
            even = jnp.where(lane < 64, r, turned).astype(BF)
            odd = jnp.where(lane < 64, turned, r).astype(BF)
            for m in range(2):
                ref[m, 2 * tile, pl.ds(q * 128, 128)] = even[128 * m : 128 * m + 128]
                ref[m, 2 * tile + 1, pl.ds(q * 128, 128)] = odd[128 * m : 128 * m + 128]

        for j in range(4):
            lin = dot(normed[q], flat(whole[:, :, :, :, pl.ds(1024 + 256 * j, 256)]))
            if j < 2:
                scale = lax.rsqrt(head_mean(lin * lin, ones) + EPS)

                @pl.when(q == own)
                def _():
                    lin_key[:, pl.ds(256 * j, 256)] = lin

                for h in range(2):
                    cut = slice(128 * h, 128 * h + 128)
                    v = lin[:, cut] * scale[:, cut] * kn
                    put(keys, 2 * j + h, v * cosine + halves_swapped(v) * sine)
            else:
                for h in range(2):
                    put(values, 2 * (j - 2) + h, lin[:, 128 * h : 128 * h + 128])
        return 0

    lax.fori_loop(0, 4, step, 0)


def own_queries(whole, tables, gain, normed, lin_query, queries, own):
    ones = head_ones()
    cosine, sine = angle_tables(tables[own])
    qn = gain[2:3, 0:128]
    lane = lanes_of((256, 128))

    def step(j, _):
        lin = dot(normed[own], flat(whole[:, :, :, :, pl.ds(pl.multiple_of(256 * j, 256), 256)]))
        lin_query[:, pl.ds(pl.multiple_of(256 * j, 256), 256)] = lin
        scale = lax.rsqrt(head_mean(lin * lin, ones) + EPS)
        for h in range(2):
            cut = slice(128 * h, 128 * h + 128)
            v = lin[:, cut] * scale[:, cut] * qn
            r = (v * cosine + halves_swapped(v) * sine) * HEAD_SIZE ** (-0.5)
            first = jnp.where(lane < 64, r, 0.0).astype(BF)
            second = jnp.where(lane < 64, 0.0, r).astype(BF)
            for m in range(2):
                queries[m, 2 * j + h, 0:128] = first[128 * m : 128 * m + 128]
                queries[m, 2 * j + h, 128:256] = second[128 * m : 128 * m + 128]
        return 0

    lax.fori_loop(0, 4, step, 0)


def attend(m, queries, keys, values, starts, probs, mixed, own):
    key_pos = lax.broadcasted_iota(jnp.int32, (512, 256), 0)
    query_pos = own * 128 + lax.broadcasted_iota(jnp.int32, (1, 256), 1) % 128
    lane = lanes_of((128, 128))

    row = starts[m : m + 1]
    begin = jnp.concatenate([row, row], axis=1)

    def step(k, _):
        scores = dot(keys[m, k], queries[m, k], ROWS)
        scores = jnp.where((key_pos <= query_pos) & (key_pos >= begin), scores, -1e30)
        raised = jnp.exp(scores - jnp.max(scores, axis=0, keepdims=True))
        chance = (raised * (1.0 / jnp.sum(raised, axis=0, keepdims=True))).astype(BF)
        probs[8 * m + k] = chance
        got = dot(values[m, k], chance, TOKENS).T
        both = jnp.where(lane < 64, got[0:128], got[128:256]).astype(BF)
        mixed[128 * m : 128 * m + 128, pl.ds(pl.multiple_of(k * 128, 128), 128)] = both
        return 0

    lax.fori_loop(0, 8, step, 0)


def out_project(m, whole, sources, gain, mixed, middle, normed_ffn, own):
    rows = pl.ds(128 * m, 128)

    def step(j, _):
        cut = pl.ds(pl.multiple_of(256 * j, 256), 256)
        w = flat(whole[:, :, :, :, pl.ds(pl.multiple_of(2176 + 256 * j, 128), 256)])
        middle[rows, cut] = sources[own, rows, cut].astype(F32) + dot(mixed[rows], w)
        return 0

    lax.fori_loop(0, 4, step, 0)
    mid = middle[rows]
    normed_ffn[own, rows] = (mid * row_scale(mid) * gain[1:2]).astype(BF)


def own_gains(params, dp):
    row = jnp.broadcast_to(params, (32, 128))
    line = lax.broadcasted_iota(jnp.int32, (32, 128), 0)
    lane = lanes_of((32, 128))
    spot = dp % 4 * 32
    window = (lane >= spot) & (lane < spot + 32)
    got = jnp.where((line == 8 + dp // 4) & window, pltpu.roll(row, spot, 1), 0.0)
    got = got + jnp.where((line == 16 + dp // 4) & window, pltpu.roll(row, (spot + 96) % 128, 1), 0.0)
    pair = (lane % 64 >= 2 * dp) & (lane % 64 < 2 * dp + 2)
    for k in range(2):
        low = pltpu.roll(row, (2 * dp + 64 - 2 * k) % 128, 1)
        high = pltpu.roll(row, (2 * dp + 128 - 2 * k) % 128, 1)
        got = got + jnp.where((line == k) & pair, jnp.where(lane < 64, low, high), 0.0)
    return got.astype(BF)


def feed_back_in(cots, down, grad_hidden):
    def step(i, _):
        grad_hidden[i] = dot(cots[i], flat(down[...]), ROWS, BF)
        return 0

    lax.fori_loop(0, 4, step, 0)


def feed_chunk(i, ffn, gate_up, down, grad_hidden, hidden, turned, ffn_turned, grad_both, grad_ffn, out_part):
    def step(j, _):
        cut = pl.ds(pl.multiple_of(384 * j, 128), 384)
        cut_up = pl.ds(pl.multiple_of(1152 + 384 * j, 128), 384)
        gated = dot(ffn[i], flat(gate_up[:, :, :, :, cut]))
        upward = dot(ffn[i], flat(gate_up[:, :, :, :, cut_up]))
        sigma = 1.0 / (1.0 + jnp.exp(-gated))
        silu = gated * sigma
        made = (silu * upward).astype(BF)
        hidden[:, cut] = made
        turned[i, cut] = made.T
        back = grad_hidden[i, :, cut].astype(F32)
        grad_both[i, :, cut] = (back * upward * sigma * (1.0 + gated * (1.0 - sigma))).astype(BF)
        grad_both[i, :, cut_up] = (back * silu).astype(BF)
        return 0

    lax.fori_loop(0, 3, step, 0)

    def last(j, _):
        cut = pl.ds(pl.multiple_of(256 * j, 256), 256)
        grad_ffn[i, :, cut] = dot(grad_both[i], flat(gate_up[j]), ROWS, BF)
        out_part[i, :, cut] = dot(hidden[...], flat(down[:, :, :, cut]), kind=BF)
        ffn_turned[i, cut] = ffn[i, :, cut].T
        return 0

    lax.fori_loop(0, 4, last, 0)


def feed_grads(left, right, out, tiles):
    def step(j, _):
        cut = pl.ds(pl.multiple_of(256 * j, 256), 256)
        got = dot(left[0], right[0, :, cut])
        for i in range(1, 4):
            got = got + dot(left[i], right[i, :, cut])
        lead = out.shape[:-1]
        out[(slice(None),) * len(lead) + (cut,)] = got.astype(BF).reshape(*lead, 256)
        return 0

    lax.fori_loop(0, tiles, step, 0)


FWD_SCRATCH = [
    pltpu.VMEM((4, 4, 2, 32, WA), BF),
    pltpu.VMEM((4, 4, 2, 32, GU), BF),
    pltpu.VMEM((4, 2, DN, 1024), BF),
    pltpu.VMEM((4, 256, 1024), BF),
    pltpu.VMEM((4, 256, 128), F32),
    pltpu.VMEM((4, 256, 1024), BF),
    pltpu.VMEM((4, 256, 1024), BF),
    pltpu.VMEM((4, 256, 1024), BF),
    pltpu.VMEM((256, 1024), F32),
    pltpu.VMEM((256, 512), F32),
    pltpu.VMEM((2, 8, 512, 128), BF),
    pltpu.VMEM((2, 8, 512, 128), BF),
    pltpu.VMEM((2, 8, 256, 128), BF),
    pltpu.VMEM((16, 512, 256), BF),
    pltpu.VMEM((256, 1024), BF),
    pltpu.VMEM((256, 1024), F32),
    pltpu.VMEM((8, 1024), F32),
    pltpu.VMEM((4, 256, 1152), BF),
    pltpu.VMEM((256, 1152), BF),
    pltpu.VMEM((4, 1152, 256), BF),
    pltpu.VMEM((4, 1024, 256), BF),
    pltpu.VMEM((4, 256, GU), BF),
    pltpu.VMEM((4, 256, 1024), BF),
    pltpu.VMEM((4, 256, 1024), BF),
    pltpu.VMEM((256, 1024), BF),
    pltpu.VMEM((256, 1024), BF),
    pltpu.VMEM((4, 64, 1024), BF),
    pltpu.VMEM((4, 64, 1024), BF),
    pltpu.VMEM((2, 128), jnp.int32),
    pltpu.VMEM((32, WA), BF),
    pltpu.VMEM((32, GU), BF),
    pltpu.VMEM((1, 128), F32),
]

FWD_OUT = (
    shape(4, 4, 2, 32, WA),
    shape(256, 1024),
    shape(256, 1024, dtype=F32),
    shape(256, 512, dtype=F32),
    shape(2, 8, 512, 128),
    shape(2, 8, 512, 128),
    shape(2, 8, 256, 128),
    shape(16, 512, 256),
    shape(256, 1024),
    shape(256, 1024, dtype=F32),
    shape(8, 1024, dtype=F32),
    shape(4, 4, 2, 32, GU),
    shape(4, 2, DN, 1024),
    shape(4, 256, 1024),
    shape(256, 1024, dtype=F32),
)


FWD_IN = 12


def go(*steps):
    for s in steps:
        next(s, None)


def fwd_kernel(*refs):
    w_query, key_weight, value_weight, w_out, w_gate, w_up, dn, x, cot, tab, starts_hbm, params_hbm = refs[:FWD_IN]
    refs = refs[FWD_IN:]
    outs, refs = refs[: len(FWD_OUT)], refs[len(FWD_OUT) :]
    lk = Links(*refs[:3])
    (
        whole, gate_up, down, sources, tables, cots, ffn, normed, lin_query, lin_key, keys, values, queries,
        probs, mixed, middle, gain, grad_hidden, hidden, turned, ffn_turned, grad_both, grad_ffn, out_part,
        from_right, from_left, passing, from_far, starts, wa, gu, own_params,
    ) = refs[3:]
    own = lk.z
    before, after, far = lk.ring["z"]
    quarter = pl.ds(pl.multiple_of(own * 1152, 128), 1152)
    staged = [
        lk.keep(params_hbm, own_params),
        lk.keep(starts_hbm, starts),
        lk.keep(w_query, wa.at[:, pl.ds(0, 1024)]),
        lk.keep(key_weight, wa.at[:, pl.ds(1024, 512)]),
        lk.keep(value_weight, wa.at[:, pl.ds(1536, 512)]),
        lk.keep(w_out, wa.at[:, pl.ds(2176, 1024)]),
        lk.keep(w_gate.at[:, quarter], gu.at[:, pl.ds(0, 1152)]),
        lk.keep(w_up.at[:, quarter], gu.at[:, pl.ds(1152, 1152)]),
    ]
    staged[0].wait()
    wa[:, 2048:2176] = own_gains(own_params[...], lax.axis_index("dp"))
    for copy in staged[1:]:
        copy.wait()
    lk.barrier("xyzc")
    a1 = plane_gather(lk, wa, whole, "x", 0, 1536)
    a2 = plane_gather(lk, wa, whole, "y", 1536, WA)
    t1 = line_gather(lk, tab, tables, 128)
    x1 = line_gather(lk, x, sources, 128)
    g1 = plane_gather(lk, gu, gate_up, "x", 0, 1152)
    g2 = plane_gather(lk, gu, gate_up, "y", 1152, GU)
    d1 = down_gather(lk, dn, down)
    c1 = line_gather(lk, cot, cots, 128)
    go(a1, a2, t1, x1)
    go(a1, a2)
    go(g1, g2)
    go(a1, a2)
    go(t1, x1)
    go(a1, a2)
    go(g1, g2)
    go(a1, a2)
    go(g1, g2)
    go(d1)
    go(t1, x1)
    go(c1)
    drive(a1, a2, t1, x1)
    gain_rows(whole, gain)
    saved = [lk.keep(whole, outs[0])]
    keys_values(whole, sources, tables, gain, normed, keys, values, lin_key, own)
    go(g1, g2)
    go(d1)
    go(c1)
    own_queries(whole, tables, gain, normed, lin_query, queries, own)
    for k, ref in enumerate((normed.at[own], lin_query, lin_key, keys, values, queries)):
        saved.append(lk.keep(ref, outs[1 + k]))
    passed = []
    for m in range(2):
        attend(m, queries, keys, values, starts, probs, mixed, own)
        out_project(m, whole, sources, gain, mixed, middle, ffn, own)
        rows = pl.ds(128 * m, 128)

        def part(i, k, m=m):
            return ffn.at[i, pl.ds(128 * m + 64 * k, 64)]

        passed.append(
            ring_gather(lk, ffn.at[own, rows], lambda i, rows=rows: ffn.at[i, rows], part, "z", own)
        )
        go(passed[m])
        if m == 0:
            go(g1, g2)
            go(d1)
            go(c1)
    go(passed[0])
    for k, ref in enumerate((probs, mixed, middle, gain)):
        saved.append(lk.keep(ref, outs[7 + k]))
    drive(g1, g2, d1, c1)
    feed_back_in(cots, down, grad_hidden)
    go(*passed)

    def chunk(i):
        feed_chunk(
            i, ffn, gate_up, down, grad_hidden, hidden, turned, ffn_turned, grad_both, grad_ffn, out_part
        )

    right, left = lk.sides("z")
    chunk(own)
    lk.flush()
    chunk(before)
    sent = [lk.put(grad_ffn.at[before], from_right, left)]
    chunk(after)
    sent.append(lk.put(grad_ffn.at[after], from_left, right))
    go(*passed)
    chunk(far)
    saved.append(lk.keep(out_part, outs[13]))
    hops = []
    for k in range(4):
        to = right if k % 2 == 0 else left
        hops.append((lk.put(grad_ffn.at[far, pl.ds(64 * k, 64)], passing.at[k], to), to))
    feed_grads(ffn_turned, grad_both, gate_up, 9)
    saved.append(lk.keep(gate_up, outs[11]))
    for k, (copy, to) in enumerate(hops):
        copy.wait_recv()
        sent.append(lk.put(passing.at[k], from_far.at[k], to))
    feed_grads(turned, cots, down, 4)
    saved.append(lk.keep(down, outs[12]))
    for copy in sent:
        copy.wait_recv()
    for copy in saved:
        copy.wait()
    total = grad_ffn[own].astype(F32) + from_right[...].astype(F32) + from_left[...].astype(F32)
    lin_query[...] = total + flat(from_far[...]).astype(F32)
    lk.keep(lin_query, outs[14]).wait()
    lk.flush()


def forward(*args):
    return pl.pallas_call(
        fwd_kernel,
        out_shape=FWD_OUT,
        in_specs=[ANY] * FWD_IN,
        out_specs=[ANY] * len(FWD_OUT),
        scratch_shapes=sems(96) + FWD_SCRATCH,
        compiler_params=pltpu.CompilerParams(
            collective_id=0, has_side_effects=True, vmem_limit_bytes=60 * 2**20
        ),
    )(*args)


BWD_IN = 18
PIECES = (1152, 1152, 512, 512, 512, 512, 512, 640)
BWD_OUT = (
    shape(256, 1024),
    shape(256, 1024, dtype=F32),
    shape(4, 32, WA),
    shape(4, 32, GU),
    shape(DN, 1024),
)
BWD_SCRATCH = [
    pltpu.VMEM((4, 4, 2, 32, WA), BF),
    pltpu.VMEM((256, 1024), BF),
    pltpu.VMEM((256, 1024), F32),
    pltpu.VMEM((256, 512), F32),
    pltpu.VMEM((2, 8, 512, 128), BF),
    pltpu.VMEM((2, 8, 512, 128), BF),
    pltpu.VMEM((2, 8, 256, 128), BF),
    pltpu.VMEM((16, 512, 256), BF),
    pltpu.VMEM((256, 1024), BF),
    pltpu.VMEM((256, 1024), F32),
    pltpu.VMEM((8, 1024), F32),
    pltpu.VMEM((4, 256, 1024), BF),
    pltpu.VMEM((256, 1024), F32),
    pltpu.VMEM((256, 1024), BF),
    pltpu.VMEM((256, 1024), BF),
    pltpu.VMEM((256, 128), F32),
]
BWD_WORK = [
    pltpu.VMEM((256, 1024), BF),
    pltpu.VMEM((2, 8, 256, 128), BF),
    pltpu.VMEM((256, 1024), F32),
    pltpu.VMEM((4, 256, 1024), BF),
    pltpu.VMEM((256, 2048), BF),
    pltpu.VMEM((1024, 256), BF),
    pltpu.VMEM((256, 1024), F32),
    pltpu.VMEM((8, 1024), F32),
    pltpu.VMEM((4, 4, 2, 32, WA), BF),
    pltpu.VMEM((4, 4, 32, 1152), BF),
    pltpu.VMEM((4, 4, 32, 1152), BF),
    pltpu.VMEM((256, 1024), BF),
]
Z_RING = [
    pltpu.VMEM((128, 1024), BF),
    pltpu.VMEM((128, 1024), BF),
    pltpu.VMEM((256, 1024), BF),
    pltpu.VMEM((256, 1024), BF),
]
Z_HALF = [
    pltpu.VMEM((64, 1024), BF),
    pltpu.VMEM((64, 1024), BF),
    pltpu.VMEM((128, 1024), BF),
    pltpu.VMEM((128, 1024), BF),
]


def norm_back(v, g, dy):
    r = row_scale(v)
    gdy = g * dy
    back = r * gdy - v * (r * r * r * jnp.mean(v * gdy, axis=-1, keepdims=True))
    return back, jnp.sum(v * r * dy, axis=0, keepdims=True)


def heads_back(lin, grad, gain, cosine, sine, ones):
    parts = []
    for h in range(2):
        part = grad[:, 128 * h : 128 * h + 128]
        parts.append(part * cosine + halves_swapped(part * sine))
    dy = jnp.concatenate(parts, axis=1)
    r = lax.rsqrt(head_mean(lin * lin, ones) + EPS)
    gdy = dy * gain
    back = r * gdy - lin * (r * r * r * head_mean(lin * gdy, ones))
    return back, jnp.sum(lin * r * dy, axis=0, keepdims=True)


def turned_grads(turned, right, out, start, tiles, base=0):
    def step(j, _):
        got = dot(turned[...], right[:, pl.ds(pl.multiple_of(base + 256 * j, 256), 256)], kind=BF)
        out[:, :, :, :, pl.ds(pl.multiple_of(start + 256 * j, 128), 256)] = got.reshape(4, 4, 2, 32, 256)
        return 0

    lax.fori_loop(0, tiles, step, 0)


def attend_back(m, queries, keys, values, probs, grad_mixed, grad_queries, grad_kv):
    lane = lanes_of((128, 128))
    lane_keys = lanes_of((512, 128))

    def step(j, _):
        folded = []
        for e in range(2):
            k = 2 * j + e
            i = m * 8 + k
            chance = probs[i]
            back = dot(values[m, k], grad_mixed[m, k], ROWS)
            p = chance.astype(F32)
            p_back = p * back
            grad_scores = (p_back - p * jnp.sum(p_back, axis=0, keepdims=True)).astype(BF)
            got = dot(keys[m, k], grad_scores, TOKENS).T
            cut = pl.ds(pl.multiple_of(128 * k, 128), 128)
            grad_queries[pl.ds(128 * m, 128), cut] = jnp.where(
                lane < 64, got[0:128], got[128:256]
            )
            for v in (dot(grad_scores, queries[m, k]), dot(chance, grad_mixed[m, k])):
                folded.append(v + pltpu.roll(v, 64, 1))
        for s in range(2):
            tile = jnp.where(lane_keys < 64, folded[s], folded[2 + s]).astype(BF)
            cut = pl.ds(pl.multiple_of(512 * s + 128 * j, 128), 128)
            for q in range(4):
                grad_kv[q, pl.ds(128 * m, 128), cut] = tile[128 * q : 128 * q + 128]

        return 0

    lax.fori_loop(0, 4, step, 0)


def bwd_kernel(*refs):
    ins, refs = refs[:BWD_IN], refs[BWD_IN:]
    outs, refs = refs[: len(BWD_OUT)], refs[len(BWD_OUT) :]
    lk = Links(*refs[:3])
    refs = refs[3:]
    n = len(BWD_SCRATCH)
    held, refs = refs[:n], refs[n:]
    (
        whole, normed, lin_query, lin_key, keys, values, queries, probs, mixed, middle, gain, out_part, grad_middle,
        upstream, source, table,
    ) = held
    grad_gu, grad_down = ins[16:]
    n = len(BWD_WORK)
    work, refs = refs[:n], refs[n:]
    (
        grad_branch, grad_mixed, grad_queries, grad_kv, grad_lin, turned, grad_normed, gains_back, grad_whole, acc_a,
        acc_b, made,
    ) = work
    z_out, z_kv, refs = refs[:4], refs[4:12], refs[12:]
    down_refs, refs = refs[:10], refs[10:]
    rings = [refs[9 * i : 9 * i + 9] for i in range(len(PIECES))]
    outputs, grad_inputs, a_all, gu_all, down_own = outs
    own, c = lk.z, lk.c

    order = [12, 9, 13, 10, 0, 8, 5, 7, 6, 4, 11, 2, 15, 1, 3, 14]
    loads = {}
    for k in order[:6]:
        loads[k] = lk.keep(ins[k], held[k])
    lk.barrier("xyzc")

    def piece(k, spot, src, out, first, kept=None):
        ring = rings[k]
        return plane_reduce(lk, spot, src, ring[0], (ring[1:5], ring[5:9]), out, first, kept)

    def feed_piece(k, acc, lo, first):
        cols = pl.ds(lo, 1152)
        kept = lk.keep(grad_gu.at[:, :, c, :, cols], acc)
        return piece(
            k, lambda i, j: acc.at[i, j], grad_gu.at[:, :, lk.other, :, cols], gu_all.at[:, :, cols], first, kept
        )

    def whole_piece(k, lo, first):
        cols = pl.ds(lo, PIECES[k])
        return piece(
            k, lambda i, j: grad_whole.at[i, j, c, :, cols], grad_whole.at[:, :, lk.other, :, cols],
            a_all.at[:, :, cols], first,
        )

    def out_chain():
        yield from ring_reduce(
            lk, lambda i: out_part.at[i], lambda i, k: out_part.at[i, pl.ds(128 * k, 128)], z_out, "z", own
        )
        made[...] = (middle[...] + out_part[own].astype(F32)).astype(BF)
        done = lk.keep(made, outputs)
        yield 1
        done.wait()

    def need(*names):
        for k in names:
            loads.pop(k).wait()

    f1, f2 = feed_piece(0, acc_a, 0, "y"), feed_piece(1, acc_b, 1152, "x")
    d1 = down_reduce(lk, grad_down, down_refs, down_own)
    go(f1, f2, d1)
    for k in order[6:]:
        loads[k] = lk.keep(ins[k], held[k])
    need(12, 9, 13, 10)
    back, row = norm_back(middle[...], gain[1:2], grad_middle[...])
    total = upstream[...].astype(F32) + back
    grad_middle[...] = total
    grad_branch[...] = total.astype(BF)
    gains_back[1:2] = row
    need(0, 8)
    lane = lanes_of((256, 128))

    def back_mixed(j, _):
        got = dot(grad_branch[...], flat(whole[j, :, :, :, pl.ds(2176, 1024)]), ROWS)
        for h in range(2):
            r = got[:, 128 * h : 128 * h + 128]
            first = jnp.where(lane < 64, r, 0.0).astype(BF)
            second = jnp.where(lane < 64, 0.0, r).astype(BF)
            for m in range(2):
                grad_mixed[m, 2 * j + h, 0:128] = first[128 * m : 128 * m + 128]
                grad_mixed[m, 2 * j + h, 128:256] = second[128 * m : 128 * m + 128]
        return 0

    lax.fori_loop(0, 4, back_mixed, 0)
    go(f1, f2, d1)
    need(5, 7, 6, 4)
    z_kv_m = []
    for m in range(2):
        attend_back(m, queries, keys, values, probs, grad_mixed, grad_queries, grad_kv)
        rows = pl.ds(128 * m, 128)

        def part(i, k, m=m):
            return grad_kv.at[i, pl.ds(128 * m + 64 * k, 64)]

        z_kv_m.append(
            ring_reduce(lk, lambda i, rows=rows: grad_kv.at[i, rows], part, z_kv[4 * m : 4 * m + 4], "z", own)
        )
        go(z_kv_m[m])
        go(f1, f2, d1)
    turned[...] = mixed[...].T
    turned_grads(turned, grad_branch, grad_whole, 2176, 4)
    p2, p3 = whole_piece(2, 2176, "y"), whole_piece(3, 2688, "x")
    go(p2, p3)
    go(*z_kv_m)
    go(f1, f2, d1)
    need(2, 15, 1)
    ones = head_ones()
    cosine, sine = angle_tables(table[...])

    def back_query(j, _):
        cut = pl.ds(pl.multiple_of(256 * j, 256), 256)
        grad = grad_queries[:, cut] * HEAD_SIZE ** (-0.5)
        got, line = heads_back(lin_query[:, cut], grad, gain[2:3, 0:256], cosine, sine, ones)
        grad_lin[:, cut] = got.astype(BF)
        gains_back[2:3, cut] = line
        return 0

    lax.fori_loop(0, 4, back_query, 0)
    go(p2, p3)
    go(f1, f2, d1)
    turned[...] = normed[...].T
    turned_grads(turned, grad_lin, grad_whole, 0, 4)
    p4, p5 = whole_piece(4, 0, "y"), whole_piece(5, 512, "x")
    go(p4, p5)
    go(p2, p3)
    go(f1, f2, d1)
    need(3, 14, 11)
    drive(*z_kv_m)

    def back_key(j, _):
        cut = pl.ds(pl.multiple_of(256 * j, 256), 256)
        grad = grad_kv[own, :, cut].astype(F32)
        got, line = heads_back(lin_key[:, cut], grad, gain[3:4, 0:256], cosine, sine, ones)
        grad_lin[:, pl.ds(pl.multiple_of(1024 + 256 * j, 256), 256)] = got.astype(BF)
        gains_back[3:4, cut] = line
        return 0

    lax.fori_loop(0, 2, back_key, 0)
    grad_lin[:, 1536:2048] = grad_kv[own, :, 512:1024]

    def back_normed(j, _):
        grad_normed[:, pl.ds(pl.multiple_of(256 * j, 256), 256)] = dot(
            grad_lin[...], flat(whole[j, :, :, :, pl.ds(0, 2048)]), ROWS
        )
        return 0

    lax.fori_loop(0, 4, back_normed, 0)
    back, row = norm_back(source[...].astype(F32), gain[0:1], grad_normed[...])
    gains_back[0:1] = row
    grad_normed[...] = grad_middle[...] + back
    small = [jnp.zeros((1, 128), F32)] * 2
    for s, tiles in ((0, 8), (1, 4)):
        for k in range(tiles):
            small[s] = small[s] + gains_back[2 + s : 3 + s, 128 * k : 128 * k + 128]
        small[s] = small[s] + pltpu.roll(jnp.broadcast_to(small[s], (8, 128)), 64, 1)[0:1]
    heads = jnp.where(lanes_of((1, 128)) < 64, small[0], small[1])
    line = lax.broadcasted_iota(jnp.int32, (32, 128), 0)
    for k in range(8):
        cut = slice(128 * k, 128 * k + 128)
        block = jnp.where(line == 8, gains_back[0:1, cut], 0.0)
        block = jnp.where(line == 16, gains_back[1:2, cut], block)
        block = jnp.where(line == 0, heads, block).astype(BF)
        for d in range(4 * k, 4 * k + 4):
            grad_whole[d // 8, (d // 2) % 4, d % 2, :, 2048:2176] = block
    turned_grads(turned, grad_lin, grad_whole, 1024, 4, 1024)
    p6, p7 = whole_piece(6, 1024, "y"), whole_piece(7, 1536, "x")
    go(p6, p7)
    final = lk.keep(grad_normed, grad_inputs)
    o1 = out_chain()
    go(o1)
    go(p4, p5)
    go(p2, p3)
    drive(p6, p7, p4, p5, p2, p3, f1, f2, d1, o1)
    final.wait()
    lk.flush()


def backward(*args):
    return pl.pallas_call(
        bwd_kernel,
        out_shape=BWD_OUT,
        in_specs=[ANY] * BWD_IN,
        out_specs=[ANY] * len(BWD_OUT),
        scratch_shapes=sems(160) + BWD_SCRATCH + BWD_WORK + Z_RING + Z_HALF * 2 + down_scratch()
        + [v for cols in PIECES for v in ring_scratch(cols)],
        compiler_params=pltpu.CompilerParams(
            collective_id=1, has_side_effects=True, vmem_limit_bytes=62 * 2**20
        ),
    )(*args)


def finish_kernel(outputs, grad_inputs, a_all, gu_all, down, *outs):
    o_out, o_in, o_query, o_key, o_value, o_wout, o_gate, o_up, o_down, o_gains = outs
    o_out[...] = outputs[...]
    o_in[...] = grad_inputs[...]
    for ref, lo, size in (
        (o_query, 0, 1024), (o_key, 1024, 512), (o_value, 1536, 512), (o_gains, 2048, 128), (o_wout, 2176, 1024),
    ):
        total = a_all[0, :, lo : lo + size].astype(F32)
        for i in range(1, 4):
            total = total + a_all[i, :, lo : lo + size].astype(F32)
        ref[...] = total
    for i in range(4):
        o_gate[:, 1152 * i : 1152 * i + 1152] = gu_all[i, :, 0:1152].astype(F32)
        o_up[:, 1152 * i : 1152 * i + 1152] = gu_all[i, :, 1152:2304].astype(F32)
    o_down[...] = down[...].astype(F32)


def finish(*args):
    return pl.pallas_call(
        finish_kernel,
        out_shape=(
            shape(256, 1024), shape(256, 1024, dtype=F32), shape(32, 1024, dtype=F32), shape(32, 512, dtype=F32),
            shape(32, 512, dtype=F32), shape(32, 1024, dtype=F32), shape(32, 4608, dtype=F32),
            shape(32, 4608, dtype=F32), shape(DN, 1024, dtype=F32), shape(32, 128, dtype=F32),
        ),
        compiler_params=pltpu.CompilerParams(vmem_limit_bytes=32 * 2**20),
    )(*args)


def body(
    inputs, starts, w_query, key_weight, value_weight, w_out, w_gate, w_up, w_down,
    prenorm, midnorm, querynorm, keynorm, cotangent,
):
    z = lax.axis_index("seq")
    dp = lax.axis_index("dp")
    params = jnp.concatenate([prenorm, midnorm, querynorm, keynorm, jnp.zeros((60,), BF)])
    params = params.astype(F32).reshape(1, 128)
    pos = z * 128 + jnp.arange(128, dtype=jnp.int32)
    inside = pos - starts[:, 0]
    frequency = ROPE_BASE ** (-(jnp.arange(32, dtype=F32) * 2.0 / 64))
    angle = inside.reshape(256, 1).astype(F32) * frequency[None, :]
    cosine, sine = jnp.cos(angle), jnp.sin(angle)
    tab = jnp.concatenate([cosine, cosine, -sine, sine], axis=1)
    source = inputs.reshape(256, 1024)
    upstream = cotangent.reshape(256, 1024)
    (
        whole, normed, lin_query, lin_key, keys, values, queries, probs, mixed, middle, gain, grad_gu, grad_down,
        out_part, grad_ffn,
    ) = forward(
        w_query, key_weight, value_weight, w_out, w_gate, w_up, w_down, source, upstream, tab, starts[:, 0], params
    )
    done = backward(
        whole, normed, lin_query, lin_key, keys, values, queries, probs, mixed, middle, gain, out_part, grad_ffn,
        upstream, source, tab, grad_gu, grad_down,
    )
    outputs, grad_inputs, d_query, d_key, d_value, d_out, d_gate, d_up, d_down, d_gains = finish(*done)
    both = dp % 4 * 32
    return (
        outputs.reshape(2, 1, 128, 1024),
        grad_inputs.reshape(2, 1, 128, 1024),
        d_query,
        d_key,
        d_value,
        d_out,
        d_gate,
        d_up,
        d_down,
        lax.dynamic_slice(d_gains, (8, both), (1, 32))[0],
        lax.dynamic_slice(d_gains, (16, both), (1, 32))[0],
        lax.dynamic_slice(d_gains, (0, 2 * dp), (1, 2))[0],
        lax.dynamic_slice(d_gains, (0, 64 + 2 * dp), (1, 2))[0],
    )


def solution(mesh):
    tokens, matrix, vector = P(None, "dp", "seq", None), P("dp", None), P("dp")
    return jax.shard_map(
        body,
        mesh=mesh,
        in_specs=(tokens, P(None, "dp", "seq")) + (matrix,) * 7 + (vector,) * 4 + (tokens,),
        out_specs=(tokens, tokens) + (matrix,) * 7 + (vector,) * 4,
        check_vma=False,
    )
```

```python
from functools import partial

import jax
import jax.numpy as jnp
from jax import lax
from jax.experimental import pallas as pl
from jax.experimental.pallas import tpu as pltpu
from jax.sharding import PartitionSpec as P

QUERY_HEADS = 16
KEY_VALUE_HEADS = 8
HEAD_SIZE = 64
EPS = 1e-05
ROPE_BASE = 1000000.0

MESH = pl.DeviceIdType.MESH
BF = jnp.bfloat16
F32 = jnp.float32
WA = 3200
GU = 2304
DN = 144


class Links:
    def __init__(self, send, recv, local):
        dp = lax.axis_index("dp")
        self.z = lax.axis_index("seq")
        self.x, self.y, self.c = dp // 8, (dp // 2) % 4, dp % 2
        self.send, self.recv, self.local = send, recv, local
        self.n = self.m = 0
        self.out = []
        self.other = 1 - self.c
        place = {"x": self.x, "y": self.y, "z": self.z}
        self.ring = {k: ((v + 3) % 4, (v + 1) % 4, (v + 2) % 4) for k, v in place.items()}
        self.past_x = (self.x - self.z + 4) % 4
        self.past_z = (self.z - self.x + 4) % 4
        self.near = {("c", 1): self.dev(self.x, self.y, self.other, self.z)}
        for k, (before, after, far) in self.ring.items():
            for step, v in ((-1, before), (1, after)):
                spot = dict(place, **{k: v})
                self.near[k, step] = self.dev(spot["x"], spot["y"], self.c, spot["z"])

    def dev(self, x, y, c, z):
        return ((x * 4 + y) * 2 + c, z)

    def nbr(self, axis, step):
        return self.near[axis, step]

    def sides(self, axis):
        return self.nbr(axis, 1), self.nbr(axis, -1)

    def barrier(self, axes):
        sem = pltpu.get_barrier_semaphore()
        count = 0
        for axis in axes:
            for step in (1,) if axis == "c" else (1, -1):
                pl.semaphore_signal(sem, inc=1, device_id=self.nbr(axis, step), device_id_type=MESH)
                count += 1
        pl.semaphore_wait(sem, count)

    def make(self, src, dst, to):
        copy = pltpu.make_async_remote_copy(
            src_ref=src,
            dst_ref=dst,
            send_sem=self.send.at[self.n],
            recv_sem=self.recv.at[self.n],
            device_id=to,
            device_id_type=MESH,
        )
        self.n += 1
        assert self.n <= self.send.shape[0]
        return copy

    def put(self, src, dst, to):
        copy = self.make(src, dst, to)
        copy.start()
        self.out.append(copy)
        return copy

    def keep(self, src, dst):
        copy = pltpu.make_async_copy(src, dst, self.local.at[self.m])
        self.m += 1
        assert self.m <= self.local.shape[0]
        copy.start()
        return copy

    def flush(self):
        for copy in self.out:
            copy.wait_send()
        self.out = []


def drive(*steps):
    steps = list(steps)
    while steps:
        steps = [s for s in steps if next(s, "end") != "end"]


def ring_gather(lk, own, slot, part, axis, me, ready=None):
    right, left = lk.sides(axis)
    before, after, far = lk.ring[axis]
    a = lk.put(own, slot(me), right)
    b = lk.put(own, slot(me), left)
    yield 1
    a.wait_recv()
    c = lk.put(part(before, 0), part(before, 0), right)
    if ready:
        ready(before)
    b.wait_recv()
    d = lk.put(part(after, 1), part(after, 1), left)
    if ready:
        ready(after)
    yield 1
    c.wait_recv()
    d.wait_recv()
    if ready:
        ready(far)


def plane_gather(lk, own, out, first, lo, hi):
    cols = pl.ds(lo, hi - lo)
    x, y, c = lk.x, lk.y, lk.c
    kept = lk.keep(own.at[:, cols], out.at[x, y, c, :, cols])
    crossing = []

    def cross(ref):
        crossing.append(lk.put(ref, ref, lk.nbr("c", 1)))

    def rows(k):
        return pl.ds(16 * k, 16)

    def two(k):
        return pl.ds(2 * k, 2)

    if first == "x":
        yield from ring_gather(
            lk, own.at[:, cols], lambda i: out.at[i, y, c, :, cols],
            lambda i, k: out.at[i, y, c, rows(k), cols], "x", x,
        )
        kept.wait()
        whole = out.at[:, y, c, :, cols]
        cross(whole)
        yield from ring_gather(
            lk, whole, lambda j: out.at[:, j, c, :, cols],
            lambda j, k: out.at[two(k), j, c, :, cols], "y", y,
            lambda j: cross(out.at[:, j, c, :, cols]),
        )
    else:
        yield from ring_gather(
            lk, own.at[:, cols], lambda j: out.at[x, j, c, :, cols],
            lambda j, k: out.at[x, j, c, rows(k), cols], "y", y,
        )
        kept.wait()
        whole = out.at[x, :, c, :, cols]
        cross(whole)
        yield from ring_gather(
            lk, whole, lambda i: out.at[i, :, c, :, cols],
            lambda i, k: out.at[i, two(k), c, :, cols], "x", x,
            lambda i: cross(out.at[i, :, c, :, cols]),
        )
    yield 1
    for copy in crossing:
        copy.wait_recv()


def ring_spread(lk, own, dst, part, axis, place):
    right, left = lk.sides(axis)
    a, b = lk.make(own, dst, right), lk.make(own, dst, left)
    c, d = lk.make(part(0), part(0), right), lk.make(part(1), part(1), left)
    kept = pltpu.make_async_copy(own, dst, lk.local.at[lk.m])
    lk.m += 1

    @pl.when(place == 0)
    def _():
        a.start()
        b.start()
        kept.start()

    yield 1

    @pl.when(place == 1)
    def _():
        a.wait_recv()
        c.start()

    @pl.when(place == 3)
    def _():
        b.wait_recv()
        d.start()

    yield 1

    @pl.when(place == 2)
    def _():
        c.wait_recv()
        d.wait_recv()

    @pl.when(place == 0)
    def _():
        kept.wait()
        a.wait_send()
        b.wait_send()

    @pl.when(place == 1)
    def _():
        c.wait_send()

    @pl.when(place == 3)
    def _():
        d.wait_send()


def down_part(k):
    return pl.ds(0, 80) if k == 0 else pl.ds(80, 64)


def down_gather(lk, own, out):
    y, c = lk.y, lk.c
    yield from ring_spread(
        lk, own, out.at[y, c], lambda k: out.at[y, c, down_part(k)], "x", lk.past_x
    )
    crossing = []

    def cross(j):
        crossing.append(lk.put(out.at[j, c], out.at[j, c], lk.nbr("c", 1)))

    cross(y)
    yield from ring_gather(
        lk, out.at[y, c], lambda j: out.at[j, c], lambda j, k: out.at[j, c, down_part(k)], "y", y, cross
    )
    yield 1
    for copy in crossing:
        copy.wait_recv()


def line_gather(lk, own, out, cut):
    z, rows = lk.z, own.shape[0]
    kept = lk.keep(own, out.at[z])

    def part(i, k):
        return out.at[i, pl.ds(0, cut)] if k == 0 else out.at[i, pl.ds(cut, rows - cut)]

    rest = ring_gather(lk, own, lambda i: out.at[i], part, "z", z)
    yield next(rest)
    kept.wait()
    yield from rest


def add_into(dst, src):
    if len(dst.shape) == 2:
        dst[...] = (dst[...].astype(F32) + src[...].astype(F32)).astype(BF)
    else:
        for i in range(dst.shape[0]):
            dst[i] = (dst[i].astype(F32) + src[i].astype(F32)).astype(BF)


def ring_reduce(lk, p, part, bufs, axis, me):
    right, left = lk.sides(axis)
    r0, r1, ra, rb = bufs
    before, after, far = lk.ring[axis]
    a = lk.put(part(far, 0), r0, right)
    b = lk.put(part(far, 1), r1, left)
    yield 1
    a.wait_recv()
    add_into(part(after, 0), r0)
    c = lk.put(p(after), ra, right)
    b.wait_recv()
    add_into(part(before, 1), r1)
    d = lk.put(p(before), rb, left)
    yield 1
    c.wait_recv()
    add_into(p(me), ra)
    d.wait_recv()
    add_into(p(me), rb)


def plane_reduce(lk, spot, sib_src, sib, bufs, out, first, kept=None):
    x, y, c = lk.x, lk.y, lk.c
    one, two = bufs
    got = lk.put(sib_src, sib, lk.nbr("c", 1))
    yield 1
    if kept is not None:
        kept.wait()
    got.wait_recv()

    def step(i, _):
        ref = spot(i // 4, i % 4)
        ref[...] = (ref[...].astype(F32) + sib[i // 4, i % 4].astype(F32)).astype(BF)
        return 0

    lax.fori_loop(0, 16, step, 0)
    every = slice(None)

    def pair(k):
        return pl.ds(2 * k, 2)

    def rows(ref, k):
        return ref.at[pl.ds(16 * k, 16)]

    if first == "y":
        yield from ring_reduce(lk, lambda j: spot(every, j), lambda j, k: spot(pair(k), j), one, "y", y)
        yield from ring_reduce(lk, lambda i: spot(i, y), lambda i, k: rows(spot(i, y), k), two, "x", x)
    else:
        yield from ring_reduce(lk, lambda i: spot(i, every), lambda i, k: spot(i, pair(k)), one, "x", x)
        yield from ring_reduce(lk, lambda j: spot(x, j), lambda j, k: rows(spot(x, j), k), two, "y", y)
    yield 1
    yield from line_gather(lk, spot(x, y), out, 16)


def ring_scratch(cols):
    return [
        pltpu.VMEM((4, 4, 32, cols), BF),
        pltpu.VMEM((2, 32, cols), BF),
        pltpu.VMEM((2, 32, cols), BF),
        pltpu.VMEM((4, 32, cols), BF),
        pltpu.VMEM((4, 32, cols), BF),
        pltpu.VMEM((16, cols), BF),
        pltpu.VMEM((16, cols), BF),
        pltpu.VMEM((32, cols), BF),
        pltpu.VMEM((32, cols), BF),
    ]


def down_scratch():
    return [
        pltpu.VMEM((4, DN, 1024), BF),
        pltpu.VMEM((4, DN, 1024), BF),
        pltpu.VMEM((80, 1024), BF),
        pltpu.VMEM((64, 1024), BF),
        pltpu.VMEM((DN, 1024), BF),
        pltpu.VMEM((DN, 1024), BF),
        pltpu.VMEM((80, 1024), BF),
        pltpu.VMEM((64, 1024), BF),
        pltpu.VMEM((DN, 1024), BF),
        pltpu.VMEM((DN, 1024), BF),
    ]


def down_reduce(lk, part_hbm, s, out):
    acc, sib, one, (x0, x1, xa, xb) = s[0], s[1], s[2:6], s[6:10]
    y, c = lk.y, lk.c
    kept = lk.keep(part_hbm.at[:, c], acc)
    got = lk.put(part_hbm.at[:, 1 - c], sib, lk.nbr("c", 1))
    yield 1
    kept.wait()
    got.wait_recv()
    add_into(acc, sib)
    yield from ring_reduce(
        lk, lambda j: acc.at[j], lambda j, k: acc.at[j, down_part(k)], one, "y", y
    )
    mine = acc.at[y]
    right, left = lk.sides("x")
    place = lk.past_x
    a = lk.make(acc.at[y, down_part(0)], x0, left)
    b = lk.make(acc.at[y, down_part(1)], x1, right)
    e = lk.make(mine, xa, left)
    f = lk.make(mine, xb, right)

    @pl.when(place == 2)
    def _():
        a.start()
        b.start()

    yield 1

    @pl.when(place == 1)
    def _():
        a.wait_recv()
        add_into(acc.at[y, down_part(0)], x0)
        e.start()

    @pl.when(place == 3)
    def _():
        b.wait_recv()
        add_into(acc.at[y, down_part(1)], x1)
        f.start()

    yield 1

    @pl.when(place == 0)
    def _():
        e.wait_recv()
        add_into(mine, xa)
        f.wait_recv()
        add_into(mine, xb)

    @pl.when(place == 1)
    def _():
        e.wait_send()

    @pl.when(place == 3)
    def _():
        f.wait_send()

    @pl.when(place == 2)
    def _():
        a.wait_send()
        b.wait_send()

    yield from ring_spread(
        lk, mine, out, lambda k: out.at[down_part(k)], "z", lk.past_z
    )


ANY = pl.BlockSpec(memory_space=pl.ANY)


def sems(n):
    return [pltpu.SemaphoreType.DMA((n,)), pltpu.SemaphoreType.DMA((n,)), pltpu.SemaphoreType.DMA((40,))]


def params(number):
    return pltpu.CompilerParams(collective_id=number, has_side_effects=True, vmem_limit_bytes=56 * 2**20)


def shape(*dims, dtype=BF):
    return jax.ShapeDtypeStruct(dims, dtype)


def lanes_of(shape):
    return lax.broadcasted_iota(jnp.int32, shape, len(shape) - 1)


def dot(left, right, dims=((1,), (0,)), kind=F32):
    return lax.dot_general(left, right, (dims, ((), ())), preferred_element_type=F32).astype(kind)


TOKENS = ((0,), (0,))
ROWS = ((1,), (1,))


def flat(value):
    return value.reshape(-1, value.shape[-1])


def head_ones():
    row = lax.broadcasted_iota(jnp.int32, (256, 256), 0) // 64
    col = lax.broadcasted_iota(jnp.int32, (256, 256), 1) // 64
    return jnp.where(row == col, 1.0 / 64, 0.0).astype(BF)


def head_mean(v, ones):
    high = v.astype(BF)
    low = (v - high.astype(F32)).astype(BF)
    return dot(high, ones) + dot(low, ones)


def halves_swapped(v):
    lane = lanes_of(v.shape)
    return jnp.where(lane % 64 < 32, pltpu.roll(v, 96, 1), pltpu.roll(v, 32, 1))


def angle_tables(tab):
    lane = lanes_of(tab.shape)
    other = pltpu.roll(tab, 64, 1)
    return jnp.where(lane < 64, tab, other), jnp.where(lane < 64, other, tab)


def row_scale(v):
    return lax.rsqrt(jnp.mean(v * v, axis=-1, keepdims=True) + EPS)


def gain_rows(whole, gain):
    def step(i, total):
        return total + whole[i // 8, (i // 2) % 4, i % 2, :, pl.ds(2048, 128)].astype(F32)

    total = lax.fori_loop(0, 32, step, jnp.zeros((32, 128), F32))
    for k in range(8):
        gain[0:1, pl.ds(128 * k, 128)] = total[8 + k : 9 + k]
        gain[1:2, pl.ds(128 * k, 128)] = total[16 + k : 17 + k]
        gain[2:3, pl.ds(128 * k, 128)] = total[0:1]
        gain[3:4, pl.ds(128 * k, 128)] = total[1:2]


def keys_values(q, whole, sources, gain, normed, keys, values, lin_key):
    ones = head_ones()
    src = sources[q, :, 0:1024].astype(F32)
    normed[q] = (src * row_scale(src) * gain[0:1]).astype(BF)
    cosine, sine = angle_tables(sources[q, :, 1024:1152].astype(F32))
    kn = gain[3:4, 0:128]
    lane = lanes_of((256, 128))
    here = pl.ds(pl.multiple_of(q * 128, 128), 128)

    def put(ref, tile, r):
        turned = pltpu.roll(r, 64, 1)
        even = jnp.where(lane < 64, r, turned).astype(BF)
        odd = jnp.where(lane < 64, turned, r).astype(BF)
        for m in range(2):
            ref[m, 2 * tile, here] = even[128 * m : 128 * m + 128]
            ref[m, 2 * tile + 1, here] = odd[128 * m : 128 * m + 128]

    for j in range(4):
        lin = dot(normed[q], flat(whole[:, :, :, :, pl.ds(1024 + 256 * j, 256)]))
        if j < 2:
            scale = lax.rsqrt(head_mean(lin * lin, ones) + EPS)
            if lin_key is not None:
                lin_key[:, pl.ds(256 * j, 256)] = lin
            for h in range(2):
                cut = slice(128 * h, 128 * h + 128)
                v = lin[:, cut] * scale[:, cut] * kn
                put(keys, 2 * j + h, v * cosine + halves_swapped(v) * sine)
        else:
            for h in range(2):
                put(values, 2 * (j - 2) + h, lin[:, 128 * h : 128 * h + 128])


def own_queries(whole, table, gain, normed, lin_query, queries, own):
    ones = head_ones()
    cosine, sine = angle_tables(table[...])
    qn = gain[2:3, 0:128]
    lane = lanes_of((256, 128))

    def step(j, _):
        lin = dot(normed[own], flat(whole[:, :, :, :, pl.ds(pl.multiple_of(256 * j, 256), 256)]))
        lin_query[:, pl.ds(pl.multiple_of(256 * j, 256), 256)] = lin
        scale = lax.rsqrt(head_mean(lin * lin, ones) + EPS)
        for h in range(2):
            cut = slice(128 * h, 128 * h + 128)
            v = lin[:, cut] * scale[:, cut] * qn
            r = (v * cosine + halves_swapped(v) * sine) * HEAD_SIZE ** (-0.5)
            first = jnp.where(lane < 64, r, 0.0).astype(BF)
            second = jnp.where(lane < 64, 0.0, r).astype(BF)
            for m in range(2):
                queries[m, 2 * j + h, 0:128] = first[128 * m : 128 * m + 128]
                queries[m, 2 * j + h, 128:256] = second[128 * m : 128 * m + 128]
        return 0

    lax.fori_loop(0, 4, step, 0)


def attend(m, queries, keys, values, starts, mask, probs, mixed, own):
    key_pos = lax.broadcasted_iota(jnp.int32, (512, 256), 0)
    query_pos = own * 128 + lax.broadcasted_iota(jnp.int32, (1, 256), 1) % 128
    lane = lanes_of((128, 128))
    row = starts[m : m + 1]
    begin = jnp.concatenate([row, row], axis=1)
    mask[...] = jnp.where((key_pos <= query_pos) & (key_pos >= begin), 1.0, 0.0)

    def step(k, _):
        scores = dot(keys[m, k], queries[m, k], ROWS)
        raised = jnp.exp(scores) * mask[...]
        chance = (raised * (1.0 / jnp.sum(raised, axis=0, keepdims=True))).astype(BF)
        probs[8 * m + k] = chance
        got = dot(values[m, k], chance, TOKENS).T
        both = jnp.where(lane < 64, got[0:128], got[128:256]).astype(BF)
        mixed[128 * m : 128 * m + 128, pl.ds(pl.multiple_of(k * 128, 128), 128)] = both
        return 0

    lax.fori_loop(0, 8, step, 0, unroll=UNROLL)


UNROLL = 4


def out_project(m, whole, sources, gain, mixed, middle, normed_ffn, own):
    rows = pl.ds(128 * m, 128)

    def step(j, _):
        cut = pl.ds(pl.multiple_of(256 * j, 256), 256)
        w = flat(whole[:, :, :, :, pl.ds(pl.multiple_of(2176 + 256 * j, 128), 256)])
        middle[rows, cut] = sources[own, rows, cut].astype(F32) + dot(mixed[rows], w)
        return 0

    lax.fori_loop(0, 4, step, 0)
    mid = middle[rows]
    normed_ffn[own, rows] = (mid * row_scale(mid) * gain[1:2]).astype(BF)


def own_gains(params, dp):
    row = jnp.broadcast_to(params, (32, 128))
    line = lax.broadcasted_iota(jnp.int32, (32, 128), 0)
    lane = lanes_of((32, 128))
    spot = dp % 4 * 32
    window = (lane >= spot) & (lane < spot + 32)
    got = jnp.where((line == 8 + dp // 4) & window, pltpu.roll(row, spot, 1), 0.0)
    got = got + jnp.where((line == 16 + dp // 4) & window, pltpu.roll(row, (spot + 96) % 128, 1), 0.0)
    pair = (lane % 64 >= 2 * dp) & (lane % 64 < 2 * dp + 2)
    for k in range(2):
        low = pltpu.roll(row, (2 * dp + 64 - 2 * k) % 128, 1)
        high = pltpu.roll(row, (2 * dp + 128 - 2 * k) % 128, 1)
        got = got + jnp.where((line == k) & pair, jnp.where(lane < 64, low, high), 0.0)
    return got.astype(BF)


def feed_back_in(slots, cots, down, grad_hidden):
    tokens = jnp.concatenate([cots[i] for i in slots], axis=0) if len(slots) > 1 else cots[slots[0]]
    got = dot(tokens, flat(down[...]), ROWS, BF)
    for n, i in enumerate(slots):
        grad_hidden[i] = got[256 * n : 256 * n + 256]


def feed_chunk(slots, ffn, gate_up, down, grad_hidden, hidden, turned, ffn_turned, grad_both, grad_ffn, out_part):
    def load(ref, *cut):
        return jnp.concatenate([ref[(i, *cut)] for i in slots], axis=0) if len(slots) > 1 else ref[(slots[0], *cut)]

    def store(ref, value, *cut):
        for n, i in enumerate(slots):
            ref[(i, *cut)] = value[256 * n : 256 * n + 256]

    every = slice(None)
    size = 256 * len(slots)

    def step(j, _):
        cut = pl.ds(pl.multiple_of(384 * j, 128), 384)
        cut_up = pl.ds(pl.multiple_of(1152 + 384 * j, 128), 384)
        tokens = load(ffn, every, every)
        gated = dot(tokens, flat(gate_up[:, :, :, :, cut]))
        upward = dot(tokens, flat(gate_up[:, :, :, :, cut_up]))
        sigma = 1.0 / (1.0 + jnp.exp(-gated))
        silu = gated * sigma
        made = (silu * upward).astype(BF)
        hidden[0:size, cut] = made
        for n, i in enumerate(slots):
            turned[cut, pl.ds(pl.multiple_of(256 * i, 256), 256)] = made[256 * n : 256 * n + 256].T
        back = load(grad_hidden, every, cut).astype(F32)
        store(grad_both, (back * upward * sigma * (1.0 + gated * (1.0 - sigma))).astype(BF), every, cut)
        store(grad_both, (back * silu).astype(BF), every, cut_up)
        return 0

    lax.fori_loop(0, 3, step, 0)

    def last(j, _):
        cut = pl.ds(pl.multiple_of(256 * j, 256), 256)
        store(grad_ffn, dot(load(grad_both, every, every), flat(gate_up[j]), ROWS, BF), every, cut)
        store(out_part, dot(hidden[0:size], flat(down[:, :, :, cut]), kind=BF), every, cut)
        for i in slots:
            ffn_turned[cut, pl.ds(pl.multiple_of(256 * i, 256), 256)] = ffn[i, :, cut].T
        return 0

    lax.fori_loop(0, 4, last, 0)


def feed_grads(left, right, out, tiles):
    def step(j, _):
        cut = pl.ds(pl.multiple_of(256 * j, 256), 256)
        got = dot(left[...], flat(right[:, :, cut]), kind=BF)
        lead = out.shape[:-1]
        out[(slice(None),) * len(lead) + (cut,)] = got.reshape(*lead, 256)
        return 0

    lax.fori_loop(0, tiles, step, 0)


FWD_SCRATCH = [
    pltpu.VMEM((4, 4, 2, 32, WA), BF),
    pltpu.VMEM((4, 4, 2, 32, GU), BF),
    pltpu.VMEM((4, 2, DN, 1024), BF),
    pltpu.VMEM((4, 256, 1152), BF),
    pltpu.VMEM((256, 128), F32),
    pltpu.VMEM((256, 1152), BF),
    pltpu.VMEM((4, 256, 1024), BF),
    pltpu.VMEM((4, 256, 1024), BF),
    pltpu.VMEM((4, 256, 1024), BF),
    pltpu.VMEM((256, 1024), F32),
    pltpu.VMEM((256, 512), F32),
    pltpu.VMEM((2, 8, 512, 128), BF),
    pltpu.VMEM((2, 8, 512, 128), BF),
    pltpu.VMEM((2, 8, 256, 128), BF),
    pltpu.VMEM((16, 512, 256), BF),
    pltpu.VMEM((256, 1024), BF),
    pltpu.VMEM((256, 1024), F32),
    pltpu.VMEM((8, 1024), F32),
    pltpu.VMEM((4, 256, 1152), BF),
    pltpu.VMEM((512, 1152), BF),
    pltpu.VMEM((1152, 1024), BF),
    pltpu.VMEM((1024, 1024), BF),
    pltpu.VMEM((4, 256, GU), BF),
    pltpu.VMEM((4, 256, 1024), BF),
    pltpu.VMEM((4, 256, 1024), BF),
    pltpu.VMEM((256, 1024), BF),
    pltpu.VMEM((256, 1024), BF),
    pltpu.VMEM((4, 64, 1024), BF),
    pltpu.VMEM((2, 128), jnp.int32),
    pltpu.VMEM((32, WA), BF),
    pltpu.VMEM((32, GU), BF),
    pltpu.VMEM((1, 128), F32),
    pltpu.VMEM((512, 256), F32),
]

FWD_OUT = (
    shape(4, 4, 2, 32, WA),
    shape(256, 1024),
    shape(256, 1024, dtype=F32),
    shape(256, 512, dtype=F32),
    shape(2, 8, 512, 128),
    shape(2, 8, 512, 128),
    shape(2, 8, 256, 128),
    shape(16, 512, 256),
    shape(256, 1024),
    shape(256, 1024, dtype=F32),
    shape(8, 1024, dtype=F32),
    shape(4, 4, 2, 32, GU),
    shape(4, 2, DN, 1024),
    shape(4, 256, 1024),
    shape(256, 1024, dtype=F32),
)


FWD_IN = 12


def go(*steps):
    for s in steps:
        next(s, None)


def fwd_kernel(*refs):
    w_query, key_weight, value_weight, w_out, w_gate, w_up, dn, x, cot, tab, starts_hbm, params_hbm = refs[:FWD_IN]
    refs = refs[FWD_IN:]
    outs, refs = refs[: len(FWD_OUT)], refs[len(FWD_OUT) :]
    lk = Links(*refs[:3])
    (
        whole, gate_up, down, sources, table, source, cots, ffn, normed, lin_query, lin_key, keys, values, queries,
        probs, mixed, middle, gain, grad_hidden, hidden, turned, ffn_turned, grad_both, grad_ffn, out_part,
        from_right, from_left, passing, starts, wa, gu, own_params, mask,
    ) = refs[3:]
    own = lk.z
    before, after, far = lk.ring["z"]
    quarter = pl.ds(pl.multiple_of(own * 1152, 128), 1152)
    staged = [
        lk.keep(params_hbm, own_params),
        lk.keep(tab, table),
        lk.keep(x, source.at[:, pl.ds(0, 1024)]),
        lk.keep(starts_hbm, starts),
        lk.keep(w_query, wa.at[:, pl.ds(0, 1024)]),
        lk.keep(key_weight, wa.at[:, pl.ds(1024, 512)]),
        lk.keep(value_weight, wa.at[:, pl.ds(1536, 512)]),
        lk.keep(w_out, wa.at[:, pl.ds(2176, 1024)]),
        lk.keep(w_gate.at[:, quarter], gu.at[:, pl.ds(0, 1152)]),
        lk.keep(w_up.at[:, quarter], gu.at[:, pl.ds(1152, 1152)]),
    ]
    staged[0].wait()
    staged[1].wait()
    source[:, 1024:1152] = table[...].astype(BF)
    wa[:, 2048:2176] = own_gains(own_params[...], lax.axis_index("dp"))
    for copy in staged[2:]:
        copy.wait()
    lk.barrier("xyzc")
    k1 = plane_gather(lk, wa, whole, "x", 1024, 1536)
    k2 = plane_gather(lk, wa, whole, "y", 1536, 2176)
    a1 = plane_gather(lk, wa, whole, "x", 0, 1024)
    a2 = plane_gather(lk, wa, whole, "y", 2176, WA)
    x1 = line_gather(lk, source, sources, 128)
    g1 = plane_gather(lk, gu, gate_up, "x", 0, 1152)
    g2 = plane_gather(lk, gu, gate_up, "y", 1152, GU)
    d1 = down_gather(lk, dn, down)
    c1 = line_gather(lk, cot, cots, 128)
    go(k1, k2, x1)
    go(a1, a2)
    go(k1, k2)
    go(a1, a2)
    go(k1, k2)
    go(a1, a2)
    go(k1, k2)
    go(g1, g2)
    go(k1, k2)
    go(a1, a2)
    go(x1)
    go(d1)
    drive(k1, k2)
    gain_rows(whole, gain)
    keys_values(own, whole, sources, gain, normed, keys, values, lin_key)

    def sides(i, _):
        keys_values((own + 3 + 2 * i) % 4, whole, sources, gain, normed, keys, values, None)
        return 0

    lax.fori_loop(0, 2, sides, 0)
    go(a1, a2)
    go(g1, g2)
    drive(x1)
    go(c1)
    keys_values(far, whole, sources, gain, normed, keys, values, None)
    go(g1, g2)
    drive(a1, a2)
    own_queries(whole, table, gain, normed, lin_query, queries, own)
    go(d1)
    saved = []
    for k, ref in enumerate((normed.at[own], lin_query, lin_key, keys, values, queries)):
        saved.append(lk.keep(ref, outs[1 + k]))
    passed = []
    for m in range(2):
        attend(m, queries, keys, values, starts, mask, probs, mixed, own)
        if m == 0:
            saved.append(lk.keep(whole, outs[0]))
        out_project(m, whole, sources, gain, mixed, middle, ffn, own)
        rows = pl.ds(128 * m, 128)

        def part(i, k, m=m):
            return ffn.at[i, pl.ds(128 * m + 64 * k, 64)]

        passed.append(
            ring_gather(lk, ffn.at[own, rows], lambda i, rows=rows: ffn.at[i, rows], part, "z", own)
        )
        go(passed[m])
        if m == 0:
            go(g1, g2)
            go(d1)
            go(c1)
    go(passed[0])
    go(d1)
    go(g1, g2)
    for k, ref in enumerate((probs, mixed, middle, gain)):
        saved.append(lk.keep(ref, outs[7 + k]))
    drive(g1, g2, d1)
    feed_back_in((own,), cots, down, grad_hidden)
    go(passed[1])

    def chunk(*slots):
        feed_chunk(
            slots, ffn, gate_up, down, grad_hidden, hidden, turned, ffn_turned, grad_both, grad_ffn, out_part
        )

    right, left = lk.sides("z")
    chunk(own)
    go(c1)
    lk.flush()
    feed_back_in((before, after), cots, down, grad_hidden)
    chunk(before, after)
    low, high = pl.ds(0, 128), pl.ds(128, 128)
    sent = [
        lk.put(grad_ffn.at[after, high], from_left.at[high], right),
        lk.put(grad_ffn.at[before, low], from_right.at[low], left),
    ]
    drive(c1)
    feed_back_in((far,), cots, down, grad_hidden)
    drive(*passed)
    chunk(far)
    saved.append(lk.keep(out_part, outs[13]))
    hops = []
    for k in range(2):
        rows = pl.ds(64 * k, 64)
        hops.append((lk.put(grad_ffn.at[far, rows], passing.at[k], right), after, rows, from_left, right))
    for k in range(2):
        rows = pl.ds(128 + 64 * k, 64)
        hops.append((lk.put(grad_ffn.at[far, rows], passing.at[2 + k], left), before, rows, from_right, left))

    def hop(k):
        copy, slot, rows, landing, to = hops[k]
        copy.wait_recv()
        add_into(grad_ffn.at[slot, rows], passing.at[k])
        sent.append(lk.put(grad_ffn.at[slot, rows], landing.at[rows], to))

    feed_grads(turned, cots, down, 4)
    saved.append(lk.keep(down, outs[12]))
    hop(0)
    hop(2)
    feed_grads(ffn_turned, grad_both, gate_up, 9)
    hop(1)
    hop(3)
    saved.append(lk.keep(gate_up, outs[11]))
    for copy in sent:
        copy.wait_recv()
    for copy in saved:
        copy.wait()
    total = grad_ffn[own].astype(F32) + from_right[...].astype(F32) + from_left[...].astype(F32)
    lin_query[...] = total
    lk.keep(lin_query, outs[14]).wait()
    lk.flush()


def forward(*args):
    return pl.pallas_call(
        fwd_kernel,
        out_shape=FWD_OUT,
        in_specs=[ANY] * FWD_IN,
        out_specs=[ANY] * len(FWD_OUT),
        scratch_shapes=sems(128) + FWD_SCRATCH,
        compiler_params=pltpu.CompilerParams(
            collective_id=0, has_side_effects=True, vmem_limit_bytes=60 * 2**20
        ),
    )(*args)


BWD_IN = 18
PIECES = (1152, 1152, 512, 512, 512, 512, 512, 512, 128)
BWD_OUT = (
    shape(256, 1024),
    shape(256, 1024, dtype=F32),
    shape(4, 32, WA),
    shape(4, 32, GU),
    shape(DN, 1024),
)
BWD_SCRATCH = [
    pltpu.VMEM((4, 4, 2, 32, WA), BF),
    pltpu.VMEM((256, 1024), BF),
    pltpu.VMEM((256, 1024), F32),
    pltpu.VMEM((256, 512), F32),
    pltpu.VMEM((2, 8, 512, 128), BF),
    pltpu.VMEM((2, 8, 512, 128), BF),
    pltpu.VMEM((2, 8, 256, 128), BF),
    pltpu.VMEM((16, 512, 256), BF),
    pltpu.VMEM((256, 1024), BF),
    pltpu.VMEM((256, 1024), F32),
    pltpu.VMEM((8, 1024), F32),
    pltpu.VMEM((4, 256, 1024), BF),
    pltpu.VMEM((256, 1024), F32),
    pltpu.VMEM((256, 1024), BF),
    pltpu.VMEM((256, 1024), BF),
    pltpu.VMEM((256, 128), F32),
]
BWD_WORK = [
    pltpu.VMEM((256, 1024), BF),
    pltpu.VMEM((2, 8, 256, 128), BF),
    pltpu.VMEM((256, 1024), F32),
    pltpu.VMEM((4, 256, 1024), BF),
    pltpu.VMEM((256, 2048), BF),
    pltpu.VMEM((1024, 256), BF),
    pltpu.VMEM((256, 1024), F32),
    pltpu.VMEM((8, 1024), F32),
    pltpu.VMEM((4, 4, 2, 32, WA), BF),
    pltpu.VMEM((4, 4, 32, 1152), BF),
    pltpu.VMEM((4, 4, 32, 1152), BF),
    pltpu.VMEM((256, 1024), BF),
]
Z_RING = [
    pltpu.VMEM((128, 1024), BF),
    pltpu.VMEM((128, 1024), BF),
    pltpu.VMEM((256, 1024), BF),
    pltpu.VMEM((256, 1024), BF),
]
Z_HALF = [
    pltpu.VMEM((64, 1024), BF),
    pltpu.VMEM((64, 1024), BF),
    pltpu.VMEM((128, 1024), BF),
    pltpu.VMEM((128, 1024), BF),
]


def norm_back(v, g, dy):
    r = row_scale(v)
    gdy = g * dy
    back = r * gdy - v * (r * r * r * jnp.mean(v * gdy, axis=-1, keepdims=True))
    return back, jnp.sum(v * r * dy, axis=0, keepdims=True)


def heads_back(lin, grad, gain, cosine, sine, ones):
    parts = []
    for h in range(2):
        part = grad[:, 128 * h : 128 * h + 128]
        parts.append(part * cosine + halves_swapped(part * sine))
    dy = jnp.concatenate(parts, axis=1)
    r = lax.rsqrt(head_mean(lin * lin, ones) + EPS)
    gdy = dy * gain
    back = r * gdy - lin * (r * r * r * head_mean(lin * gdy, ones))
    return back, jnp.sum(lin * r * dy, axis=0, keepdims=True)


def turned_grads(turned, right, out, start, tiles, base=0):
    def step(j, _):
        got = dot(turned[...], right[:, pl.ds(pl.multiple_of(base + 256 * j, 256), 256)], kind=BF)
        out[:, :, :, :, pl.ds(pl.multiple_of(start + 256 * j, 128), 256)] = got.reshape(4, 4, 2, 32, 256)
        return 0

    lax.fori_loop(0, tiles, step, 0)


def attend_back(m, queries, keys, values, probs, grad_mixed, grad_queries, grad_kv):
    lane = lanes_of((128, 128))
    lane_keys = lanes_of((512, 128))

    def step(j, _):
        folded = []
        for e in range(2):
            k = 2 * j + e
            i = m * 8 + k
            chance = probs[i]
            back = dot(values[m, k], grad_mixed[m, k], ROWS)
            p = chance.astype(F32)
            p_back = p * back
            grad_scores = (p_back - p * jnp.sum(p_back, axis=0, keepdims=True)).astype(BF)
            got = dot(keys[m, k], grad_scores, TOKENS).T
            cut = pl.ds(pl.multiple_of(128 * k, 128), 128)
            grad_queries[pl.ds(128 * m, 128), cut] = jnp.where(
                lane < 64, got[0:128], got[128:256]
            )
            for v in (dot(grad_scores, queries[m, k]), dot(chance, grad_mixed[m, k])):
                folded.append(v + pltpu.roll(v, 64, 1))
        for s in range(2):
            tile = jnp.where(lane_keys < 64, folded[s], folded[2 + s]).astype(BF)
            cut = pl.ds(pl.multiple_of(512 * s + 128 * j, 128), 128)
            for q in range(4):
                grad_kv[q, pl.ds(128 * m, 128), cut] = tile[128 * q : 128 * q + 128]

        return 0

    lax.fori_loop(0, 4, step, 0, unroll=2)


def bwd_kernel(*refs):
    ins, refs = refs[:BWD_IN], refs[BWD_IN:]
    outs, refs = refs[: len(BWD_OUT)], refs[len(BWD_OUT) :]
    lk = Links(*refs[:3])
    refs = refs[3:]
    n = len(BWD_SCRATCH)
    held, refs = refs[:n], refs[n:]
    (
        whole, normed, lin_query, lin_key, keys, values, queries, probs, mixed, middle, gain, out_part, grad_middle,
        upstream, source, table,
    ) = held
    grad_gu, grad_down = ins[16:]
    n = len(BWD_WORK)
    work, refs = refs[:n], refs[n:]
    (
        grad_branch, grad_mixed, grad_queries, grad_kv, grad_lin, turned, grad_normed, gains_back, grad_whole, acc_a,
        acc_b, made,
    ) = work
    z_out, z_kv, refs = refs[:4], refs[4:12], refs[12:]
    down_refs, refs = refs[:10], refs[10:]
    rings = [refs[9 * i : 9 * i + 9] for i in range(len(PIECES))]
    outputs, grad_inputs, a_all, gu_all, down_own = outs
    own, c = lk.z, lk.c

    order = [11, 12, 9, 13, 10, 0, 8, 5, 7, 6, 4, 2, 15, 1, 3, 14]
    loads = {}
    for k in order[:7]:
        loads[k] = lk.keep(ins[k], held[k])
    lk.barrier("xyzc")

    def piece(k, spot, src, out, first, kept=None):
        ring = rings[k]
        return plane_reduce(lk, spot, src, ring[0], (ring[1:5], ring[5:9]), out, first, kept)

    def feed_piece(k, acc, lo, first):
        cols = pl.ds(lo, 1152)
        kept = lk.keep(grad_gu.at[:, :, c, :, cols], acc)
        return piece(
            k, lambda i, j: acc.at[i, j], grad_gu.at[:, :, lk.other, :, cols], gu_all.at[:, :, cols], first, kept
        )

    def whole_piece(k, lo, first):
        cols = pl.ds(lo, PIECES[k])
        return piece(
            k, lambda i, j: grad_whole.at[i, j, c, :, cols], grad_whole.at[:, :, lk.other, :, cols],
            a_all.at[:, :, cols], first,
        )

    def out_chain():
        yield from ring_reduce(
            lk, lambda i: out_part.at[i], lambda i, k: out_part.at[i, pl.ds(128 * k, 128)], z_out, "z", own
        )
        made[...] = (middle[...] + out_part[own].astype(F32)).astype(BF)
        done = lk.keep(made, outputs)
        yield 1
        done.wait()

    def need(*names):
        for k in names:
            loads.pop(k).wait()

    f1, f2 = feed_piece(0, acc_a, 0, "y"), feed_piece(1, acc_b, 1152, "x")
    d1 = down_reduce(lk, grad_down, down_refs, down_own)
    go(d1, f1, f2)
    o1 = out_chain()
    need(11)
    go(o1)
    for k in order[7:]:
        loads[k] = lk.keep(ins[k], held[k])
    need(12, 9, 13, 10)
    back, row = norm_back(middle[...], gain[1:2], grad_middle[...])
    total = upstream[...].astype(F32) + back
    grad_middle[...] = total
    grad_branch[...] = total.astype(BF)
    gains_back[1:2] = row
    need(0, 8)
    go(d1)
    lane = lanes_of((256, 128))

    def back_mixed(j, _):
        got = dot(grad_branch[...], flat(whole[j, :, :, :, pl.ds(2176, 1024)]), ROWS)
        for h in range(2):
            r = got[:, 128 * h : 128 * h + 128]
            first = jnp.where(lane < 64, r, 0.0).astype(BF)
            second = jnp.where(lane < 64, 0.0, r).astype(BF)
            for m in range(2):
                grad_mixed[m, 2 * j + h, 0:128] = first[128 * m : 128 * m + 128]
                grad_mixed[m, 2 * j + h, 128:256] = second[128 * m : 128 * m + 128]
        return 0

    lax.fori_loop(0, 4, back_mixed, 0)
    go(f2, f1)
    need(5, 7, 6, 4)
    z_kv_m = []
    for m in range(2):
        attend_back(m, queries, keys, values, probs, grad_mixed, grad_queries, grad_kv)
        rows = pl.ds(128 * m, 128)

        def part(i, k, m=m):
            return grad_kv.at[i, pl.ds(128 * m + 64 * k, 64)]

        z_kv_m.append(
            ring_reduce(lk, lambda i, rows=rows: grad_kv.at[i, rows], part, z_kv[4 * m : 4 * m + 4], "z", own)
        )
        go(z_kv_m[m])
        if m == 0:
            go(d1)
            go(f2, f1)
    go(z_kv_m[0])
    turned[...] = mixed[...].T
    turned_grads(turned, grad_branch, grad_whole, 2176, 4)
    p2, p3 = whole_piece(2, 2176, "y"), whole_piece(3, 2688, "x")
    go(p2, p3)
    go(d1)
    go(f2)
    need(2, 15, 1)
    ones = head_ones()
    cosine, sine = angle_tables(table[...])

    def back_query(j, _):
        cut = pl.ds(pl.multiple_of(256 * j, 256), 256)
        grad = grad_queries[:, cut] * HEAD_SIZE ** (-0.5)
        got, line = heads_back(lin_query[:, cut], grad, gain[2:3, 0:256], cosine, sine, ones)
        grad_lin[:, cut] = got.astype(BF)
        gains_back[2:3, cut] = line
        return 0

    lax.fori_loop(0, 4, back_query, 0)
    go(z_kv_m[1])
    go(d1)
    go(f2)
    turned[...] = normed[...].T
    turned_grads(turned, grad_lin, grad_whole, 0, 4)
    p4, p5 = whole_piece(4, 0, "y"), whole_piece(5, 512, "x")
    go(p4, p5)
    go(p2, p3)
    go(f1)
    go(f2)
    go(p4, p5)
    go(p2, p3)
    go(f1)
    need(3, 14)
    drive(*z_kv_m)
    go(o1)

    def back_key(j, _):
        cut = pl.ds(pl.multiple_of(256 * j, 256), 256)
        grad = grad_kv[own, :, cut].astype(F32)
        got, line = heads_back(lin_key[:, cut], grad, gain[3:4, 0:256], cosine, sine, ones)
        grad_lin[:, pl.ds(pl.multiple_of(1024 + 256 * j, 256), 256)] = got.astype(BF)
        gains_back[3:4, cut] = line
        return 0

    lax.fori_loop(0, 2, back_key, 0)
    grad_lin[:, 1536:2048] = grad_kv[own, :, 512:1024]

    turned_grads(turned, grad_lin, grad_whole, 1024, 4, 1024)
    p6, p7 = whole_piece(6, 1024, "y"), whole_piece(7, 1536, "x")
    go(p6, p7)
    go(d1)
    go(p2, p3)
    go(p4, p5)
    go(f1)

    def back_normed(j, _):
        grad_normed[:, pl.ds(pl.multiple_of(256 * j, 256), 256)] = dot(
            grad_lin[...], flat(whole[j, :, :, :, pl.ds(0, 2048)]), ROWS
        )
        return 0

    lax.fori_loop(0, 4, back_normed, 0)
    go(p6, p7)
    go(p2, p3)
    go(p4, p5)
    go(f2, f1)
    back, row = norm_back(source[...].astype(F32), gain[0:1], grad_normed[...])
    gains_back[0:1] = row
    grad_normed[...] = grad_middle[...] + back
    final = lk.keep(grad_normed, grad_inputs)
    small = [jnp.zeros((1, 128), F32)] * 2
    for s, tiles in ((0, 8), (1, 4)):
        for k in range(tiles):
            small[s] = small[s] + gains_back[2 + s : 3 + s, 128 * k : 128 * k + 128]
        small[s] = small[s] + pltpu.roll(jnp.broadcast_to(small[s], (8, 128)), 64, 1)[0:1]
    heads = jnp.where(lanes_of((1, 128)) < 64, small[0], small[1])
    line = lax.broadcasted_iota(jnp.int32, (32, 128), 0)
    for k in range(8):
        cut = slice(128 * k, 128 * k + 128)
        block = jnp.where(line == 8, gains_back[0:1, cut], 0.0)
        block = jnp.where(line == 16, gains_back[1:2, cut], block)
        block = jnp.where(line == 0, heads, block).astype(BF)
        for d in range(4 * k, 4 * k + 4):
            grad_whole[d // 8, (d // 2) % 4, d % 2, :, 2048:2176] = block
    p8 = whole_piece(8, 2048, "y")
    go(p8)
    go(p6, p7)
    go(p4, p5)
    go(p8)
    go(p2, p3)
    go(d1)
    go(p6, p7)
    go(p8)
    go(p4, p5)
    go(f2, f1)
    go(p6, p7)
    go(p8)
    go(p2, p3)
    go(p6, p7)
    go(p8)
    go(p4, p5)
    go(p6, p7)
    go(p8)
    go(d1)
    drive(p6, p7, p8, p4, p5, p2, p3, f1, f2, o1, d1)
    final.wait()
    lk.flush()


def backward(*args):
    return pl.pallas_call(
        bwd_kernel,
        out_shape=BWD_OUT,
        in_specs=[ANY] * BWD_IN,
        out_specs=[ANY] * len(BWD_OUT),
        scratch_shapes=sems(160) + BWD_SCRATCH + BWD_WORK + Z_RING + Z_HALF * 2 + down_scratch()
        + [v for cols in PIECES for v in ring_scratch(cols)],
        compiler_params=pltpu.CompilerParams(
            collective_id=1, has_side_effects=True, vmem_limit_bytes=62 * 2**20
        ),
    )(*args)


def finish_kernel(*refs):
    ins, outs, held, local = refs[:5], refs[5:15], refs[15:18], refs[18]
    o_out, o_in, o_query, o_key, o_value, o_wout, o_gate, o_up, o_down, o_gains = outs
    a_all, gu_all, down = held
    pairs = [(ins[2], a_all), (ins[3], gu_all), (ins[4], down), (ins[0], o_out), (ins[1], o_in)]
    copies = [pltpu.make_async_copy(src, dst, local.at[k]) for k, (src, dst) in enumerate(pairs)]
    for copy in copies:
        copy.start()
    copies[0].wait()
    for ref, lo, size in (
        (o_query, 0, 1024), (o_key, 1024, 512), (o_value, 1536, 512), (o_gains, 2048, 128), (o_wout, 2176, 1024),
    ):
        total = a_all[0, :, lo : lo + size].astype(F32)
        for i in range(1, 4):
            total = total + a_all[i, :, lo : lo + size].astype(F32)
        ref[...] = total
    copies[1].wait()
    for i in range(4):
        o_gate[:, 1152 * i : 1152 * i + 1152] = gu_all[i, :, 0:1152].astype(F32)
        o_up[:, 1152 * i : 1152 * i + 1152] = gu_all[i, :, 1152:2304].astype(F32)
    copies[2].wait()
    o_down[...] = down[...].astype(F32)
    copies[3].wait()
    copies[4].wait()


def finish(*args):
    vmem = pl.BlockSpec(memory_space=pltpu.VMEM)
    return pl.pallas_call(
        finish_kernel,
        out_shape=(
            shape(256, 1024), shape(256, 1024, dtype=F32), shape(32, 1024, dtype=F32), shape(32, 512, dtype=F32),
            shape(32, 512, dtype=F32), shape(32, 1024, dtype=F32), shape(32, 4608, dtype=F32),
            shape(32, 4608, dtype=F32), shape(DN, 1024, dtype=F32), shape(32, 128, dtype=F32),
        ),
        in_specs=[ANY] * 5,
        out_specs=[ANY, ANY] + [vmem] * 8,
        scratch_shapes=[
            pltpu.VMEM((4, 32, WA), BF), pltpu.VMEM((4, 32, GU), BF), pltpu.VMEM((DN, 1024), BF),
            pltpu.SemaphoreType.DMA((5,)),
        ],
        compiler_params=pltpu.CompilerParams(vmem_limit_bytes=32 * 2**20),
    )(*args)


def body(
    inputs, starts, w_query, key_weight, value_weight, w_out, w_gate, w_up, w_down,
    prenorm, midnorm, querynorm, keynorm, cotangent,
):
    z = lax.axis_index("seq")
    dp = lax.axis_index("dp")
    params = jnp.concatenate([prenorm, midnorm, querynorm, keynorm, jnp.zeros((60,), BF)])
    params = params.astype(F32).reshape(1, 128)
    pos = z * 128 + jnp.arange(128, dtype=jnp.int32)
    inside = pos - starts[:, 0]
    frequency = ROPE_BASE ** (-(jnp.arange(32, dtype=F32) * 2.0 / 64))
    angle = inside.reshape(256, 1).astype(F32) * frequency[None, :]
    cosine, sine = jnp.cos(angle), jnp.sin(angle)
    tab = jnp.concatenate([cosine, cosine, -sine, sine], axis=1)
    source = inputs.reshape(256, 1024)
    upstream = cotangent.reshape(256, 1024)
    (
        whole, normed, lin_query, lin_key, keys, values, queries, probs, mixed, middle, gain, grad_gu, grad_down,
        out_part, grad_ffn,
    ) = forward(
        w_query, key_weight, value_weight, w_out, w_gate, w_up, w_down, source, upstream, tab, starts[:, 0], params
    )
    done = backward(
        whole, normed, lin_query, lin_key, keys, values, queries, probs, mixed, middle, gain, out_part, grad_ffn,
        upstream, source, tab, grad_gu, grad_down,
    )
    outputs, grad_inputs, d_query, d_key, d_value, d_out, d_gate, d_up, d_down, d_gains = finish(*done)
    both = dp % 4 * 32
    return (
        outputs.reshape(2, 1, 128, 1024),
        grad_inputs.reshape(2, 1, 128, 1024),
        d_query,
        d_key,
        d_value,
        d_out,
        d_gate,
        d_up,
        d_down,
        lax.dynamic_slice(d_gains, (8, both), (1, 32))[0],
        lax.dynamic_slice(d_gains, (16, both), (1, 32))[0],
        lax.dynamic_slice(d_gains, (0, 2 * dp), (1, 2))[0],
        lax.dynamic_slice(d_gains, (0, 64 + 2 * dp), (1, 2))[0],
    )


def solution(mesh):
    tokens, matrix, vector = P(None, "dp", "seq", None), P("dp", None), P("dp")
    return jax.shard_map(
        body,
        mesh=mesh,
        in_specs=(tokens, P(None, "dp", "seq")) + (matrix,) * 7 + (vector,) * 4 + (tokens,),
        out_specs=(tokens, tokens) + (matrix,) * 7 + (vector,) * 4,
        check_vma=False,
    )
```

```python
from functools import partial

import jax
import jax.numpy as jnp
from jax import lax
from jax.experimental import pallas as pl
from jax.experimental.pallas import tpu as pltpu
from jax.sharding import PartitionSpec as P

QUERY_HEADS = 16
KEY_VALUE_HEADS = 8
HEAD_SIZE = 64
EPS = 1e-05
ROPE_BASE = 1000000.0

MESH = pl.DeviceIdType.MESH
BF = jnp.bfloat16
F32 = jnp.float32
WA = 3200
GU = 2304
DN = 144


class Links:
    def __init__(self, send, recv, local):
        dp = lax.axis_index("dp")
        self.z = lax.axis_index("seq")
        self.x, self.y, self.c = dp // 8, (dp // 2) % 4, dp % 2
        self.send, self.recv, self.local = send, recv, local
        self.n = self.m = 0
        self.out = []
        self.other = 1 - self.c
        place = {"x": self.x, "y": self.y, "z": self.z}
        self.ring = {k: ((v + 3) % 4, (v + 1) % 4, (v + 2) % 4) for k, v in place.items()}
        self.past_x = (self.x - self.z + 4) % 4
        self.past_z = (self.z - self.x + 4) % 4
        self.near = {("c", 1): self.dev(self.x, self.y, self.other, self.z)}
        for k, (before, after, far) in self.ring.items():
            for step, v in ((-1, before), (1, after)):
                spot = dict(place, **{k: v})
                self.near[k, step] = self.dev(spot["x"], spot["y"], self.c, spot["z"])

    def dev(self, x, y, c, z):
        return ((x * 4 + y) * 2 + c, z)

    def nbr(self, axis, step):
        return self.near[axis, step]

    def sides(self, axis):
        return self.nbr(axis, 1), self.nbr(axis, -1)

    def barrier(self):
        sem = pltpu.get_barrier_semaphore()
        targets = [self.nbr(axis, step) for axis in "xy" for step in (1, -1)]
        for k in range(1, 8):
            spot = (self.z * 2 + self.c + k) % 8
            targets.append(self.dev(self.x, self.y, spot % 2, spot // 2))
        for device in targets:
            pl.semaphore_signal(sem, inc=1, device_id=device, device_id_type=MESH)
        pl.semaphore_wait(sem, len(targets))

    def make(self, src, dst, to):
        copy = pltpu.make_async_remote_copy(
            src_ref=src,
            dst_ref=dst,
            send_sem=self.send.at[self.n],
            recv_sem=self.recv.at[self.n],
            device_id=to,
            device_id_type=MESH,
        )
        self.n += 1
        assert self.n <= self.send.shape[0]
        return copy

    def put(self, src, dst, to):
        copy = self.make(src, dst, to)
        copy.start()
        self.out.append(copy)
        return copy

    def keep(self, src, dst):
        copy = pltpu.make_async_copy(src, dst, self.local.at[self.m])
        self.m += 1
        assert self.m <= self.local.shape[0]
        copy.start()
        return copy

    def flush(self):
        for copy in self.out:
            copy.wait_send()
        self.out = []


def drive(*steps):
    steps = list(steps)
    while steps:
        steps = [s for s in steps if next(s, "end") != "end"]


def ring_gather(lk, own, slot, part, axis, me, ready=None):
    right, left = lk.sides(axis)
    before, after, far = lk.ring[axis]
    a = lk.put(own, slot(me), right)
    b = lk.put(own, slot(me), left)
    yield 1
    a.wait_recv()
    c = lk.put(part(before, 0), part(before, 0), right)
    if ready:
        ready(before)
    b.wait_recv()
    d = lk.put(part(after, 1), part(after, 1), left)
    if ready:
        ready(after)
    yield 1
    c.wait_recv()
    d.wait_recv()
    if ready:
        ready(far)


def plane_gather(lk, own, out, first, lo, hi):
    cols = pl.ds(lo, hi - lo)
    x, y, c = lk.x, lk.y, lk.c
    kept = lk.keep(own.at[:, cols], out.at[x, y, c, :, cols])
    crossing = []

    def cross(ref):
        crossing.append(lk.put(ref, ref, lk.nbr("c", 1)))

    def rows(k):
        return pl.ds(16 * k, 16)

    def two(k):
        return pl.ds(2 * k, 2)

    if first == "x":
        yield from ring_gather(
            lk, own.at[:, cols], lambda i: out.at[i, y, c, :, cols],
            lambda i, k: out.at[i, y, c, rows(k), cols], "x", x,
        )
        kept.wait()
        whole = out.at[:, y, c, :, cols]
        cross(whole)
        yield from ring_gather(
            lk, whole, lambda j: out.at[:, j, c, :, cols],
            lambda j, k: out.at[two(k), j, c, :, cols], "y", y,
            lambda j: cross(out.at[:, j, c, :, cols]),
        )
    else:
        yield from ring_gather(
            lk, own.at[:, cols], lambda j: out.at[x, j, c, :, cols],
            lambda j, k: out.at[x, j, c, rows(k), cols], "y", y,
        )
        kept.wait()
        whole = out.at[x, :, c, :, cols]
        cross(whole)
        yield from ring_gather(
            lk, whole, lambda i: out.at[i, :, c, :, cols],
            lambda i, k: out.at[i, two(k), c, :, cols], "x", x,
            lambda i: cross(out.at[i, :, c, :, cols]),
        )
    yield 1
    for copy in crossing:
        copy.wait_recv()


def ring_spread(lk, own, dst, part, axis, place):
    right, left = lk.sides(axis)
    a, b = lk.make(own, dst, right), lk.make(own, dst, left)
    c, d = lk.make(part(0), part(0), right), lk.make(part(1), part(1), left)
    kept = pltpu.make_async_copy(own, dst, lk.local.at[lk.m])
    lk.m += 1

    @pl.when(place == 0)
    def _():
        a.start()
        b.start()
        kept.start()

    yield 1

    @pl.when(place == 1)
    def _():
        a.wait_recv()
        c.start()

    @pl.when(place == 3)
    def _():
        b.wait_recv()
        d.start()

    yield 1

    @pl.when(place == 2)
    def _():
        c.wait_recv()
        d.wait_recv()

    @pl.when(place == 0)
    def _():
        kept.wait()
        a.wait_send()
        b.wait_send()

    @pl.when(place == 1)
    def _():
        c.wait_send()

    @pl.when(place == 3)
    def _():
        d.wait_send()


def down_part(k):
    return pl.ds(0, 80) if k == 0 else pl.ds(80, 64)


def down_gather(lk, own, out):
    y, c = lk.y, lk.c
    yield from ring_spread(
        lk, own, out.at[y, c], lambda k: out.at[y, c, down_part(k)], "x", lk.past_x
    )
    crossing = []

    def cross(j):
        crossing.append(lk.put(out.at[j, c], out.at[j, c], lk.nbr("c", 1)))

    cross(y)
    yield from ring_gather(
        lk, out.at[y, c], lambda j: out.at[j, c], lambda j, k: out.at[j, c, down_part(k)], "y", y, cross
    )
    yield 1
    for copy in crossing:
        copy.wait_recv()


def line_gather(lk, own, out, cut):
    z, rows = lk.z, own.shape[0]
    kept = lk.keep(own, out.at[z])

    def part(i, k):
        return out.at[i, pl.ds(0, cut)] if k == 0 else out.at[i, pl.ds(cut, rows - cut)]

    rest = ring_gather(lk, own, lambda i: out.at[i], part, "z", z)
    yield next(rest)
    kept.wait()
    yield from rest


def swap_blocks(lk, src, dst, to_row):
    z, c, n = lk.z, lk.c, lk.n
    lk.n += 2
    assert lk.n <= lk.send.shape[0]
    first = lk.m
    lk.m += 2
    copies, keeps, selves = [], [], []
    for k in range(2):
        if to_row:
            slot, core, place = z % 2, z // 2, 2 * k + c
        else:
            slot, core, place = z // 2, z % 2, 2 * c + k
        selves.append((place == z) & (core == c))
        copies.append(
            pltpu.make_async_remote_copy(
                src_ref=src(k),
                dst_ref=dst(slot),
                send_sem=lk.send.at[n + k],
                recv_sem=lk.recv.at[n + slot],
                device_id=lk.dev(lk.x, lk.y, core, place),
                device_id_type=MESH,
            )
        )
        keeps.append(pltpu.make_async_copy(src(k), dst(k), lk.local.at[first + k]))
        pl.when(selves[k])(keeps[k].start)
        pl.when(jnp.logical_not(selves[k]))(copies[k].start)
    yield 1
    for k in range(2):
        if to_row:
            own = (z == 2 * c + k) & (c == z % 2)
        else:
            own = (z == 2 * k + c) & (c == z // 2)
        landed = pltpu.make_async_remote_copy(
            src_ref=src(k),
            dst_ref=dst(k),
            send_sem=lk.send.at[n + k],
            recv_sem=lk.recv.at[n + k],
            device_id=lk.near["c", 1],
            device_id_type=MESH,
        )
        pl.when(own)(keeps[k].wait)
        pl.when(jnp.logical_not(own))(landed.wait_recv)
        pl.when(jnp.logical_not(selves[k]))(copies[k].wait_send)


def cots_gather(lk, home, out):
    z, c = lk.z, lk.c
    source, place = c == z // 2, (z + 4 - 2 * c) % 4
    here, there = pl.ds(pl.multiple_of(128 * (z % 2), 128), 128), pl.ds(pl.multiple_of(128 - 128 * (z % 2), 128), 128)
    over, keeps = [], []
    for m in range(2):
        block = home.at[pl.ds(128 * m, 128)]
        over.append(lk.make(block, out.at[2 * m + c, here], lk.nbr("c", 1)))
        keeps.append(pltpu.make_async_copy(block, out.at[2 * m + c, here], lk.local.at[lk.m + m]))
    lk.m += 2
    right, left = lk.sides("z")
    own = out.at[:, here]
    a, b = lk.make(own, own, right), lk.make(own, own, left)
    half = out.at[pl.ds(0, 2), there]
    rest = out.at[pl.ds(2, 2), there]
    e, f = lk.make(half, half, right), lk.make(rest, rest, left)
    from_left = (place == 1) | (place == 2)
    from_right = jnp.logical_not(from_left)

    @pl.when(source)
    def _():
        for copy in keeps:
            copy.start()

    @pl.when(jnp.logical_not(source))
    def _():
        for copy in over:
            copy.start()

    yield 1

    @pl.when(source)
    def _():
        for copy in keeps:
            copy.wait()
        for copy in over:
            copy.wait_recv()
        a.start()
        b.start()

    @pl.when(jnp.logical_not(source))
    def _():
        for copy in over:
            copy.wait_send()

    yield 1

    @pl.when(from_left)
    def _():
        a.wait_recv()
        e.start()

    @pl.when(from_right)
    def _():
        b.wait_recv()
        f.start()

    yield 1

    @pl.when(jnp.logical_not(source))
    def _():
        e.wait_recv()
        f.wait_recv()

    @pl.when(source)
    def _():
        a.wait_send()
        b.wait_send()

    pl.when(from_left)(e.wait_send)
    pl.when(from_right)(f.wait_send)


def add_into(dst, src):
    if len(dst.shape) == 2:
        dst[...] = (dst[...].astype(F32) + src[...].astype(F32)).astype(BF)
    else:
        for i in range(dst.shape[0]):
            dst[i] = (dst[i].astype(F32) + src[i].astype(F32)).astype(BF)


def ring_reduce(lk, p, part, bufs, axis, me):
    right, left = lk.sides(axis)
    r0, r1, ra, rb = bufs
    before, after, far = lk.ring[axis]
    a = lk.put(part(far, 0), r0, right)
    b = lk.put(part(far, 1), r1, left)
    yield 1
    a.wait_recv()
    add_into(part(after, 0), r0)
    c = lk.put(p(after), ra, right)
    b.wait_recv()
    add_into(part(before, 1), r1)
    d = lk.put(p(before), rb, left)
    yield 1
    c.wait_recv()
    add_into(p(me), ra)
    d.wait_recv()
    add_into(p(me), rb)


def plane_reduce(lk, spot, sib_src, sib, bufs, out, first, kept=None):
    x, y, c = lk.x, lk.y, lk.c
    one, two = bufs
    got = lk.put(sib_src, sib, lk.nbr("c", 1))
    yield 1
    if kept is not None:
        kept.wait()
    got.wait_recv()

    def step(i, _):
        ref = spot(i // 4, i % 4)
        ref[...] = (ref[...].astype(F32) + sib[i // 4, i % 4].astype(F32)).astype(BF)
        return 0

    lax.fori_loop(0, 16, step, 0)
    every = slice(None)

    def pair(k):
        return pl.ds(2 * k, 2)

    def rows(ref, k):
        return ref.at[pl.ds(16 * k, 16)]

    if first == "y":
        yield from ring_reduce(lk, lambda j: spot(every, j), lambda j, k: spot(pair(k), j), one, "y", y)
        yield from ring_reduce(lk, lambda i: spot(i, y), lambda i, k: rows(spot(i, y), k), two, "x", x)
    else:
        yield from ring_reduce(lk, lambda i: spot(i, every), lambda i, k: spot(i, pair(k)), one, "x", x)
        yield from ring_reduce(lk, lambda j: spot(x, j), lambda j, k: rows(spot(x, j), k), two, "y", y)
    yield 1
    yield from line_gather(lk, spot(x, y), out, 16)


def ring_scratch(cols):
    return [
        pltpu.VMEM((4, 4, 32, cols), BF),
        pltpu.VMEM((2, 32, cols), BF),
        pltpu.VMEM((2, 32, cols), BF),
        pltpu.VMEM((4, 32, cols), BF),
        pltpu.VMEM((4, 32, cols), BF),
        pltpu.VMEM((16, cols), BF),
        pltpu.VMEM((16, cols), BF),
        pltpu.VMEM((32, cols), BF),
        pltpu.VMEM((32, cols), BF),
    ]


def down_scratch():
    return [
        pltpu.VMEM((4, DN, 1024), BF),
        pltpu.VMEM((4, DN, 1024), BF),
        pltpu.VMEM((80, 1024), BF),
        pltpu.VMEM((64, 1024), BF),
        pltpu.VMEM((DN, 1024), BF),
        pltpu.VMEM((DN, 1024), BF),
        pltpu.VMEM((80, 1024), BF),
        pltpu.VMEM((64, 1024), BF),
        pltpu.VMEM((DN, 1024), BF),
        pltpu.VMEM((DN, 1024), BF),
    ]


def down_reduce(lk, part_hbm, s, out):
    acc, sib, one, (x0, x1, xa, xb) = s[0], s[1], s[2:6], s[6:10]
    y, c = lk.y, lk.c
    kept = lk.keep(part_hbm.at[:, c], acc)
    got = lk.put(part_hbm.at[:, 1 - c], sib, lk.nbr("c", 1))
    yield 1
    kept.wait()
    got.wait_recv()
    add_into(acc, sib)
    yield from ring_reduce(
        lk, lambda j: acc.at[j], lambda j, k: acc.at[j, down_part(k)], one, "y", y
    )
    mine = acc.at[y]
    right, left = lk.sides("x")
    place = lk.past_x
    a = lk.make(acc.at[y, down_part(0)], x0, left)
    b = lk.make(acc.at[y, down_part(1)], x1, right)
    e = lk.make(mine, xa, left)
    f = lk.make(mine, xb, right)

    @pl.when(place == 2)
    def _():
        a.start()
        b.start()

    yield 1

    @pl.when(place == 1)
    def _():
        a.wait_recv()
        add_into(acc.at[y, down_part(0)], x0)
        e.start()

    @pl.when(place == 3)
    def _():
        b.wait_recv()
        add_into(acc.at[y, down_part(1)], x1)
        f.start()

    yield 1

    @pl.when(place == 0)
    def _():
        e.wait_recv()
        add_into(mine, xa)
        f.wait_recv()
        add_into(mine, xb)

    @pl.when(place == 1)
    def _():
        e.wait_send()

    @pl.when(place == 3)
    def _():
        f.wait_send()

    @pl.when(place == 2)
    def _():
        a.wait_send()
        b.wait_send()

    yield from ring_spread(
        lk, mine, out, lambda k: out.at[down_part(k)], "z", lk.past_z
    )


ANY = pl.BlockSpec(memory_space=pl.ANY)


def sems(n):
    return [pltpu.SemaphoreType.DMA((n,)), pltpu.SemaphoreType.DMA((n,)), pltpu.SemaphoreType.DMA((40,))]


def params(number):
    return pltpu.CompilerParams(collective_id=number, has_side_effects=True, vmem_limit_bytes=56 * 2**20)


def shape(*dims, dtype=BF):
    return jax.ShapeDtypeStruct(dims, dtype)


def lanes_of(shape):
    return lax.broadcasted_iota(jnp.int32, shape, len(shape) - 1)


def dot(left, right, dims=((1,), (0,)), kind=F32):
    return lax.dot_general(left, right, (dims, ((), ())), preferred_element_type=F32).astype(kind)


TOKENS = ((0,), (0,))
ROWS = ((1,), (1,))


def flat(value):
    return value.reshape(-1, value.shape[-1])


def head_ones():
    row = lax.broadcasted_iota(jnp.int32, (256, 256), 0) // 64
    col = lax.broadcasted_iota(jnp.int32, (256, 256), 1) // 64
    return jnp.where(row == col, 1.0 / 64, 0.0).astype(BF)


def head_mean(v, ones):
    high = v.astype(BF)
    low = (v - high.astype(F32)).astype(BF)
    return dot(high, ones) + dot(low, ones)


def halves_swapped(v):
    lane = lanes_of(v.shape)
    return jnp.where(lane % 64 < 32, pltpu.roll(v, 96, 1), pltpu.roll(v, 32, 1))


def angle_tables(tab):
    lane = lanes_of(tab.shape)
    other = pltpu.roll(tab, 64, 1)
    return jnp.where(lane < 64, tab, other), jnp.where(lane < 64, other, tab)


def row_scale(v):
    return lax.rsqrt(jnp.mean(v * v, axis=-1, keepdims=True) + EPS)


def gain_rows(whole, gain):
    def step(i, total):
        return total + whole[i // 8, (i // 2) % 4, i % 2, :, pl.ds(2048, 128)].astype(F32)

    total = lax.fori_loop(0, 32, step, jnp.zeros((32, 128), F32))
    for k in range(8):
        gain[0:1, pl.ds(128 * k, 128)] = total[8 + k : 9 + k]
        gain[1:2, pl.ds(128 * k, 128)] = total[16 + k : 17 + k]
        gain[2:3, pl.ds(128 * k, 128)] = total[0:1]
        gain[3:4, pl.ds(128 * k, 128)] = total[1:2]


def keys_values(whole, source, gain, normed, keys, values, lin_key, core):
    ones = head_ones()
    src = source[:, 0:1024].astype(F32)
    normed[...] = (src * row_scale(src) * gain[0:1]).astype(BF)
    cosine, sine = angle_tables(source[:, 1024:1152].astype(F32))
    kn = gain[3:4, 0:128]
    lane = lanes_of((256, 128))
    here = pl.ds(pl.multiple_of(core * 256, 256), 256)

    def put(ref, tile, r):
        turned = pltpu.roll(r, 64, 1)
        ref[2 * tile, here] = jnp.where(lane < 64, r, turned).astype(BF)
        ref[2 * tile + 1, here] = jnp.where(lane < 64, turned, r).astype(BF)

    for j in range(4):
        lin = dot(normed[...], flat(whole[:, :, :, :, pl.ds(1024 + 256 * j, 256)]))
        if j < 2:
            scale = lax.rsqrt(head_mean(lin * lin, ones) + EPS)
            lin_key[:, pl.ds(256 * j, 256)] = lin
            for h in range(2):
                cut = slice(128 * h, 128 * h + 128)
                v = lin[:, cut] * scale[:, cut] * kn
                put(keys, 2 * j + h, v * cosine + halves_swapped(v) * sine)
        else:
            for h in range(2):
                put(values, 2 * (j - 2) + h, lin[:, 128 * h : 128 * h + 128])


def own_queries(whole, source, gain, normed, lin_query, queries):
    ones = head_ones()
    cosine, sine = angle_tables(source[:, 1024:1152].astype(F32))
    qn = gain[2:3, 0:128]
    lane = lanes_of((256, 128))

    def step(j, _):
        lin = dot(normed[...], flat(whole[:, :, :, :, pl.ds(pl.multiple_of(256 * j, 256), 256)]))
        lin_query[:, pl.ds(pl.multiple_of(256 * j, 256), 256)] = lin
        scale = lax.rsqrt(head_mean(lin * lin, ones) + EPS)
        for h in range(2):
            cut = slice(128 * h, 128 * h + 128)
            v = lin[:, cut] * scale[:, cut] * qn
            r = (v * cosine + halves_swapped(v) * sine) * HEAD_SIZE ** (-0.5)
            first = jnp.where(lane < 64, r, 0.0).astype(BF)
            second = jnp.where(lane < 64, 0.0, r).astype(BF)
            for m in range(2):
                queries[m, 2 * j + h, 0:128] = first[128 * m : 128 * m + 128]
                queries[m, 2 * j + h, 128:256] = second[128 * m : 128 * m + 128]
        return 0

    lax.fori_loop(0, 4, step, 0)


def attend(m, queries, keys, values, starts, mask, probs, mixed, core):
    key_pos = lax.broadcasted_iota(jnp.int32, (512, 256), 0)
    query_pos = core * 256 + 128 * m + lax.broadcasted_iota(jnp.int32, (1, 256), 1) % 128
    lane = lanes_of((128, 128))
    row = starts[m, 0:1]
    begin = jnp.concatenate([row, row], axis=1)
    mask[...] = jnp.where((key_pos <= query_pos) & (key_pos.astype(F32) >= begin), 1.0, 0.0)

    def step(k, _):
        scores = dot(keys[k], queries[m, k], ROWS)
        raised = jnp.exp(scores) * mask[...]
        chance = (raised * (1.0 / jnp.sum(raised, axis=0, keepdims=True))).astype(BF)
        probs[8 * m + k] = chance
        got = dot(values[k], chance, TOKENS).T
        both = jnp.where(lane < 64, got[0:128], got[128:256]).astype(BF)
        mixed[128 * m : 128 * m + 128, pl.ds(pl.multiple_of(k * 128, 128), 128)] = both
        return 0

    lax.fori_loop(0, 8, step, 0, unroll=UNROLL)


UNROLL = 4


def out_project(m, whole, source, gain, mixed, middle, normed_ffn, own):
    rows = pl.ds(128 * m, 128)

    def step(j, _):
        cut = pl.ds(pl.multiple_of(256 * j, 256), 256)
        w = flat(whole[:, :, :, :, pl.ds(pl.multiple_of(2176 + 256 * j, 128), 256)])
        middle[rows, cut] = source[rows, cut].astype(F32) + dot(mixed[rows], w)
        return 0

    lax.fori_loop(0, 4, step, 0)
    mid = middle[rows]
    normed_ffn[own, rows] = (mid * row_scale(mid) * gain[1:2]).astype(BF)


def own_gains(params, dp):
    row = jnp.broadcast_to(params, (32, 128))
    line = lax.broadcasted_iota(jnp.int32, (32, 128), 0)
    lane = lanes_of((32, 128))
    spot = dp % 4 * 32
    window = (lane >= spot) & (lane < spot + 32)
    got = jnp.where((line == 8 + dp // 4) & window, pltpu.roll(row, spot, 1), 0.0)
    got = got + jnp.where((line == 16 + dp // 4) & window, pltpu.roll(row, (spot + 96) % 128, 1), 0.0)
    pair = (lane % 64 >= 2 * dp) & (lane % 64 < 2 * dp + 2)
    for k in range(2):
        low = pltpu.roll(row, (2 * dp + 64 - 2 * k) % 128, 1)
        high = pltpu.roll(row, (2 * dp + 128 - 2 * k) % 128, 1)
        got = got + jnp.where((line == k) & pair, jnp.where(lane < 64, low, high), 0.0)
    return got.astype(BF)


def feed_back_in(slots, cots, down, grad_hidden):
    tokens = jnp.concatenate([cots[i] for i in slots], axis=0) if len(slots) > 1 else cots[slots[0]]
    got = dot(tokens, flat(down[...]), ROWS, BF)
    for n, i in enumerate(slots):
        grad_hidden[i] = got[256 * n : 256 * n + 256]


def feed_chunk(slots, ffn, gate_up, down, grad_hidden, hidden, turned, ffn_turned, grad_both, grad_ffn, out_part):
    def load(ref, *cut):
        return jnp.concatenate([ref[(i, *cut)] for i in slots], axis=0) if len(slots) > 1 else ref[(slots[0], *cut)]

    def store(ref, value, *cut):
        for n, i in enumerate(slots):
            ref[(i, *cut)] = value[256 * n : 256 * n + 256]

    every = slice(None)
    size = 256 * len(slots)

    def step(j, _):
        cut = pl.ds(pl.multiple_of(384 * j, 128), 384)
        cut_up = pl.ds(pl.multiple_of(1152 + 384 * j, 128), 384)
        tokens = load(ffn, every, every)
        gated = dot(tokens, flat(gate_up[:, :, :, :, cut]))
        upward = dot(tokens, flat(gate_up[:, :, :, :, cut_up]))
        sigma = 1.0 / (1.0 + jnp.exp(-gated))
        silu = gated * sigma
        made = (silu * upward).astype(BF)
        hidden[0:size, cut] = made
        for n, i in enumerate(slots):
            turned[cut, pl.ds(pl.multiple_of(256 * i, 256), 256)] = made[256 * n : 256 * n + 256].T
        back = load(grad_hidden, every, cut).astype(F32)
        store(grad_both, (back * upward * sigma * (1.0 + gated * (1.0 - sigma))).astype(BF), every, cut)
        store(grad_both, (back * silu).astype(BF), every, cut_up)
        return 0

    lax.fori_loop(0, 3, step, 0)

    def last(j, _):
        cut = pl.ds(pl.multiple_of(256 * j, 256), 256)
        store(grad_ffn, dot(load(grad_both, every, every), flat(gate_up[j]), ROWS, BF), every, cut)
        store(out_part, dot(hidden[0:size], flat(down[:, :, :, cut]), kind=BF), every, cut)
        for i in slots:
            ffn_turned[cut, pl.ds(pl.multiple_of(256 * i, 256), 256)] = ffn[i, :, cut].T
        return 0

    lax.fori_loop(0, 4, last, 0)


def feed_grads(left, right, out, tiles):
    def step(j, _):
        cut = pl.ds(pl.multiple_of(256 * j, 256), 256)
        got = dot(left[...], flat(right[:, :, cut]), kind=BF)
        lead = out.shape[:-1]
        out[(slice(None),) * len(lead) + (cut,)] = got.reshape(*lead, 256)
        return 0

    lax.fori_loop(0, tiles, step, 0)


FWD_SCRATCH = [
    pltpu.VMEM((4, 4, 2, 32, WA), BF),
    pltpu.VMEM((4, 4, 2, 32, GU), BF),
    pltpu.VMEM((4, 2, DN, 1024), BF),
    pltpu.VMEM((256, 1152), BF),
    pltpu.VMEM((256, 128), F32),
    pltpu.VMEM((256, 1152), BF),
    pltpu.VMEM((4, 256, 1024), BF),
    pltpu.VMEM((4, 256, 1024), BF),
    pltpu.VMEM((256, 1024), BF),
    pltpu.VMEM((256, 1024), F32),
    pltpu.VMEM((256, 512), F32),
    pltpu.VMEM((8, 512, 128), BF),
    pltpu.VMEM((8, 512, 128), BF),
    pltpu.VMEM((2, 8, 256, 128), BF),
    pltpu.VMEM((16, 512, 256), BF),
    pltpu.VMEM((256, 1024), BF),
    pltpu.VMEM((256, 1024), F32),
    pltpu.VMEM((8, 1024), F32),
    pltpu.VMEM((4, 256, 1152), BF),
    pltpu.VMEM((512, 1152), BF),
    pltpu.VMEM((1152, 1024), BF),
    pltpu.VMEM((1024, 1024), BF),
    pltpu.VMEM((4, 256, GU), BF),
    pltpu.VMEM((4, 256, 1024), BF),
    pltpu.VMEM((4, 256, 1024), BF),
    pltpu.VMEM((256, 1024), BF),
    pltpu.VMEM((256, 1024), BF),
    pltpu.VMEM((4, 64, 1024), BF),
    pltpu.VMEM((2, 8, 128), F32),
    pltpu.VMEM((32, WA), BF),
    pltpu.VMEM((32, GU), BF),
    pltpu.VMEM((1, 128), F32),
    pltpu.VMEM((512, 256), F32),
]

FWD_OUT = (
    shape(4, 4, 2, 32, WA),
    shape(256, 1024),
    shape(256, 1024, dtype=F32),
    shape(256, 512, dtype=F32),
    shape(8, 512, 128),
    shape(8, 512, 128),
    shape(2, 8, 256, 128),
    shape(16, 512, 256),
    shape(256, 1024),
    shape(256, 1024, dtype=F32),
    shape(8, 1024, dtype=F32),
    shape(4, 4, 2, 32, GU),
    shape(4, 2, DN, 1024),
    shape(4, 256, 1024),
    shape(256, 1024, dtype=F32),
    shape(256, 1152),
    shape(256, 1024),
)


FWD_IN = 12


def go(*steps):
    for s in steps:
        next(s, None)


def fwd_kernel(*refs):
    w_query, key_weight, value_weight, w_out, w_gate, w_up, dn, x, cot, tab, starts_hbm, params_hbm = refs[:FWD_IN]
    refs = refs[FWD_IN:]
    outs, refs = refs[: len(FWD_OUT)], refs[len(FWD_OUT) :]
    lk = Links(*refs[:3])
    (
        whole, gate_up, down, source, table, at_home, cots, ffn, normed, lin_query, lin_key, keys, values, queries,
        probs, mixed, middle, gain, grad_hidden, hidden, turned, ffn_turned, grad_both, grad_ffn, out_part,
        from_right, from_left, passing, starts, wa, gu, own_params, mask,
    ) = refs[3:]
    own = lk.z
    before, after, far = lk.ring["z"]
    quarter = pl.ds(pl.multiple_of(own * 1152, 128), 1152)
    staged = [
        lk.keep(params_hbm, own_params),
        lk.keep(tab, table),
        lk.keep(x, at_home.at[:, pl.ds(0, 1024)]),
        lk.keep(w_query, wa.at[:, pl.ds(0, 1024)]),
        lk.keep(key_weight, wa.at[:, pl.ds(1024, 512)]),
        lk.keep(value_weight, wa.at[:, pl.ds(1536, 512)]),
        lk.keep(w_out, wa.at[:, pl.ds(2176, 1024)]),
        lk.keep(w_gate.at[:, quarter], gu.at[:, pl.ds(0, 1152)]),
        lk.keep(w_up.at[:, quarter], gu.at[:, pl.ds(1152, 1152)]),
    ]
    staged[0].wait()
    staged[1].wait()
    at_home[:, 1024:1152] = table[...].astype(BF)
    wa[:, 2048:2176] = own_gains(own_params[...], lax.axis_index("dp"))
    for copy in staged[2:]:
        copy.wait()
    lk.barrier()
    k1 = plane_gather(lk, wa, whole, "x", 1024, 1536)
    k2 = plane_gather(lk, wa, whole, "y", 1536, 2176)
    a1 = plane_gather(lk, wa, whole, "x", 0, 1024)
    a2 = plane_gather(lk, wa, whole, "y", 2176, WA)
    half = [pl.ds(0, 128), pl.ds(128, 128)]

    def slot(j):
        return pl.ds(128 * j, 128) if isinstance(j, int) else pl.ds(pl.multiple_of(128 * j, 128), 128)

    x1 = swap_blocks(lk, lambda m: at_home.at[half[m]], lambda j: source.at[slot(j)], True)
    s1 = swap_blocks(lk, lambda m: starts_hbm.at[m], lambda j: starts.at[j], True)
    g1 = plane_gather(lk, gu, gate_up, "x", 0, 1152)
    g2 = plane_gather(lk, gu, gate_up, "y", 1152, GU)
    d1 = down_gather(lk, dn, down)
    c1 = cots_gather(lk, cot, cots)
    go(x1, s1, c1)
    go(k1, k2)
    go(a1, a2)
    go(k1, k2)
    go(a1, a2)
    go(k1, k2)
    go(a1, a2)
    go(x1, s1)
    go(c1)
    go(k1, k2)
    go(g1, g2)
    go(k1, k2)
    go(a1, a2)
    go(d1)
    drive(k1, k2, x1, s1)
    gain_rows(whole, gain)
    keys_values(whole, source, gain, normed, keys, values, lin_key, lk.c)
    mine = pl.ds(pl.multiple_of(lk.c * 256, 256), 256)
    crossed = [lk.put(ref.at[:, mine], ref.at[:, mine], lk.nbr("c", 1)) for ref in (keys, values)]
    go(a1, a2)
    drive(a1, a2)
    own_queries(whole, source, gain, normed, lin_query, queries)
    go(g1, g2)
    go(c1)
    for copy in crossed:
        copy.wait_recv()
    saved = [lk.keep(source, outs[15])]
    for k, ref in enumerate((normed, lin_query, lin_key, keys, values, queries)):
        saved.append(lk.keep(ref, outs[1 + k]))
    passed = []
    for m in range(2):
        attend(m, queries, keys, values, starts, mask, probs, mixed, lk.c)
        if m == 0:
            go(g1, g2)
            go(d1)
            saved.append(lk.keep(whole, outs[0]))
        out_project(m, whole, source, gain, mixed, middle, ffn, own)
        rows = pl.ds(128 * m, 128)

        def part(i, k, m=m):
            return ffn.at[i, pl.ds(128 * m + 64 * k, 64)]

        passed.append(
            ring_gather(lk, ffn.at[own, rows], lambda i, rows=rows: ffn.at[i, rows], part, "z", own)
        )
        go(passed[m])
        if m == 0:
            go(c1)
            go(g1, g2)
            go(d1)
    go(passed[0])
    go(g1, g2)
    go(d1)
    drive(c1)
    saved.append(lk.keep(cots.at[own], outs[16]))
    for k, ref in enumerate((probs, mixed, middle, gain)):
        saved.append(lk.keep(ref, outs[7 + k]))
    drive(g1, g2, d1)
    feed_back_in((own,), cots, down, grad_hidden)
    go(passed[1])

    def chunk(*slots):
        feed_chunk(
            slots, ffn, gate_up, down, grad_hidden, hidden, turned, ffn_turned, grad_both, grad_ffn, out_part
        )

    right, left = lk.sides("z")
    chunk(own)
    lk.flush()
    feed_back_in((before, after), cots, down, grad_hidden)
    chunk(before, after)
    low, high = pl.ds(0, 128), pl.ds(128, 128)
    sent = [
        lk.put(grad_ffn.at[after, high], from_left.at[high], right),
        lk.put(grad_ffn.at[before, low], from_right.at[low], left),
    ]
    feed_back_in((far,), cots, down, grad_hidden)
    drive(*passed)
    chunk(far)
    saved.append(lk.keep(out_part, outs[13]))
    hops = []
    for k in range(2):
        rows = pl.ds(64 * k, 64)
        hops.append((lk.put(grad_ffn.at[far, rows], passing.at[k], right), after, rows, from_left, right))
    for k in range(2):
        rows = pl.ds(128 + 64 * k, 64)
        hops.append((lk.put(grad_ffn.at[far, rows], passing.at[2 + k], left), before, rows, from_right, left))

    def hop(k):
        copy, slot, rows, landing, to = hops[k]
        copy.wait_recv()
        add_into(grad_ffn.at[slot, rows], passing.at[k])
        sent.append(lk.put(grad_ffn.at[slot, rows], landing.at[rows], to))

    feed_grads(turned, cots, down, 4)
    saved.append(lk.keep(down, outs[12]))
    hop(0)
    hop(2)
    feed_grads(ffn_turned, grad_both, gate_up, 9)
    hop(1)
    hop(3)
    saved.append(lk.keep(gate_up, outs[11]))
    for copy in sent:
        copy.wait_recv()
    for copy in saved:
        copy.wait()
    total = grad_ffn[own].astype(F32) + from_right[...].astype(F32) + from_left[...].astype(F32)
    lin_query[...] = total
    lk.keep(lin_query, outs[14]).wait()
    lk.flush()


def forward(*args):
    return pl.pallas_call(
        fwd_kernel,
        out_shape=FWD_OUT,
        in_specs=[ANY] * FWD_IN,
        out_specs=[ANY] * len(FWD_OUT),
        scratch_shapes=sems(128) + FWD_SCRATCH,
        compiler_params=pltpu.CompilerParams(
            collective_id=0, has_side_effects=True, vmem_limit_bytes=60 * 2**20
        ),
    )(*args)


BWD_IN = 17
PIECES = (1152, 1152, 512, 512, 512, 512, 512, 512, 128)
BWD_OUT = (
    shape(2, 128, 1024),
    shape(2, 128, 1024),
    shape(4, 32, WA),
    shape(4, 32, GU),
    shape(DN, 1024),
)
BWD_SCRATCH = [
    pltpu.VMEM((4, 4, 2, 32, WA), BF),
    pltpu.VMEM((256, 1024), BF),
    pltpu.VMEM((256, 1024), F32),
    pltpu.VMEM((256, 512), F32),
    pltpu.VMEM((8, 512, 128), BF),
    pltpu.VMEM((8, 512, 128), BF),
    pltpu.VMEM((2, 8, 256, 128), BF),
    pltpu.VMEM((16, 512, 256), BF),
    pltpu.VMEM((256, 1024), BF),
    pltpu.VMEM((256, 1024), F32),
    pltpu.VMEM((8, 1024), F32),
    pltpu.VMEM((4, 256, 1024), BF),
    pltpu.VMEM((256, 1024), F32),
    pltpu.VMEM((256, 1024), BF),
    pltpu.VMEM((256, 1152), BF),
]
BWD_WORK = [
    pltpu.VMEM((256, 1024), BF),
    pltpu.VMEM((2, 8, 256, 128), BF),
    pltpu.VMEM((256, 1024), F32),
    pltpu.VMEM((2, 256, 1024), BF),
    pltpu.VMEM((256, 2048), BF),
    pltpu.VMEM((1024, 256), BF),
    pltpu.VMEM((256, 1024), F32),
    pltpu.VMEM((8, 1024), F32),
    pltpu.VMEM((4, 4, 2, 32, WA), BF),
    pltpu.VMEM((4, 4, 32, 1152), BF),
    pltpu.VMEM((4, 4, 32, 1152), BF),
    pltpu.VMEM((256, 1024), BF),
    pltpu.VMEM((256, 1024), BF),
    pltpu.VMEM((256, 1024), BF),
]
Z_RING = [
    pltpu.VMEM((128, 1024), BF),
    pltpu.VMEM((128, 1024), BF),
    pltpu.VMEM((256, 1024), BF),
    pltpu.VMEM((256, 1024), BF),
]


def norm_back(v, g, dy):
    r = row_scale(v)
    gdy = g * dy
    back = r * gdy - v * (r * r * r * jnp.mean(v * gdy, axis=-1, keepdims=True))
    return back, jnp.sum(v * r * dy, axis=0, keepdims=True)


def heads_back(lin, grad, gain, cosine, sine, ones):
    parts = []
    for h in range(2):
        part = grad[:, 128 * h : 128 * h + 128]
        parts.append(part * cosine + halves_swapped(part * sine))
    dy = jnp.concatenate(parts, axis=1)
    r = lax.rsqrt(head_mean(lin * lin, ones) + EPS)
    gdy = dy * gain
    back = r * gdy - lin * (r * r * r * head_mean(lin * gdy, ones))
    return back, jnp.sum(lin * r * dy, axis=0, keepdims=True)


def turned_grads(turned, right, out, start, tiles, base=0):
    def step(j, _):
        got = dot(turned[...], right[:, pl.ds(pl.multiple_of(base + 256 * j, 256), 256)], kind=BF)
        out[:, :, :, :, pl.ds(pl.multiple_of(start + 256 * j, 128), 256)] = got.reshape(4, 4, 2, 32, 256)
        return 0

    lax.fori_loop(0, tiles, step, 0)


def attend_back(queries, keys, values, probs, grad_mixed, grad_queries, grad_kv):
    lane = lanes_of((128, 128))
    lane_keys = lanes_of((512, 128))

    def step(j, _):
        folded = []
        for e in range(2):
            k = 2 * j + e
            cut = pl.ds(pl.multiple_of(128 * k, 128), 128)
            key_sum = value_sum = None
            for m in range(2):
                chance = probs[8 * m + k]
                back = dot(values[k], grad_mixed[m, k], ROWS)
                p = chance.astype(F32)
                p_back = p * back
                grad_scores = (p_back - p * jnp.sum(p_back, axis=0, keepdims=True)).astype(BF)
                got = dot(keys[k], grad_scores, TOKENS).T
                grad_queries[128 * m : 128 * m + 128, cut] = jnp.where(lane < 64, got[0:128], got[128:256])
                more_keys, more_values = dot(grad_scores, queries[m, k]), dot(chance, grad_mixed[m, k])
                key_sum = more_keys if m == 0 else key_sum + more_keys
                value_sum = more_values if m == 0 else value_sum + more_values
            folded += [v + pltpu.roll(v, 64, 1) for v in (key_sum, value_sum)]
        for s in range(2):
            tile = jnp.where(lane_keys < 64, folded[s], folded[2 + s]).astype(BF)
            cut = pl.ds(pl.multiple_of(512 * s + 128 * j, 128), 128)
            grad_kv[0, :, cut] = tile[0:256]
            grad_kv[1, :, cut] = tile[256:512]
        return 0

    lax.fori_loop(0, 4, step, 0)


def bwd_kernel(*refs):
    ins, refs = refs[:BWD_IN], refs[BWD_IN:]
    outs, refs = refs[: len(BWD_OUT)], refs[len(BWD_OUT) :]
    lk = Links(*refs[:3])
    refs = refs[3:]
    n = len(BWD_SCRATCH)
    held, refs = refs[:n], refs[n:]
    (
        whole, normed, lin_query, lin_key, keys, values, queries, probs, mixed, middle, gain, out_part, grad_middle,
        upstream, source,
    ) = held
    grad_gu, grad_down = ins[15:]
    n = len(BWD_WORK)
    work, refs = refs[:n], refs[n:]
    (
        grad_branch, grad_mixed, grad_queries, grad_kv, grad_lin, turned, grad_normed, gains_back, grad_whole, acc_a,
        acc_b, made, sent_back, kv_other,
    ) = work
    z_out, refs = refs[:4], refs[4:]
    down_refs, refs = refs[:10], refs[10:]
    rings = [refs[9 * i : 9 * i + 9] for i in range(len(PIECES))]
    outputs, grad_inputs, a_all, gu_all, down_own = outs
    own, c = lk.z, lk.c

    order = [11, 12, 9, 13, 10, 0, 8, 5, 7, 6, 4, 2, 14, 1, 3]
    loads = {}
    for k in order[:7]:
        loads[k] = lk.keep(ins[k], held[k])
    lk.barrier()

    def piece(k, spot, src, out, first, kept=None):
        ring = rings[k]
        return plane_reduce(lk, spot, src, ring[0], (ring[1:5], ring[5:9]), out, first, kept)

    def feed_piece(k, acc, lo, first):
        cols = pl.ds(lo, 1152)
        kept = lk.keep(grad_gu.at[:, :, c, :, cols], acc)
        return piece(
            k, lambda i, j: acc.at[i, j], grad_gu.at[:, :, lk.other, :, cols], gu_all.at[:, :, cols], first, kept
        )

    def whole_piece(k, lo, first):
        cols = pl.ds(lo, PIECES[k])
        return piece(
            k, lambda i, j: grad_whole.at[i, j, c, :, cols], grad_whole.at[:, :, lk.other, :, cols],
            a_all.at[:, :, cols], first,
        )

    def out_chain():
        yield from ring_reduce(
            lk, lambda i: out_part.at[i], lambda i, k: out_part.at[i, pl.ds(128 * k, 128)], z_out, "z", own
        )
        made[...] = (middle[...] + out_part[own].astype(F32)).astype(BF)
        yield from swap_blocks(
            lk, lambda j: made.at[pl.ds(128 * j, 128)], lambda m: outputs.at[m], False
        )

    def need(*names):
        for k in names:
            loads.pop(k).wait()

    f1, f2 = feed_piece(0, acc_a, 0, "y"), feed_piece(1, acc_b, 1152, "x")
    d1 = down_reduce(lk, grad_down, down_refs, down_own)
    go(d1, f1, f2)
    o1 = out_chain()
    need(11)
    go(o1)
    for k in order[7:]:
        loads[k] = lk.keep(ins[k], held[k])
    need(12, 9, 13, 10)
    back, row = norm_back(middle[...], gain[1:2], grad_middle[...])
    total = upstream[...].astype(F32) + back
    grad_middle[...] = total
    grad_branch[...] = total.astype(BF)
    gains_back[1:2] = row
    need(0, 8)
    go(d1)
    lane = lanes_of((256, 128))

    def back_mixed(j, _):
        got = dot(grad_branch[...], flat(whole[j, :, :, :, pl.ds(2176, 1024)]), ROWS)
        for h in range(2):
            r = got[:, 128 * h : 128 * h + 128]
            first = jnp.where(lane < 64, r, 0.0).astype(BF)
            second = jnp.where(lane < 64, 0.0, r).astype(BF)
            for m in range(2):
                grad_mixed[m, 2 * j + h, 0:128] = first[128 * m : 128 * m + 128]
                grad_mixed[m, 2 * j + h, 128:256] = second[128 * m : 128 * m + 128]
        return 0

    lax.fori_loop(0, 4, back_mixed, 0)
    go(f2, f1)
    need(5, 7, 6, 4)
    attend_back(queries, keys, values, probs, grad_mixed, grad_queries, grad_kv)
    crossed = lk.put(grad_kv.at[lk.other], kv_other, lk.nbr("c", 1))
    go(d1)
    go(f2, f1)
    turned[...] = mixed[...].T
    turned_grads(turned, grad_branch, grad_whole, 2176, 4)
    p2, p3 = whole_piece(2, 2176, "y"), whole_piece(3, 2688, "x")
    go(p2, p3)
    go(d1)
    go(f2)
    need(2, 14, 1)
    ones = head_ones()
    cosine, sine = angle_tables(source[:, 1024:1152].astype(F32))

    def back_query(j, _):
        cut = pl.ds(pl.multiple_of(256 * j, 256), 256)
        grad = grad_queries[:, cut] * HEAD_SIZE ** (-0.5)
        got, line = heads_back(lin_query[:, cut], grad, gain[2:3, 0:256], cosine, sine, ones)
        grad_lin[:, cut] = got.astype(BF)
        gains_back[2:3, cut] = line
        return 0

    lax.fori_loop(0, 4, back_query, 0)
    turned[...] = normed[...].T
    need(3)
    crossed.wait_recv()

    def back_key(j, _):
        cut = pl.ds(pl.multiple_of(256 * j, 256), 256)
        grad = grad_kv[c, :, cut].astype(F32) + kv_other[:, cut].astype(F32)
        got, line = heads_back(lin_key[:, cut], grad, gain[3:4, 0:256], cosine, sine, ones)
        grad_lin[:, pl.ds(pl.multiple_of(1024 + 256 * j, 256), 256)] = got.astype(BF)
        gains_back[3:4, cut] = line
        return 0

    lax.fori_loop(0, 2, back_key, 0)
    value_sum = grad_kv[c, :, 512:1024].astype(F32) + kv_other[:, 512:1024].astype(F32)
    grad_lin[:, 1536:2048] = value_sum.astype(BF)

    turned_grads(turned, grad_lin, grad_whole, 1024, 4, 1024)
    p6, p7 = whole_piece(6, 1024, "y"), whole_piece(7, 1536, "x")
    go(p6, p7)
    go(d1)
    go(f2)
    turned_grads(turned, grad_lin, grad_whole, 0, 4)
    p4, p5 = whole_piece(4, 0, "y"), whole_piece(5, 512, "x")
    go(p4, p5)
    go(p2, p3)
    go(f1)

    def back_normed(j, _):
        grad_normed[:, pl.ds(pl.multiple_of(256 * j, 256), 256)] = dot(
            grad_lin[...], flat(whole[j, :, :, :, pl.ds(0, 2048)]), ROWS
        )
        return 0

    lax.fori_loop(0, 4, back_normed, 0)
    go(p6, p7)
    go(p2, p3)
    go(o1)
    go(f2, f1)
    back, row = norm_back(source[:, 0:1024].astype(F32), gain[0:1], grad_normed[...])
    gains_back[0:1] = row
    sent_back[...] = (grad_middle[...] + back).astype(BF)
    i1 = swap_blocks(lk, lambda j: sent_back.at[pl.ds(128 * j, 128)], lambda m: grad_inputs.at[m], False)
    go(i1)
    small = [jnp.zeros((1, 128), F32)] * 2
    for s, tiles in ((0, 8), (1, 4)):
        for k in range(tiles):
            small[s] = small[s] + gains_back[2 + s : 3 + s, 128 * k : 128 * k + 128]
        small[s] = small[s] + pltpu.roll(jnp.broadcast_to(small[s], (8, 128)), 64, 1)[0:1]
    heads = jnp.where(lanes_of((1, 128)) < 64, small[0], small[1])
    line = lax.broadcasted_iota(jnp.int32, (32, 128), 0)
    for k in range(8):
        cut = slice(128 * k, 128 * k + 128)
        block = jnp.where(line == 8, gains_back[0:1, cut], 0.0)
        block = jnp.where(line == 16, gains_back[1:2, cut], block)
        block = jnp.where(line == 0, heads, block).astype(BF)
        for d in range(4 * k, 4 * k + 4):
            grad_whole[d // 8, (d // 2) % 4, d % 2, :, 2048:2176] = block
    p8 = whole_piece(8, 2048, "y")
    go(p8)
    go(p4, p5)
    go(p6, p7)
    go(p2, p3)
    go(d1)
    go(p8)
    go(p4, p5)
    go(p6, p7)
    go(f2, f1)
    go(p2, p3)
    go(p8)
    go(d1)
    go(p4, p5)
    go(p6, p7)
    go(o1)
    go(p8)
    go(f2, f1)
    go(p2, p3)
    go(p6, p7)
    go(p4, p5)
    go(p8)
    go(p6, p7)
    go(p4, p5)
    go(p8)
    drive(p6, p7, p4, p5, p8, p2, p3, f1, f2, d1, o1, i1)
    lk.flush()


def backward(*args):
    return pl.pallas_call(
        bwd_kernel,
        out_shape=BWD_OUT,
        in_specs=[ANY] * BWD_IN,
        out_specs=[ANY] * len(BWD_OUT),
        scratch_shapes=sems(160) + BWD_SCRATCH + BWD_WORK + Z_RING + down_scratch()
        + [v for cols in PIECES for v in ring_scratch(cols)],
        compiler_params=pltpu.CompilerParams(
            collective_id=1, has_side_effects=True, vmem_limit_bytes=62 * 2**20
        ),
    )(*args)


def finish_kernel(*refs):
    ins, outs, held, local = refs[:5], refs[5:15], refs[15:19], refs[19]
    o_out, o_in, o_query, o_key, o_value, o_wout, o_gate, o_up, o_down, o_gains = outs
    a_all, gu_all, down, grad_in = held
    pairs = [(ins[2], a_all), (ins[3], gu_all), (ins[4], down), (ins[0], o_out), (ins[1], grad_in)]
    copies = [pltpu.make_async_copy(src, dst, local.at[k]) for k, (src, dst) in enumerate(pairs)]
    for copy in copies:
        copy.start()
    copies[0].wait()
    for ref, lo, size in (
        (o_query, 0, 1024), (o_key, 1024, 512), (o_value, 1536, 512), (o_gains, 2048, 128), (o_wout, 2176, 1024),
    ):
        total = a_all[0, :, lo : lo + size].astype(F32)
        for i in range(1, 4):
            total = total + a_all[i, :, lo : lo + size].astype(F32)
        ref[...] = total
    copies[1].wait()
    for i in range(4):
        o_gate[:, 1152 * i : 1152 * i + 1152] = gu_all[i, :, 0:1152].astype(F32)
        o_up[:, 1152 * i : 1152 * i + 1152] = gu_all[i, :, 1152:2304].astype(F32)
    copies[2].wait()
    o_down[...] = down[...].astype(F32)
    copies[4].wait()
    o_in[...] = grad_in[...].astype(F32)
    copies[3].wait()


def finish(*args):
    vmem = pl.BlockSpec(memory_space=pltpu.VMEM)
    return pl.pallas_call(
        finish_kernel,
        out_shape=(
            shape(2, 128, 1024), shape(2, 128, 1024, dtype=F32), shape(32, 1024, dtype=F32), shape(32, 512, dtype=F32),
            shape(32, 512, dtype=F32), shape(32, 1024, dtype=F32), shape(32, 4608, dtype=F32),
            shape(32, 4608, dtype=F32), shape(DN, 1024, dtype=F32), shape(32, 128, dtype=F32),
        ),
        in_specs=[ANY] * 5,
        out_specs=[ANY] + [vmem] * 9,
        scratch_shapes=[
            pltpu.VMEM((4, 32, WA), BF), pltpu.VMEM((4, 32, GU), BF), pltpu.VMEM((DN, 1024), BF),
            pltpu.VMEM((2, 128, 1024), BF), pltpu.SemaphoreType.DMA((5,)),
        ],
        compiler_params=pltpu.CompilerParams(vmem_limit_bytes=60 * 2**20),
    )(*args)


def body(
    inputs, starts, w_query, key_weight, value_weight, w_out, w_gate, w_up, w_down,
    prenorm, midnorm, querynorm, keynorm, cotangent,
):
    z = lax.axis_index("seq")
    dp = lax.axis_index("dp")
    params = jnp.concatenate([prenorm, midnorm, querynorm, keynorm, jnp.zeros((60,), BF)])
    params = params.astype(F32).reshape(1, 128)
    pos = z * 128 + jnp.arange(128, dtype=jnp.int32)
    inside = pos - starts[:, 0]
    frequency = ROPE_BASE ** (-(jnp.arange(32, dtype=F32) * 2.0 / 64))
    angle = inside.reshape(256, 1).astype(F32) * frequency[None, :]
    cosine, sine = jnp.cos(angle), jnp.sin(angle)
    tab = jnp.concatenate([cosine, cosine, -sine, sine], axis=1)
    begin = jnp.broadcast_to(starts.astype(F32), (2, 8, 128))
    source = inputs.reshape(256, 1024)
    upstream = cotangent.reshape(256, 1024)
    (
        whole, normed, lin_query, lin_key, keys, values, queries, probs, mixed, middle, gain, grad_gu, grad_down,
        out_part, grad_ffn, row_source, row_upstream,
    ) = forward(
        w_query, key_weight, value_weight, w_out, w_gate, w_up, w_down, source, upstream, tab, begin, params
    )
    done = backward(
        whole, normed, lin_query, lin_key, keys, values, queries, probs, mixed, middle, gain, out_part, grad_ffn,
        row_upstream, row_source, grad_gu, grad_down,
    )
    outputs, grad_inputs, d_query, d_key, d_value, d_out, d_gate, d_up, d_down, d_gains = finish(*done)
    both = dp % 4 * 32
    return (
        outputs.reshape(2, 1, 128, 1024),
        grad_inputs.reshape(2, 1, 128, 1024),
        d_query,
        d_key,
        d_value,
        d_out,
        d_gate,
        d_up,
        d_down,
        lax.dynamic_slice(d_gains, (8, both), (1, 32))[0],
        lax.dynamic_slice(d_gains, (16, both), (1, 32))[0],
        lax.dynamic_slice(d_gains, (0, 2 * dp), (1, 2))[0],
        lax.dynamic_slice(d_gains, (0, 64 + 2 * dp), (1, 2))[0],
    )


def solution(mesh):
    tokens, matrix, vector = P(None, "dp", "seq", None), P("dp", None), P("dp")
    return jax.shard_map(
        body,
        mesh=mesh,
        in_specs=(tokens, P(None, "dp", "seq")) + (matrix,) * 7 + (vector,) * 4 + (tokens,),
        out_specs=(tokens, tokens) + (matrix,) * 7 + (vector,) * 4,
        check_vma=False,
    )
```

```python
from functools import partial

import jax
import jax.numpy as jnp
from jax import lax
from jax.experimental import pallas as pl
from jax.experimental.pallas import tpu as pltpu
from jax.sharding import PartitionSpec as P

QUERY_HEADS = 16
KEY_VALUE_HEADS = 8
HEAD_SIZE = 64
EPS = 1e-05
ROPE_BASE = 1000000.0

MESH = pl.DeviceIdType.MESH
BF = jnp.bfloat16
F32 = jnp.float32
WA = 3200
GU = 2304
DN = 144


class Links:
    def __init__(self, send, recv, local):
        dp = lax.axis_index("dp")
        self.z = lax.axis_index("seq")
        self.x, self.y, self.c = dp // 8, (dp // 2) % 4, dp % 2
        self.send, self.recv, self.local = send, recv, local
        self.n = self.m = 0
        self.out = []
        self.other = 1 - self.c
        place = {"x": self.x, "y": self.y, "z": self.z}
        self.ring = {k: ((v + 3) % 4, (v + 1) % 4, (v + 2) % 4) for k, v in place.items()}
        self.past_x = (self.x - self.z + 4) % 4
        self.past_z = (self.z - self.x + 4) % 4
        self.near = {("c", 1): self.dev(self.x, self.y, self.other, self.z)}
        for k, (before, after, far) in self.ring.items():
            for step, v in ((-1, before), (1, after)):
                spot = dict(place, **{k: v})
                self.near[k, step] = self.dev(spot["x"], spot["y"], self.c, spot["z"])

    def dev(self, x, y, c, z):
        return ((x * 4 + y) * 2 + c, z)

    def nbr(self, axis, step):
        return self.near[axis, step]

    def sides(self, axis):
        return self.nbr(axis, 1), self.nbr(axis, -1)

    def barrier(self):
        sem = pltpu.get_barrier_semaphore()
        targets = [self.nbr(axis, step) for axis in "xy" for step in (1, -1)]
        for k in range(1, 8):
            spot = (self.z * 2 + self.c + k) % 8
            targets.append(self.dev(self.x, self.y, spot % 2, spot // 2))
        for device in targets:
            pl.semaphore_signal(sem, inc=1, device_id=device, device_id_type=MESH)
        pl.semaphore_wait(sem, len(targets))

    def make(self, src, dst, to):
        copy = pltpu.make_async_remote_copy(
            src_ref=src,
            dst_ref=dst,
            send_sem=self.send.at[self.n],
            recv_sem=self.recv.at[self.n],
            device_id=to,
            device_id_type=MESH,
        )
        self.n += 1
        assert self.n <= self.send.shape[0]
        return copy

    def put(self, src, dst, to):
        copy = self.make(src, dst, to)
        copy.start()
        self.out.append(copy)
        return copy

    def keep(self, src, dst):
        copy = pltpu.make_async_copy(src, dst, self.local.at[self.m])
        self.m += 1
        assert self.m <= self.local.shape[0]
        copy.start()
        return copy

    def flush(self):
        for copy in self.out:
            copy.wait_send()
        self.out = []


def drive(*steps):
    steps = list(steps)
    while steps:
        steps = [s for s in steps if next(s, "end") != "end"]


def ring_gather(lk, own, slot, part, axis, me, ready=None):
    right, left = lk.sides(axis)
    before, after, far = lk.ring[axis]
    a = lk.put(own, slot(me), right)
    b = lk.put(own, slot(me), left)
    yield 1
    a.wait_recv()
    c = lk.put(part(before, 0), part(before, 0), right)
    if ready:
        ready(before)
    b.wait_recv()
    d = lk.put(part(after, 1), part(after, 1), left)
    if ready:
        ready(after)
    yield 1
    c.wait_recv()
    d.wait_recv()
    if ready:
        ready(far)


def plane_gather(lk, own, out, first, lo, hi):
    cols = pl.ds(lo, hi - lo)
    x, y, c = lk.x, lk.y, lk.c
    kept = lk.keep(own.at[:, cols], out.at[x, y, c, :, cols])
    crossing = []

    def cross(ref):
        crossing.append(lk.put(ref, ref, lk.nbr("c", 1)))

    def rows(k):
        return pl.ds(16 * k, 16)

    def two(k):
        return pl.ds(2 * k, 2)

    if first == "x":
        yield from ring_gather(
            lk, own.at[:, cols], lambda i: out.at[i, y, c, :, cols],
            lambda i, k: out.at[i, y, c, rows(k), cols], "x", x,
        )
        kept.wait()
        whole = out.at[:, y, c, :, cols]
        cross(whole)
        yield from ring_gather(
            lk, whole, lambda j: out.at[:, j, c, :, cols],
            lambda j, k: out.at[two(k), j, c, :, cols], "y", y,
            lambda j: cross(out.at[:, j, c, :, cols]),
        )
    else:
        yield from ring_gather(
            lk, own.at[:, cols], lambda j: out.at[x, j, c, :, cols],
            lambda j, k: out.at[x, j, c, rows(k), cols], "y", y,
        )
        kept.wait()
        whole = out.at[x, :, c, :, cols]
        cross(whole)
        yield from ring_gather(
            lk, whole, lambda i: out.at[i, :, c, :, cols],
            lambda i, k: out.at[i, two(k), c, :, cols], "x", x,
            lambda i: cross(out.at[i, :, c, :, cols]),
        )
    yield 1
    for copy in crossing:
        copy.wait_recv()


def ring_spread(lk, own, dst, part, axis, place):
    right, left = lk.sides(axis)
    a, b = lk.make(own, dst, right), lk.make(own, dst, left)
    c, d = lk.make(part(0), part(0), right), lk.make(part(1), part(1), left)
    kept = pltpu.make_async_copy(own, dst, lk.local.at[lk.m])
    lk.m += 1

    @pl.when(place == 0)
    def _():
        a.start()
        b.start()
        kept.start()

    yield 1

    @pl.when(place == 1)
    def _():
        a.wait_recv()
        c.start()

    @pl.when(place == 3)
    def _():
        b.wait_recv()
        d.start()

    yield 1

    @pl.when(place == 2)
    def _():
        c.wait_recv()
        d.wait_recv()

    @pl.when(place == 0)
    def _():
        kept.wait()
        a.wait_send()
        b.wait_send()

    @pl.when(place == 1)
    def _():
        c.wait_send()

    @pl.when(place == 3)
    def _():
        d.wait_send()


def down_cut(lo, rows):
    first = (rows // 16 + 1) // 2 * 16
    return lambda k: pl.ds(lo, first) if k == 0 else pl.ds(lo + first, rows - first)


def down_gather(lk, own, out, lo, rows):
    y, c = lk.y, lk.c
    every, cut = pl.ds(lo, rows), down_cut(lo, rows)
    yield from ring_spread(
        lk, own.at[every], out.at[y, c, every], lambda k: out.at[y, c, cut(k)], "x", lk.past_x
    )
    crossing = []

    def cross(j):
        ref = out.at[j, c, every]
        crossing.append(lk.put(ref, ref, lk.nbr("c", 1)))

    cross(y)
    yield from ring_gather(
        lk, out.at[y, c, every], lambda j: out.at[j, c, every], lambda j, k: out.at[j, c, cut(k)], "y", y, cross
    )
    yield 1
    for copy in crossing:
        copy.wait_recv()


def line_gather(lk, own, out, cut):
    z, rows = lk.z, own.shape[0]
    kept = lk.keep(own, out.at[z])

    def part(i, k):
        return out.at[i, pl.ds(0, cut)] if k == 0 else out.at[i, pl.ds(cut, rows - cut)]

    rest = ring_gather(lk, own, lambda i: out.at[i], part, "z", z)
    yield next(rest)
    kept.wait()
    yield from rest


def swap_blocks(lk, src, dst, to_row):
    z, c, n = lk.z, lk.c, lk.n
    lk.n += 2
    assert lk.n <= lk.send.shape[0]
    first = lk.m
    lk.m += 2
    copies, keeps, selves = [], [], []
    for k in range(2):
        if to_row:
            slot, core, place = z % 2, z // 2, 2 * k + c
        else:
            slot, core, place = z // 2, z % 2, 2 * c + k
        selves.append((place == z) & (core == c))
        copies.append(
            pltpu.make_async_remote_copy(
                src_ref=src(k),
                dst_ref=dst(slot),
                send_sem=lk.send.at[n + k],
                recv_sem=lk.recv.at[n + slot],
                device_id=lk.dev(lk.x, lk.y, core, place),
                device_id_type=MESH,
            )
        )
        keeps.append(pltpu.make_async_copy(src(k), dst(k), lk.local.at[first + k]))
        pl.when(selves[k])(keeps[k].start)
        pl.when(jnp.logical_not(selves[k]))(copies[k].start)
    yield 1
    for k in range(2):
        if to_row:
            own = (z == 2 * c + k) & (c == z % 2)
        else:
            own = (z == 2 * k + c) & (c == z // 2)
        landed = pltpu.make_async_remote_copy(
            src_ref=src(k),
            dst_ref=dst(k),
            send_sem=lk.send.at[n + k],
            recv_sem=lk.recv.at[n + k],
            device_id=lk.near["c", 1],
            device_id_type=MESH,
        )
        pl.when(own)(keeps[k].wait)
        pl.when(jnp.logical_not(own))(landed.wait_recv)
        pl.when(jnp.logical_not(selves[k]))(copies[k].wait_send)


def cots_gather(lk, home, out):
    z, c = lk.z, lk.c
    source, place = c == z // 2, (z + 4 - 2 * c) % 4
    here, there = pl.ds(pl.multiple_of(128 * (z % 2), 128), 128), pl.ds(pl.multiple_of(128 - 128 * (z % 2), 128), 128)
    over, keeps = [], []
    for m in range(2):
        block = home.at[pl.ds(128 * m, 128)]
        over.append(lk.make(block, out.at[2 * m + c, here], lk.nbr("c", 1)))
        keeps.append(pltpu.make_async_copy(block, out.at[2 * m + c, here], lk.local.at[lk.m + m]))
    lk.m += 2
    right, left = lk.sides("z")
    own = out.at[:, here]
    a, b = lk.make(own, own, right), lk.make(own, own, left)
    half = out.at[pl.ds(0, 2), there]
    rest = out.at[pl.ds(2, 2), there]
    e, f = lk.make(half, half, right), lk.make(rest, rest, left)
    from_left = (place == 1) | (place == 2)
    from_right = jnp.logical_not(from_left)

    @pl.when(source)
    def _():
        for copy in keeps:
            copy.start()

    @pl.when(jnp.logical_not(source))
    def _():
        for copy in over:
            copy.start()

    yield 1

    @pl.when(source)
    def _():
        for copy in keeps:
            copy.wait()
        for copy in over:
            copy.wait_recv()
        a.start()
        b.start()

    @pl.when(jnp.logical_not(source))
    def _():
        for copy in over:
            copy.wait_send()

    yield 1

    @pl.when(from_left)
    def _():
        a.wait_recv()
        e.start()

    @pl.when(from_right)
    def _():
        b.wait_recv()
        f.start()

    yield 1

    @pl.when(jnp.logical_not(source))
    def _():
        e.wait_recv()
        f.wait_recv()

    @pl.when(source)
    def _():
        a.wait_send()
        b.wait_send()

    pl.when(from_left)(e.wait_send)
    pl.when(from_right)(f.wait_send)


def add_into(dst, src):
    if len(dst.shape) == 2:
        dst[...] = (dst[...].astype(F32) + src[...].astype(F32)).astype(BF)
    else:
        for i in range(dst.shape[0]):
            dst[i] = (dst[i].astype(F32) + src[i].astype(F32)).astype(BF)


def ring_reduce(lk, p, part, bufs, axis, me):
    right, left = lk.sides(axis)
    r0, r1, ra, rb = bufs
    before, after, far = lk.ring[axis]
    a = lk.put(part(far, 0), r0, right)
    b = lk.put(part(far, 1), r1, left)
    yield 1
    a.wait_recv()
    add_into(part(after, 0), r0)
    c = lk.put(p(after), ra, right)
    b.wait_recv()
    add_into(part(before, 1), r1)
    d = lk.put(p(before), rb, left)
    yield 1
    c.wait_recv()
    add_into(p(me), ra)
    d.wait_recv()
    add_into(p(me), rb)


def plane_reduce(lk, spot, sib_src, sib, bufs, out, first, kept=None):
    x, y, c = lk.x, lk.y, lk.c
    one, two = bufs
    got = lk.put(sib_src, sib, lk.nbr("c", 1))
    yield 1
    if kept is not None:
        kept.wait()
    got.wait_recv()

    def step(i, _):
        ref = spot(i // 4, i % 4)
        ref[...] = (ref[...].astype(F32) + sib[i // 4, i % 4].astype(F32)).astype(BF)
        return 0

    lax.fori_loop(0, 16, step, 0)
    every = slice(None)

    def pair(k):
        return pl.ds(2 * k, 2)

    def rows(ref, k):
        return ref.at[pl.ds(16 * k, 16)]

    if first == "y":
        yield from ring_reduce(lk, lambda j: spot(every, j), lambda j, k: spot(pair(k), j), one, "y", y)
        yield from ring_reduce(lk, lambda i: spot(i, y), lambda i, k: rows(spot(i, y), k), two, "x", x)
    else:
        yield from ring_reduce(lk, lambda i: spot(i, every), lambda i, k: spot(i, pair(k)), one, "x", x)
        yield from ring_reduce(lk, lambda j: spot(x, j), lambda j, k: rows(spot(x, j), k), two, "y", y)
    yield 1
    yield from line_gather(lk, spot(x, y), out, 16)


def ring_scratch(cols):
    return [
        pltpu.VMEM((4, 4, 32, cols), BF),
        pltpu.VMEM((2, 32, cols), BF),
        pltpu.VMEM((2, 32, cols), BF),
        pltpu.VMEM((4, 32, cols), BF),
        pltpu.VMEM((4, 32, cols), BF),
        pltpu.VMEM((16, cols), BF),
        pltpu.VMEM((16, cols), BF),
        pltpu.VMEM((32, cols), BF),
        pltpu.VMEM((32, cols), BF),
    ]


def down_scratch(rows):
    first = (rows // 16 + 1) // 2 * 16
    ring = [(first, 1024), (rows - first, 1024), (rows, 1024), (rows, 1024)]
    return [pltpu.VMEM(dims, BF) for dims in [(4, rows, 1024)] * 2 + ring * 2]


def down_reduce(lk, part_hbm, s, out, lo, rows):
    acc, sib, one, (x0, x1, xa, xb) = s[0], s[1], s[2:6], s[6:10]
    y, c = lk.y, lk.c
    every, cut, down_part = pl.ds(lo, rows), down_cut(lo, rows), down_cut(0, rows)
    kept = lk.keep(part_hbm.at[:, c, every], acc)
    got = lk.put(part_hbm.at[:, lk.other, every], sib, lk.nbr("c", 1))
    yield 1
    kept.wait()
    got.wait_recv()
    add_into(acc, sib)
    yield from ring_reduce(
        lk, lambda j: acc.at[j], lambda j, k: acc.at[j, down_part(k)], one, "y", y
    )
    mine = acc.at[y]
    right, left = lk.sides("x")
    place = lk.past_x
    a = lk.make(acc.at[y, down_part(0)], x0, left)
    b = lk.make(acc.at[y, down_part(1)], x1, right)
    e = lk.make(mine, xa, left)
    f = lk.make(mine, xb, right)

    @pl.when(place == 2)
    def _():
        a.start()
        b.start()

    yield 1

    @pl.when(place == 1)
    def _():
        a.wait_recv()
        add_into(acc.at[y, down_part(0)], x0)
        e.start()

    @pl.when(place == 3)
    def _():
        b.wait_recv()
        add_into(acc.at[y, down_part(1)], x1)
        f.start()

    yield 1

    @pl.when(place == 0)
    def _():
        e.wait_recv()
        add_into(mine, xa)
        f.wait_recv()
        add_into(mine, xb)

    @pl.when(place == 1)
    def _():
        e.wait_send()

    @pl.when(place == 3)
    def _():
        f.wait_send()

    @pl.when(place == 2)
    def _():
        a.wait_send()
        b.wait_send()

    yield from ring_spread(
        lk, mine, out.at[every], lambda k: out.at[cut(k)], "z", lk.past_z
    )


ANY = pl.BlockSpec(memory_space=pl.ANY)


def sems(n):
    return [pltpu.SemaphoreType.DMA((n,)), pltpu.SemaphoreType.DMA((n,)), pltpu.SemaphoreType.DMA((40,))]


def params(number):
    return pltpu.CompilerParams(collective_id=number, has_side_effects=True, vmem_limit_bytes=56 * 2**20)


def shape(*dims, dtype=BF):
    return jax.ShapeDtypeStruct(dims, dtype)


def lanes_of(shape):
    return lax.broadcasted_iota(jnp.int32, shape, len(shape) - 1)


def dot(left, right, dims=((1,), (0,)), kind=F32):
    return lax.dot_general(left, right, (dims, ((), ())), preferred_element_type=F32).astype(kind)


TOKENS = ((0,), (0,))
ROWS = ((1,), (1,))


def flat(value):
    return value.reshape(-1, value.shape[-1])


def head_ones():
    row = lax.broadcasted_iota(jnp.int32, (256, 256), 0) // 64
    col = lax.broadcasted_iota(jnp.int32, (256, 256), 1) // 64
    return jnp.where(row == col, 1.0 / 64, 0.0).astype(BF)


def head_mean(v, ones):
    high = v.astype(BF)
    low = (v - high.astype(F32)).astype(BF)
    return dot(high, ones) + dot(low, ones)


def halves_swapped(v):
    lane = lanes_of(v.shape)
    return jnp.where(lane % 64 < 32, pltpu.roll(v, 96, 1), pltpu.roll(v, 32, 1))


def angle_tables(tab):
    lane = lanes_of(tab.shape)
    other = pltpu.roll(tab, 64, 1)
    return jnp.where(lane < 64, tab, other), jnp.where(lane < 64, other, tab)


def row_scale(v):
    return lax.rsqrt(jnp.mean(v * v, axis=-1, keepdims=True) + EPS)


def gain_rows(whole, gain):
    def step(i, total):
        return total + whole[i // 8, (i // 2) % 4, i % 2, :, pl.ds(2048, 128)].astype(F32)

    total = lax.fori_loop(0, 32, step, jnp.zeros((32, 128), F32))
    for k in range(8):
        gain[0:1, pl.ds(128 * k, 128)] = total[8 + k : 9 + k]
        gain[1:2, pl.ds(128 * k, 128)] = total[16 + k : 17 + k]
        gain[2:3, pl.ds(128 * k, 128)] = total[0:1]
        gain[3:4, pl.ds(128 * k, 128)] = total[1:2]


def keys_values(whole, source, gain, normed, keys, values, lin_key, core):
    ones = head_ones()
    src = source[:, 0:1024].astype(F32)
    normed[...] = (src * row_scale(src) * gain[0:1]).astype(BF)
    cosine, sine = angle_tables(source[:, 1024:1152].astype(F32))
    kn = gain[3:4, 0:128]
    lane = lanes_of((256, 128))
    here = pl.ds(pl.multiple_of(core * 256, 256), 256)

    def put(ref, tile, r):
        turned = pltpu.roll(r, 64, 1)
        ref[2 * tile, here] = jnp.where(lane < 64, r, turned).astype(BF)
        ref[2 * tile + 1, here] = jnp.where(lane < 64, turned, r).astype(BF)

    for j in range(4):
        lin = dot(normed[...], flat(whole[:, :, :, :, pl.ds(1024 + 256 * j, 256)]))
        if j < 2:
            scale = lax.rsqrt(head_mean(lin * lin, ones) + EPS)
            lin_key[:, pl.ds(256 * j, 256)] = lin
            for h in range(2):
                cut = slice(128 * h, 128 * h + 128)
                v = lin[:, cut] * scale[:, cut] * kn
                put(keys, 2 * j + h, v * cosine + halves_swapped(v) * sine)
        else:
            for h in range(2):
                put(values, 2 * (j - 2) + h, lin[:, 128 * h : 128 * h + 128])


def own_queries(whole, source, gain, normed, lin_query, queries):
    ones = head_ones()
    cosine, sine = angle_tables(source[:, 1024:1152].astype(F32))
    qn = gain[2:3, 0:128]
    lane = lanes_of((256, 128))

    def step(j, _):
        lin = dot(normed[...], flat(whole[:, :, :, :, pl.ds(pl.multiple_of(256 * j, 256), 256)]))
        lin_query[:, pl.ds(pl.multiple_of(256 * j, 256), 256)] = lin
        scale = lax.rsqrt(head_mean(lin * lin, ones) + EPS)
        for h in range(2):
            cut = slice(128 * h, 128 * h + 128)
            v = lin[:, cut] * scale[:, cut] * qn
            r = (v * cosine + halves_swapped(v) * sine) * HEAD_SIZE ** (-0.5)
            first = jnp.where(lane < 64, r, 0.0).astype(BF)
            second = jnp.where(lane < 64, 0.0, r).astype(BF)
            for m in range(2):
                queries[m, 2 * j + h, 0:128] = first[128 * m : 128 * m + 128]
                queries[m, 2 * j + h, 128:256] = second[128 * m : 128 * m + 128]
        return 0

    lax.fori_loop(0, 4, step, 0)


def attend(m, queries, keys, values, starts, mask, probs, mixed, core):
    key_pos = lax.broadcasted_iota(jnp.int32, (512, 256), 0)
    query_pos = core * 256 + 128 * m + lax.broadcasted_iota(jnp.int32, (1, 256), 1) % 128
    lane = lanes_of((128, 128))
    row = starts[m, 0:1]
    begin = jnp.concatenate([row, row], axis=1)
    mask[...] = jnp.where((key_pos <= query_pos) & (key_pos.astype(F32) >= begin), 1.0, 0.0)

    def step(k, _):
        scores = dot(keys[k], queries[m, k], ROWS)
        raised = jnp.exp(scores) * mask[...]
        chance = (raised * (1.0 / jnp.sum(raised, axis=0, keepdims=True))).astype(BF)
        probs[8 * m + k] = chance
        got = dot(values[k], chance, TOKENS).T
        both = jnp.where(lane < 64, got[0:128], got[128:256]).astype(BF)
        mixed[128 * m : 128 * m + 128, pl.ds(pl.multiple_of(k * 128, 128), 128)] = both
        return 0

    lax.fori_loop(0, 8, step, 0, unroll=UNROLL)


UNROLL = 4


def out_project(m, whole, source, gain, mixed, middle, normed_ffn, own):
    rows = pl.ds(128 * m, 128)

    def step(j, _):
        cut = pl.ds(pl.multiple_of(256 * j, 256), 256)
        w = flat(whole[:, :, :, :, pl.ds(pl.multiple_of(2176 + 256 * j, 128), 256)])
        middle[rows, cut] = source[rows, cut].astype(F32) + dot(mixed[rows], w)
        return 0

    lax.fori_loop(0, 4, step, 0)
    mid = middle[rows]
    normed_ffn[own, rows] = (mid * row_scale(mid) * gain[1:2]).astype(BF)


def own_gains(params, dp):
    row = jnp.broadcast_to(params, (32, 128))
    line = lax.broadcasted_iota(jnp.int32, (32, 128), 0)
    lane = lanes_of((32, 128))
    spot = dp % 4 * 32
    window = (lane >= spot) & (lane < spot + 32)
    got = jnp.where((line == 8 + dp // 4) & window, pltpu.roll(row, spot, 1), 0.0)
    got = got + jnp.where((line == 16 + dp // 4) & window, pltpu.roll(row, (spot + 96) % 128, 1), 0.0)
    pair = (lane % 64 >= 2 * dp) & (lane % 64 < 2 * dp + 2)
    for k in range(2):
        low = pltpu.roll(row, (2 * dp + 64 - 2 * k) % 128, 1)
        high = pltpu.roll(row, (2 * dp + 128 - 2 * k) % 128, 1)
        got = got + jnp.where((line == k) & pair, jnp.where(lane < 64, low, high), 0.0)
    return got.astype(BF)


def feed_back_in(slots, cots, down, grad_hidden):
    tokens = jnp.concatenate([cots[i] for i in slots], axis=0) if len(slots) > 1 else cots[slots[0]]
    got = dot(tokens, flat(down[...]), ROWS, BF)
    for n, i in enumerate(slots):
        grad_hidden[i] = got[256 * n : 256 * n + 256]


def feed_chunk(slots, ffn, gate_up, down, grad_hidden, hidden, turned, ffn_turned, grad_both, grad_ffn, out_part):
    def load(ref, *cut):
        return jnp.concatenate([ref[(i, *cut)] for i in slots], axis=0) if len(slots) > 1 else ref[(slots[0], *cut)]

    def store(ref, value, *cut):
        for n, i in enumerate(slots):
            ref[(i, *cut)] = value[256 * n : 256 * n + 256]

    every = slice(None)
    size = 256 * len(slots)

    def step(j, _):
        cut = pl.ds(pl.multiple_of(384 * j, 128), 384)
        cut_up = pl.ds(pl.multiple_of(1152 + 384 * j, 128), 384)
        tokens = load(ffn, every, every)
        gated = dot(tokens, flat(gate_up[:, :, :, :, cut]))
        upward = dot(tokens, flat(gate_up[:, :, :, :, cut_up]))
        sigma = 1.0 / (1.0 + jnp.exp(-gated))
        silu = gated * sigma
        made = (silu * upward).astype(BF)
        hidden[0:size, cut] = made
        for n, i in enumerate(slots):
            turned[cut, pl.ds(pl.multiple_of(256 * i, 256), 256)] = made[256 * n : 256 * n + 256].T
        back = load(grad_hidden, every, cut).astype(F32)
        store(grad_both, (back * upward * sigma * (1.0 + gated * (1.0 - sigma))).astype(BF), every, cut)
        store(grad_both, (back * silu).astype(BF), every, cut_up)
        return 0

    lax.fori_loop(0, 3, step, 0)

    def last(j, _):
        cut = pl.ds(pl.multiple_of(256 * j, 256), 256)
        store(grad_ffn, dot(load(grad_both, every, every), flat(gate_up[j]), ROWS, BF), every, cut)
        store(out_part, dot(hidden[0:size], flat(down[:, :, :, cut]), kind=BF), every, cut)
        for i in slots:
            ffn_turned[cut, pl.ds(pl.multiple_of(256 * i, 256), 256)] = ffn[i, :, cut].T
        return 0

    lax.fori_loop(0, 4, last, 0)


def feed_grads(left, right, out, tiles):
    def step(j, _):
        cut = pl.ds(pl.multiple_of(256 * j, 256), 256)
        got = dot(left[...], flat(right[:, :, cut]), kind=BF)
        lead = out.shape[:-1]
        out[(slice(None),) * len(lead) + (cut,)] = got.reshape(*lead, 256)
        return 0

    lax.fori_loop(0, tiles, step, 0)


FWD_SCRATCH = [
    pltpu.VMEM((4, 4, 2, 32, WA), BF),
    pltpu.VMEM((4, 4, 2, 32, GU), BF),
    pltpu.VMEM((4, 2, DN, 1024), BF),
    pltpu.VMEM((256, 1152), BF),
    pltpu.VMEM((256, 128), F32),
    pltpu.VMEM((256, 1152), BF),
    pltpu.VMEM((4, 256, 1024), BF),
    pltpu.VMEM((4, 256, 1024), BF),
    pltpu.VMEM((256, 1024), BF),
    pltpu.VMEM((256, 1024), F32),
    pltpu.VMEM((256, 512), F32),
    pltpu.VMEM((8, 512, 128), BF),
    pltpu.VMEM((8, 512, 128), BF),
    pltpu.VMEM((2, 8, 256, 128), BF),
    pltpu.VMEM((16, 512, 256), BF),
    pltpu.VMEM((256, 1024), BF),
    pltpu.VMEM((256, 1024), F32),
    pltpu.VMEM((8, 1024), F32),
    pltpu.VMEM((4, 256, 1152), BF),
    pltpu.VMEM((512, 1152), BF),
    pltpu.VMEM((1152, 1024), BF),
    pltpu.VMEM((1024, 1024), BF),
    pltpu.VMEM((4, 256, GU), BF),
    pltpu.VMEM((4, 256, 1024), BF),
    pltpu.VMEM((4, 256, 1024), BF),
    pltpu.VMEM((256, 1024), BF),
    pltpu.VMEM((256, 1024), BF),
    pltpu.VMEM((4, 64, 1024), BF),
    pltpu.VMEM((2, 8, 128), F32),
    pltpu.VMEM((32, WA), BF),
    pltpu.VMEM((32, GU), BF),
    pltpu.VMEM((1, 128), F32),
    pltpu.VMEM((512, 256), F32),
]

FWD_OUT = (
    shape(4, 4, 2, 32, WA),
    shape(256, 1024),
    shape(256, 1024, dtype=F32),
    shape(256, 512, dtype=F32),
    shape(8, 512, 128),
    shape(8, 512, 128),
    shape(2, 8, 256, 128),
    shape(16, 512, 256),
    shape(256, 1024),
    shape(256, 1024, dtype=F32),
    shape(8, 1024, dtype=F32),
    shape(4, 4, 2, 32, GU),
    shape(4, 2, DN, 1024),
    shape(4, 256, 1024),
    shape(256, 1024, dtype=F32),
    shape(256, 1152),
    shape(256, 1024),
)


FWD_IN = 12


def go(*steps):
    for s in steps:
        next(s, None)


def fwd_kernel(*refs):
    w_query, key_weight, value_weight, w_out, w_gate, w_up, dn, x, cot, tab, starts_hbm, params_hbm = refs[:FWD_IN]
    refs = refs[FWD_IN:]
    outs, refs = refs[: len(FWD_OUT)], refs[len(FWD_OUT) :]
    lk = Links(*refs[:3])
    (
        whole, gate_up, down, source, table, at_home, cots, ffn, normed, lin_query, lin_key, keys, values, queries,
        probs, mixed, middle, gain, grad_hidden, hidden, turned, ffn_turned, grad_both, grad_ffn, out_part,
        from_right, from_left, passing, starts, wa, gu, own_params, mask,
    ) = refs[3:]
    own = lk.z
    before, after, far = lk.ring["z"]
    quarter = pl.ds(pl.multiple_of(own * 1152, 128), 1152)
    staged = [
        lk.keep(params_hbm, own_params),
        lk.keep(tab, table),
        lk.keep(x, at_home.at[:, pl.ds(0, 1024)]),
        lk.keep(w_query, wa.at[:, pl.ds(0, 1024)]),
        lk.keep(key_weight, wa.at[:, pl.ds(1024, 512)]),
        lk.keep(value_weight, wa.at[:, pl.ds(1536, 512)]),
        lk.keep(w_out, wa.at[:, pl.ds(2176, 1024)]),
        lk.keep(w_gate.at[:, quarter], gu.at[:, pl.ds(0, 1152)]),
        lk.keep(w_up.at[:, quarter], gu.at[:, pl.ds(1152, 1152)]),
    ]
    staged[0].wait()
    staged[1].wait()
    at_home[:, 1024:1152] = table[...].astype(BF)
    wa[:, 2048:2176] = own_gains(own_params[...], lax.axis_index("dp"))
    for copy in staged[2:]:
        copy.wait()
    lk.barrier()
    k1 = plane_gather(lk, wa, whole, "x", 1024, 1536)
    k2 = plane_gather(lk, wa, whole, "y", 1536, 2176)
    a1 = plane_gather(lk, wa, whole, "x", 0, 1024)
    a2 = plane_gather(lk, wa, whole, "y", 2176, WA)
    half = [pl.ds(0, 128), pl.ds(128, 128)]

    def slot(j):
        return pl.ds(128 * j, 128) if isinstance(j, int) else pl.ds(pl.multiple_of(128 * j, 128), 128)

    x1 = swap_blocks(lk, lambda m: at_home.at[half[m]], lambda j: source.at[slot(j)], True)
    s1 = swap_blocks(lk, lambda m: starts_hbm.at[m], lambda j: starts.at[j], True)
    g1 = plane_gather(lk, gu, gate_up, "x", 0, 1152)
    g2 = plane_gather(lk, gu, gate_up, "y", 1152, GU)
    d1, d2 = down_gather(lk, dn, down, 0, 80), down_gather(lk, dn, down, 80, 64)
    c1 = cots_gather(lk, cot, cots)
    go(x1, s1, c1)
    go(k1, k2)
    go(a1, a2)
    go(k1, k2)
    go(a1, a2)
    go(k1, k2)
    go(a1, a2)
    go(x1, s1)
    go(c1)
    go(k1, k2)
    go(g1, g2)
    go(k1, k2)
    go(a1, a2)
    go(d1, d2)
    drive(k1, k2, x1, s1)
    gain_rows(whole, gain)
    keys_values(whole, source, gain, normed, keys, values, lin_key, lk.c)
    mine = pl.ds(pl.multiple_of(lk.c * 256, 256), 256)
    crossed = [lk.put(ref.at[:, mine], ref.at[:, mine], lk.nbr("c", 1)) for ref in (keys, values)]
    go(g1, g2)
    drive(a1, a2)
    go(g1, g2)
    own_queries(whole, source, gain, normed, lin_query, queries)
    go(d1, d2)
    go(c1)
    for copy in crossed:
        copy.wait_recv()
    saved = [lk.keep(source, outs[15])]
    for k, ref in enumerate((normed, lin_query, lin_key, keys, values, queries)):
        saved.append(lk.keep(ref, outs[1 + k]))
    passed = []
    for m in range(2):
        attend(m, queries, keys, values, starts, mask, probs, mixed, lk.c)
        go(g1, g2)
        if m == 0:
            go(d1, d2)
            saved.append(lk.keep(whole, outs[0]))
        out_project(m, whole, source, gain, mixed, middle, ffn, own)
        rows = pl.ds(128 * m, 128)

        def part(i, k, m=m):
            return ffn.at[i, pl.ds(128 * m + 64 * k, 64)]

        passed.append(
            ring_gather(lk, ffn.at[own, rows], lambda i, rows=rows: ffn.at[i, rows], part, "z", own)
        )
        go(passed[m])
        if m == 0:
            go(c1)
    go(passed[0])
    go(d1, d2)
    drive(c1)
    saved.append(lk.keep(cots.at[own], outs[16]))
    for k, ref in enumerate((probs, mixed, middle, gain)):
        saved.append(lk.keep(ref, outs[7 + k]))
    drive(g1, g2, d1, d2)
    feed_back_in((own,), cots, down, grad_hidden)

    def chunk(*slots):
        feed_chunk(
            slots, ffn, gate_up, down, grad_hidden, hidden, turned, ffn_turned, grad_both, grad_ffn, out_part
        )

    right, left = lk.sides("z")
    chunk(own)
    go(passed[1])
    feed_back_in((before, after), cots, down, grad_hidden)
    chunk(before, after)
    low, high = pl.ds(0, 128), pl.ds(128, 128)
    sent = [
        lk.put(grad_ffn.at[after, high], from_left.at[high], right),
        lk.put(grad_ffn.at[before, low], from_right.at[low], left),
    ]
    feed_back_in((far,), cots, down, grad_hidden)
    drive(*passed)
    chunk(far)
    lk.flush()
    saved.append(lk.keep(out_part, outs[13]))
    hops = []
    for k in range(2):
        rows = pl.ds(64 * k, 64)
        hops.append((lk.put(grad_ffn.at[far, rows], passing.at[k], right), after, rows, from_left, right))
    for k in range(2):
        rows = pl.ds(128 + 64 * k, 64)
        hops.append((lk.put(grad_ffn.at[far, rows], passing.at[2 + k], left), before, rows, from_right, left))

    def hop(k):
        copy, slot, rows, landing, to = hops[k]
        copy.wait_recv()
        add_into(grad_ffn.at[slot, rows], passing.at[k])
        sent.append(lk.put(grad_ffn.at[slot, rows], landing.at[rows], to))

    feed_grads(turned, cots, down, 4)
    saved.append(lk.keep(down, outs[12]))
    hop(0)
    hop(2)
    feed_grads(ffn_turned, grad_both, gate_up, 9)
    hop(1)
    hop(3)
    saved.append(lk.keep(gate_up, outs[11]))
    for copy in sent:
        copy.wait_recv()
    for copy in saved:
        copy.wait()
    total = grad_ffn[own].astype(F32) + from_right[...].astype(F32) + from_left[...].astype(F32)
    lin_query[...] = total
    lk.keep(lin_query, outs[14]).wait()
    lk.flush()


def forward(*args):
    return pl.pallas_call(
        fwd_kernel,
        out_shape=FWD_OUT,
        in_specs=[ANY] * FWD_IN,
        out_specs=[ANY] * len(FWD_OUT),
        scratch_shapes=sems(160) + FWD_SCRATCH,
        compiler_params=pltpu.CompilerParams(
            collective_id=0, has_side_effects=True, vmem_limit_bytes=60 * 2**20
        ),
    )(*args)


BWD_IN = 17
PIECES = (1152, 1152, 512, 512, 512, 512, 512, 512, 128)
BWD_OUT = (
    shape(2, 128, 1024),
    shape(2, 128, 1024),
    shape(4, 32, WA),
    shape(4, 32, GU),
    shape(DN, 1024),
)
BWD_SCRATCH = [
    pltpu.VMEM((4, 4, 2, 32, WA), BF),
    pltpu.VMEM((256, 1024), BF),
    pltpu.VMEM((256, 1024), F32),
    pltpu.VMEM((256, 512), F32),
    pltpu.VMEM((8, 512, 128), BF),
    pltpu.VMEM((8, 512, 128), BF),
    pltpu.VMEM((2, 8, 256, 128), BF),
    pltpu.VMEM((16, 512, 256), BF),
    pltpu.VMEM((256, 1024), BF),
    pltpu.VMEM((256, 1024), F32),
    pltpu.VMEM((8, 1024), F32),
    pltpu.VMEM((4, 256, 1024), BF),
    pltpu.VMEM((256, 1024), F32),
    pltpu.VMEM((256, 1024), BF),
    pltpu.VMEM((256, 1152), BF),
]
BWD_WORK = [
    pltpu.VMEM((256, 1024), BF),
    pltpu.VMEM((2, 8, 256, 128), BF),
    pltpu.VMEM((256, 1024), F32),
    pltpu.VMEM((2, 256, 1024), BF),
    pltpu.VMEM((256, 2048), BF),
    pltpu.VMEM((1024, 256), BF),
    pltpu.VMEM((256, 1024), F32),
    pltpu.VMEM((8, 1024), F32),
    pltpu.VMEM((4, 4, 2, 32, WA), BF),
    pltpu.VMEM((4, 4, 32, 1152), BF),
    pltpu.VMEM((4, 4, 32, 1152), BF),
    pltpu.VMEM((256, 1024), BF),
    pltpu.VMEM((256, 1024), BF),
    pltpu.VMEM((256, 1024), BF),
]
Z_RING = [
    pltpu.VMEM((128, 1024), BF),
    pltpu.VMEM((128, 1024), BF),
    pltpu.VMEM((256, 1024), BF),
    pltpu.VMEM((256, 1024), BF),
]


def norm_back(v, g, dy):
    r = row_scale(v)
    gdy = g * dy
    back = r * gdy - v * (r * r * r * jnp.mean(v * gdy, axis=-1, keepdims=True))
    return back, jnp.sum(v * r * dy, axis=0, keepdims=True)


def heads_back(lin, grad, gain, cosine, sine, ones):
    parts = []
    for h in range(2):
        part = grad[:, 128 * h : 128 * h + 128]
        parts.append(part * cosine + halves_swapped(part * sine))
    dy = jnp.concatenate(parts, axis=1)
    r = lax.rsqrt(head_mean(lin * lin, ones) + EPS)
    gdy = dy * gain
    back = r * gdy - lin * (r * r * r * head_mean(lin * gdy, ones))
    return back, jnp.sum(lin * r * dy, axis=0, keepdims=True)


def turned_grads(turned, right, out, start, tiles, base=0):
    def step(j, _):
        got = dot(turned[...], right[:, pl.ds(pl.multiple_of(base + 256 * j, 256), 256)], kind=BF)
        out[:, :, :, :, pl.ds(pl.multiple_of(start + 256 * j, 128), 256)] = got.reshape(4, 4, 2, 32, 256)
        return 0

    lax.fori_loop(0, tiles, step, 0)


def attend_back(half, queries, keys, values, probs, grad_mixed, grad_queries, grad_kv):
    lane = lanes_of((128, 128))
    lane_keys = lanes_of((512, 128))

    def step(j, _):
        folded = []
        for e in range(2):
            k = 2 * j + e
            cut = pl.ds(pl.multiple_of(128 * k, 128), 128)
            key_sum = value_sum = None
            for m in range(2):
                chance = probs[8 * m + k]
                back = dot(values[k], grad_mixed[m, k], ROWS)
                p = chance.astype(F32)
                p_back = p * back
                grad_scores = (p_back - p * jnp.sum(p_back, axis=0, keepdims=True)).astype(BF)
                got = dot(keys[k], grad_scores, TOKENS).T
                grad_queries[128 * m : 128 * m + 128, cut] = jnp.where(lane < 64, got[0:128], got[128:256])
                more_keys, more_values = dot(grad_scores, queries[m, k]), dot(chance, grad_mixed[m, k])
                key_sum = more_keys if m == 0 else key_sum + more_keys
                value_sum = more_values if m == 0 else value_sum + more_values
            folded += [v + pltpu.roll(v, 64, 1) for v in (key_sum, value_sum)]
        for s in range(2):
            tile = jnp.where(lane_keys < 64, folded[s], folded[2 + s]).astype(BF)
            cut = pl.ds(pl.multiple_of(512 * s + 128 * j, 128), 128)
            grad_kv[0, :, cut] = tile[0:256]
            grad_kv[1, :, cut] = tile[256:512]
        return 0

    lax.fori_loop(2 * half, 2 * half + 2, step, 0)


def bwd_kernel(*refs):
    ins, refs = refs[:BWD_IN], refs[BWD_IN:]
    outs, refs = refs[: len(BWD_OUT)], refs[len(BWD_OUT) :]
    lk = Links(*refs[:3])
    refs = refs[3:]
    n = len(BWD_SCRATCH)
    held, refs = refs[:n], refs[n:]
    (
        whole, normed, lin_query, lin_key, keys, values, queries, probs, mixed, middle, gain, out_part, grad_middle,
        upstream, source,
    ) = held
    grad_gu, grad_down = ins[15:]
    n = len(BWD_WORK)
    work, refs = refs[:n], refs[n:]
    (
        grad_branch, grad_mixed, grad_queries, grad_kv, grad_lin, turned, grad_normed, gains_back, grad_whole, acc_a,
        acc_b, made, sent_back, kv_other,
    ) = work
    z_out, refs = refs[:4], refs[4:]
    down_refs, refs = refs[:20], refs[20:]
    rings = [refs[9 * i : 9 * i + 9] for i in range(len(PIECES))]
    outputs, grad_inputs, a_all, gu_all, down_own = outs
    own, c = lk.z, lk.c

    order = [11, 12, 9, 13, 10, 0, 8, 5, 7, 6, 4, 2, 14, 1, 3]
    loads = {}
    for k in order[:7]:
        loads[k] = lk.keep(ins[k], held[k])
    lk.barrier()

    def piece(k, spot, src, out, first, kept=None):
        ring = rings[k]
        return plane_reduce(lk, spot, src, ring[0], (ring[1:5], ring[5:9]), out, first, kept)

    def feed_piece(k, acc, lo, first):
        cols = pl.ds(lo, 1152)
        kept = lk.keep(grad_gu.at[:, :, c, :, cols], acc)
        return piece(
            k, lambda i, j: acc.at[i, j], grad_gu.at[:, :, lk.other, :, cols], gu_all.at[:, :, cols], first, kept
        )

    def whole_piece(k, lo, first):
        cols = pl.ds(lo, PIECES[k])
        return piece(
            k, lambda i, j: grad_whole.at[i, j, c, :, cols], grad_whole.at[:, :, lk.other, :, cols],
            a_all.at[:, :, cols], first,
        )

    def out_chain():
        yield from ring_reduce(
            lk, lambda i: out_part.at[i], lambda i, k: out_part.at[i, pl.ds(128 * k, 128)], z_out, "z", own
        )
        made[...] = (middle[...] + out_part[own].astype(F32)).astype(BF)
        yield from swap_blocks(
            lk, lambda j: made.at[pl.ds(128 * j, 128)], lambda m: outputs.at[m], False
        )

    def need(*names):
        for k in names:
            loads.pop(k).wait()

    f1, f2 = feed_piece(0, acc_a, 0, "y"), feed_piece(1, acc_b, 1152, "x")
    d1 = down_reduce(lk, grad_down, down_refs[:10], down_own, 0, 80)
    d2 = down_reduce(lk, grad_down, down_refs[10:], down_own, 80, 64)
    go(d1, d2, f1, f2)
    o1 = out_chain()
    need(11)
    go(o1)
    for k in order[7:]:
        loads[k] = lk.keep(ins[k], held[k])
    need(12, 9, 13, 10)
    back, row = norm_back(middle[...], gain[1:2], grad_middle[...])
    total = upstream[...].astype(F32) + back
    grad_middle[...] = total
    grad_branch[...] = total.astype(BF)
    gains_back[1:2] = row
    need(0, 8)
    go(d1, d2)
    lane = lanes_of((256, 128))

    def back_mixed(j, _):
        got = dot(grad_branch[...], flat(whole[j, :, :, :, pl.ds(2176, 1024)]), ROWS)
        for h in range(2):
            r = got[:, 128 * h : 128 * h + 128]
            first = jnp.where(lane < 64, r, 0.0).astype(BF)
            second = jnp.where(lane < 64, 0.0, r).astype(BF)
            for m in range(2):
                grad_mixed[m, 2 * j + h, 0:128] = first[128 * m : 128 * m + 128]
                grad_mixed[m, 2 * j + h, 128:256] = second[128 * m : 128 * m + 128]
        return 0

    lax.fori_loop(0, 4, back_mixed, 0)
    go(f2, f1)
    need(5, 7, 6, 4)
    attend_back(0, queries, keys, values, probs, grad_mixed, grad_queries, grad_kv)
    go(d1, d2)
    go(f2, f1)
    go(o1)
    attend_back(1, queries, keys, values, probs, grad_mixed, grad_queries, grad_kv)
    crossed = lk.put(grad_kv.at[lk.other], kv_other, lk.nbr("c", 1))
    turned[...] = mixed[...].T
    turned_grads(turned, grad_branch, grad_whole, 2176, 4)
    p2, p3 = whole_piece(2, 2176, "y"), whole_piece(3, 2688, "x")
    go(p2, p3)
    go(d1, d2)
    go(f2)
    need(2, 14, 1)
    ones = head_ones()
    cosine, sine = angle_tables(source[:, 1024:1152].astype(F32))

    def back_query(j, _):
        cut = pl.ds(pl.multiple_of(256 * j, 256), 256)
        grad = grad_queries[:, cut] * HEAD_SIZE ** (-0.5)
        got, line = heads_back(lin_query[:, cut], grad, gain[2:3, 0:256], cosine, sine, ones)
        grad_lin[:, cut] = got.astype(BF)
        gains_back[2:3, cut] = line
        return 0

    lax.fori_loop(0, 4, back_query, 0)
    turned[...] = normed[...].T
    need(3)
    crossed.wait_recv()

    def back_key(j, _):
        cut = pl.ds(pl.multiple_of(256 * j, 256), 256)
        grad = grad_kv[c, :, cut].astype(F32) + kv_other[:, cut].astype(F32)
        got, line = heads_back(lin_key[:, cut], grad, gain[3:4, 0:256], cosine, sine, ones)
        grad_lin[:, pl.ds(pl.multiple_of(1024 + 256 * j, 256), 256)] = got.astype(BF)
        gains_back[3:4, cut] = line
        return 0

    lax.fori_loop(0, 2, back_key, 0)
    value_sum = grad_kv[c, :, 512:1024].astype(F32) + kv_other[:, 512:1024].astype(F32)
    grad_lin[:, 1536:2048] = value_sum.astype(BF)

    turned_grads(turned, grad_lin, grad_whole, 1024, 4, 1024)
    p6, p7 = whole_piece(6, 1024, "y"), whole_piece(7, 1536, "x")
    go(p6, p7)
    go(d1, d2)
    go(f1, f2)
    go(p2, p3)
    turned_grads(turned, grad_lin, grad_whole, 0, 4)
    go(o1)
    p4, p5 = whole_piece(4, 0, "y"), whole_piece(5, 512, "x")
    go(p4, p5)
    go(p6, p7)
    go(d1, d2)

    def back_normed(j, _):
        grad_normed[:, pl.ds(pl.multiple_of(256 * j, 256), 256)] = dot(
            grad_lin[...], flat(whole[j, :, :, :, pl.ds(0, 2048)]), ROWS
        )
        return 0

    lax.fori_loop(0, 4, back_normed, 0)
    go(p2, p3)
    go(p6, p7)
    go(p4, p5)
    go(f2, f1)
    go(d1, d2)
    back, row = norm_back(source[:, 0:1024].astype(F32), gain[0:1], grad_normed[...])
    gains_back[0:1] = row
    sent_back[...] = (grad_middle[...] + back).astype(BF)
    i1 = swap_blocks(lk, lambda j: sent_back.at[pl.ds(128 * j, 128)], lambda m: grad_inputs.at[m], False)
    go(i1)
    small = [jnp.zeros((1, 128), F32)] * 2
    for s, tiles in ((0, 8), (1, 4)):
        for k in range(tiles):
            small[s] = small[s] + gains_back[2 + s : 3 + s, 128 * k : 128 * k + 128]
        small[s] = small[s] + pltpu.roll(jnp.broadcast_to(small[s], (8, 128)), 64, 1)[0:1]
    heads = jnp.where(lanes_of((1, 128)) < 64, small[0], small[1])
    line = lax.broadcasted_iota(jnp.int32, (32, 128), 0)
    for k in range(8):
        cut = slice(128 * k, 128 * k + 128)
        block = jnp.where(line == 8, gains_back[0:1, cut], 0.0)
        block = jnp.where(line == 16, gains_back[1:2, cut], block)
        block = jnp.where(line == 0, heads, block).astype(BF)
        for d in range(4 * k, 4 * k + 4):
            grad_whole[d // 8, (d // 2) % 4, d % 2, :, 2048:2176] = block
    p8 = whole_piece(8, 2048, "y")
    go(p8)
    go(p2, p3)
    go(p6, p7)
    go(p4, p5)
    go(p8)
    go(d1, d2)
    go(p2, p3)
    go(p6, p7)
    go(p4, p5)
    go(p8)
    go(f2, f1)
    go(p2, p3)
    go(p6, p7)
    go(p4, p5)
    go(p8)
    go(d1, d2)
    go(o1)
    go(p2, p3)
    go(p6, p7)
    go(p4, p5)
    go(p8)
    go(i1)
    go(f2, f1)
    go(d1, d2)
    drive(p6, p7, p4, p5, p8, p2, p3, f1, f2, d1, d2, o1, i1)
    lk.flush()


def backward(*args):
    return pl.pallas_call(
        bwd_kernel,
        out_shape=BWD_OUT,
        in_specs=[ANY] * BWD_IN,
        out_specs=[ANY] * len(BWD_OUT),
        scratch_shapes=sems(180) + BWD_SCRATCH + BWD_WORK + Z_RING + down_scratch(80) + down_scratch(64)
        + [v for cols in PIECES for v in ring_scratch(cols)],
        compiler_params=pltpu.CompilerParams(
            collective_id=1, has_side_effects=True, vmem_limit_bytes=62 * 2**20
        ),
    )(*args)


def finish_kernel(*refs):
    ins, outs, held, local = refs[:5], refs[5:15], refs[15:19], refs[19]
    o_out, o_in, o_query, o_key, o_value, o_wout, o_gate, o_up, o_down, o_gains = outs
    a_all, gu_all, down, grad_in = held
    pairs = [(ins[2], a_all), (ins[3], gu_all), (ins[4], down), (ins[0], o_out), (ins[1], grad_in)]
    copies = [pltpu.make_async_copy(src, dst, local.at[k]) for k, (src, dst) in enumerate(pairs)]
    for copy in copies:
        copy.start()
    copies[0].wait()
    for ref, lo, size in (
        (o_query, 0, 1024), (o_key, 1024, 512), (o_value, 1536, 512), (o_gains, 2048, 128), (o_wout, 2176, 1024),
    ):
        total = a_all[0, :, lo : lo + size].astype(F32)
        for i in range(1, 4):
            total = total + a_all[i, :, lo : lo + size].astype(F32)
        ref[...] = total
    copies[1].wait()
    for i in range(4):
        o_gate[:, 1152 * i : 1152 * i + 1152] = gu_all[i, :, 0:1152].astype(F32)
        o_up[:, 1152 * i : 1152 * i + 1152] = gu_all[i, :, 1152:2304].astype(F32)
    copies[2].wait()
    o_down[...] = down[...].astype(F32)
    copies[4].wait()
    o_in[...] = grad_in[...].astype(F32)
    copies[3].wait()


def finish(*args):
    vmem = pl.BlockSpec(memory_space=pltpu.VMEM)
    return pl.pallas_call(
        finish_kernel,
        out_shape=(
            shape(2, 128, 1024), shape(2, 128, 1024, dtype=F32), shape(32, 1024, dtype=F32), shape(32, 512, dtype=F32),
            shape(32, 512, dtype=F32), shape(32, 1024, dtype=F32), shape(32, 4608, dtype=F32),
            shape(32, 4608, dtype=F32), shape(DN, 1024, dtype=F32), shape(32, 128, dtype=F32),
        ),
        in_specs=[ANY] * 5,
        out_specs=[vmem] * 10,
        scratch_shapes=[
            pltpu.VMEM((4, 32, WA), BF), pltpu.VMEM((4, 32, GU), BF), pltpu.VMEM((DN, 1024), BF),
            pltpu.VMEM((2, 128, 1024), BF), pltpu.SemaphoreType.DMA((5,)),
        ],
        compiler_params=pltpu.CompilerParams(vmem_limit_bytes=60 * 2**20),
    )(*args)


def body(
    inputs, starts, w_query, key_weight, value_weight, w_out, w_gate, w_up, w_down,
    prenorm, midnorm, querynorm, keynorm, cotangent,
):
    z = lax.axis_index("seq")
    dp = lax.axis_index("dp")
    params = jnp.concatenate([prenorm, midnorm, querynorm, keynorm, jnp.zeros((60,), BF)])
    params = params.astype(F32).reshape(1, 128)
    pos = z * 128 + jnp.arange(128, dtype=jnp.int32)
    inside = pos - starts[:, 0]
    frequency = ROPE_BASE ** (-(jnp.arange(32, dtype=F32) * 2.0 / 64))
    angle = inside.reshape(256, 1).astype(F32) * frequency[None, :]
    cosine, sine = jnp.cos(angle), jnp.sin(angle)
    tab = jnp.concatenate([cosine, cosine, -sine, sine], axis=1)
    begin = jnp.broadcast_to(starts.astype(F32), (2, 8, 128))
    source = inputs.reshape(256, 1024)
    upstream = cotangent.reshape(256, 1024)
    (
        whole, normed, lin_query, lin_key, keys, values, queries, probs, mixed, middle, gain, grad_gu, grad_down,
        out_part, grad_ffn, row_source, row_upstream,
    ) = forward(
        w_query, key_weight, value_weight, w_out, w_gate, w_up, w_down, source, upstream, tab, begin, params
    )
    done = backward(
        whole, normed, lin_query, lin_key, keys, values, queries, probs, mixed, middle, gain, out_part, grad_ffn,
        row_upstream, row_source, grad_gu, grad_down,
    )
    outputs, grad_inputs, d_query, d_key, d_value, d_out, d_gate, d_up, d_down, d_gains = finish(*done)
    both = dp % 4 * 32
    return (
        outputs.reshape(2, 1, 128, 1024),
        grad_inputs.reshape(2, 1, 128, 1024),
        d_query,
        d_key,
        d_value,
        d_out,
        d_gate,
        d_up,
        d_down,
        lax.dynamic_slice(d_gains, (8, both), (1, 32))[0],
        lax.dynamic_slice(d_gains, (16, both), (1, 32))[0],
        lax.dynamic_slice(d_gains, (0, 2 * dp), (1, 2))[0],
        lax.dynamic_slice(d_gains, (0, 64 + 2 * dp), (1, 2))[0],
    )


def solution(mesh):
    tokens, matrix, vector = P(None, "dp", "seq", None), P("dp", None), P("dp")
    return jax.shard_map(
        body,
        mesh=mesh,
        in_specs=(tokens, P(None, "dp", "seq")) + (matrix,) * 7 + (vector,) * 4 + (tokens,),
        out_specs=(tokens, tokens) + (matrix,) * 7 + (vector,) * 4,
        check_vma=False,
    )
```

```python
from functools import partial

import jax
import jax.numpy as jnp
from jax import lax
from jax.experimental import pallas as pl
from jax.experimental.pallas import tpu as pltpu
from jax.sharding import PartitionSpec as P

QUERY_HEADS = 16
KEY_VALUE_HEADS = 8
HEAD_SIZE = 64
EPS = 1e-05
ROPE_BASE = 1000000.0

MESH = pl.DeviceIdType.MESH
BF = jnp.bfloat16
F32 = jnp.float32
WA = 3200
GU = 2304
DN = 144


class Links:
    def __init__(self, send, recv, local):
        dp = lax.axis_index("dp")
        self.z = lax.axis_index("seq")
        self.x, self.y, self.c = dp // 8, (dp // 2) % 4, dp % 2
        self.send, self.recv, self.local = send, recv, local
        self.n = self.m = 0
        self.out = []
        self.other = 1 - self.c
        place = {"x": self.x, "y": self.y, "z": self.z}
        self.ring = {k: ((v + 3) % 4, (v + 1) % 4, (v + 2) % 4) for k, v in place.items()}
        self.past_x = (self.x - self.z + 4) % 4
        self.past_z = (self.z - self.x + 4) % 4
        self.near = {("c", 1): self.dev(self.x, self.y, self.other, self.z)}
        for k, (before, after, far) in self.ring.items():
            for step, v in ((-1, before), (1, after)):
                spot = dict(place, **{k: v})
                self.near[k, step] = self.dev(spot["x"], spot["y"], self.c, spot["z"])

    def dev(self, x, y, c, z):
        return ((x * 4 + y) * 2 + c, z)

    def nbr(self, axis, step):
        return self.near[axis, step]

    def sides(self, axis):
        return self.nbr(axis, 1), self.nbr(axis, -1)

    def barrier(self):
        sem = pltpu.get_barrier_semaphore()
        targets = [self.nbr(axis, step) for axis in "xy" for step in (1, -1)]
        for k in range(1, 8):
            spot = (self.z * 2 + self.c + k) % 8
            targets.append(self.dev(self.x, self.y, spot % 2, spot // 2))
        for device in targets:
            pl.semaphore_signal(sem, inc=1, device_id=device, device_id_type=MESH)
        pl.semaphore_wait(sem, len(targets))

    def make(self, src, dst, to):
        copy = pltpu.make_async_remote_copy(
            src_ref=src,
            dst_ref=dst,
            send_sem=self.send.at[self.n],
            recv_sem=self.recv.at[self.n],
            device_id=to,
            device_id_type=MESH,
        )
        self.n += 1
        assert self.n <= self.send.shape[0]
        return copy

    def put(self, src, dst, to):
        copy = self.make(src, dst, to)
        copy.start()
        self.out.append(copy)
        return copy

    def keep(self, src, dst):
        copy = pltpu.make_async_copy(src, dst, self.local.at[self.m])
        self.m += 1
        assert self.m <= self.local.shape[0]
        copy.start()
        return copy

    def flush(self):
        for copy in self.out:
            copy.wait_send()
        self.out = []


def drive(*steps):
    steps = list(steps)
    while steps:
        steps = [s for s in steps if next(s, "end") != "end"]


def ring_gather(lk, own, slot, part, axis, me, ready=None):
    right, left = lk.sides(axis)
    before, after, far = lk.ring[axis]
    a = lk.put(own, slot(me), right)
    b = lk.put(own, slot(me), left)
    yield 1
    a.wait_recv()
    c = lk.put(part(before, 0), part(before, 0), right)
    if ready:
        ready(before)
    b.wait_recv()
    d = lk.put(part(after, 1), part(after, 1), left)
    if ready:
        ready(after)
    yield 1
    c.wait_recv()
    d.wait_recv()
    if ready:
        ready(far)


def plane_gather(lk, own, out, first, lo, hi):
    cols = pl.ds(lo, hi - lo)
    x, y, c = lk.x, lk.y, lk.c
    kept = lk.keep(own.at[:, cols], out.at[x, y, c, :, cols])
    crossing = []

    def cross(ref):
        crossing.append(lk.put(ref, ref, lk.nbr("c", 1)))

    def rows(k):
        return pl.ds(16 * k, 16)

    def two(k):
        return pl.ds(2 * k, 2)

    if first == "x":
        yield from ring_gather(
            lk, own.at[:, cols], lambda i: out.at[i, y, c, :, cols],
            lambda i, k: out.at[i, y, c, rows(k), cols], "x", x,
        )
        kept.wait()
        whole = out.at[:, y, c, :, cols]
        cross(whole)
        yield from ring_gather(
            lk, whole, lambda j: out.at[:, j, c, :, cols],
            lambda j, k: out.at[two(k), j, c, :, cols], "y", y,
            lambda j: cross(out.at[:, j, c, :, cols]),
        )
    else:
        yield from ring_gather(
            lk, own.at[:, cols], lambda j: out.at[x, j, c, :, cols],
            lambda j, k: out.at[x, j, c, rows(k), cols], "y", y,
        )
        kept.wait()
        whole = out.at[x, :, c, :, cols]
        cross(whole)
        yield from ring_gather(
            lk, whole, lambda i: out.at[i, :, c, :, cols],
            lambda i, k: out.at[i, two(k), c, :, cols], "x", x,
            lambda i: cross(out.at[i, :, c, :, cols]),
        )
    yield 1
    for copy in crossing:
        copy.wait_recv()


def ring_spread(lk, own, dst, part, axis, place):
    right, left = lk.sides(axis)
    a, b = lk.make(own, dst, right), lk.make(own, dst, left)
    c, d = lk.make(part(0), part(0), right), lk.make(part(1), part(1), left)
    kept = pltpu.make_async_copy(own, dst, lk.local.at[lk.m])
    lk.m += 1

    @pl.when(place == 0)
    def _():
        a.start()
        b.start()
        kept.start()

    yield 1

    @pl.when(place == 1)
    def _():
        a.wait_recv()
        c.start()

    @pl.when(place == 3)
    def _():
        b.wait_recv()
        d.start()

    yield 1

    @pl.when(place == 2)
    def _():
        c.wait_recv()
        d.wait_recv()

    @pl.when(place == 0)
    def _():
        kept.wait()
        a.wait_send()
        b.wait_send()

    @pl.when(place == 1)
    def _():
        c.wait_send()

    @pl.when(place == 3)
    def _():
        d.wait_send()


def down_cut(lo, rows):
    first = (rows // 16 + 1) // 2 * 16
    return lambda k: pl.ds(lo, first) if k == 0 else pl.ds(lo + first, rows - first)


def down_gather(lk, own, out, lo, rows):
    y, c = lk.y, lk.c
    every, cut = pl.ds(lo, rows), down_cut(lo, rows)
    yield from ring_spread(
        lk, own.at[every], out.at[y, c, every], lambda k: out.at[y, c, cut(k)], "x", lk.past_x
    )
    crossing = []

    def cross(j):
        ref = out.at[j, c, every]
        crossing.append(lk.put(ref, ref, lk.nbr("c", 1)))

    cross(y)
    yield from ring_gather(
        lk, out.at[y, c, every], lambda j: out.at[j, c, every], lambda j, k: out.at[j, c, cut(k)], "y", y, cross
    )
    yield 1
    for copy in crossing:
        copy.wait_recv()


def line_gather(lk, own, out, cut):
    z, rows = lk.z, own.shape[0]
    kept = lk.keep(own, out.at[z])

    def part(i, k):
        return out.at[i, pl.ds(0, cut)] if k == 0 else out.at[i, pl.ds(cut, rows - cut)]

    rest = ring_gather(lk, own, lambda i: out.at[i], part, "z", z)
    yield next(rest)
    kept.wait()
    yield from rest


def swap_blocks(lk, src, dst, to_row):
    z, c, n = lk.z, lk.c, lk.n
    lk.n += 2
    assert lk.n <= lk.send.shape[0]
    first = lk.m
    lk.m += 2
    copies, keeps, selves = [], [], []
    for k in range(2):
        if to_row:
            slot, core, place = z % 2, z // 2, 2 * k + c
        else:
            slot, core, place = z // 2, z % 2, 2 * c + k
        selves.append((place == z) & (core == c))
        copies.append(
            pltpu.make_async_remote_copy(
                src_ref=src(k),
                dst_ref=dst(slot),
                send_sem=lk.send.at[n + k],
                recv_sem=lk.recv.at[n + slot],
                device_id=lk.dev(lk.x, lk.y, core, place),
                device_id_type=MESH,
            )
        )
        keeps.append(pltpu.make_async_copy(src(k), dst(k), lk.local.at[first + k]))
        pl.when(selves[k])(keeps[k].start)
        pl.when(jnp.logical_not(selves[k]))(copies[k].start)
    yield 1
    for k in range(2):
        if to_row:
            own = (z == 2 * c + k) & (c == z % 2)
        else:
            own = (z == 2 * k + c) & (c == z // 2)
        landed = pltpu.make_async_remote_copy(
            src_ref=src(k),
            dst_ref=dst(k),
            send_sem=lk.send.at[n + k],
            recv_sem=lk.recv.at[n + k],
            device_id=lk.near["c", 1],
            device_id_type=MESH,
        )
        pl.when(own)(keeps[k].wait)
        pl.when(jnp.logical_not(own))(landed.wait_recv)
        pl.when(jnp.logical_not(selves[k]))(copies[k].wait_send)


def cots_gather(lk, home, out):
    z, c = lk.z, lk.c
    source, place = c == z // 2, (z + 4 - 2 * c) % 4
    here, there = pl.ds(pl.multiple_of(128 * (z % 2), 128), 128), pl.ds(pl.multiple_of(128 - 128 * (z % 2), 128), 128)
    over, keeps = [], []
    for m in range(2):
        block = home.at[pl.ds(128 * m, 128)]
        over.append(lk.make(block, out.at[2 * m + c, here], lk.nbr("c", 1)))
        keeps.append(pltpu.make_async_copy(block, out.at[2 * m + c, here], lk.local.at[lk.m + m]))
    lk.m += 2
    right, left = lk.sides("z")
    own = out.at[:, here]
    a, b = lk.make(own, own, right), lk.make(own, own, left)
    half = out.at[pl.ds(0, 2), there]
    rest = out.at[pl.ds(2, 2), there]
    e, f = lk.make(half, half, right), lk.make(rest, rest, left)
    from_left = (place == 1) | (place == 2)
    from_right = jnp.logical_not(from_left)

    @pl.when(source)
    def _():
        for copy in keeps:
            copy.start()

    @pl.when(jnp.logical_not(source))
    def _():
        for copy in over:
            copy.start()

    yield 1

    @pl.when(source)
    def _():
        for copy in keeps:
            copy.wait()
        for copy in over:
            copy.wait_recv()
        a.start()
        b.start()

    @pl.when(jnp.logical_not(source))
    def _():
        for copy in over:
            copy.wait_send()

    yield 1

    @pl.when(from_left)
    def _():
        a.wait_recv()
        e.start()

    @pl.when(from_right)
    def _():
        b.wait_recv()
        f.start()

    yield 1

    @pl.when(jnp.logical_not(source))
    def _():
        e.wait_recv()
        f.wait_recv()

    @pl.when(source)
    def _():
        a.wait_send()
        b.wait_send()

    pl.when(from_left)(e.wait_send)
    pl.when(from_right)(f.wait_send)


def add_into(dst, src):
    if len(dst.shape) == 2:
        dst[...] = (dst[...].astype(F32) + src[...].astype(F32)).astype(BF)
    else:
        for i in range(dst.shape[0]):
            dst[i] = (dst[i].astype(F32) + src[i].astype(F32)).astype(BF)


def ring_reduce(lk, p, part, bufs, axis, me):
    right, left = lk.sides(axis)
    r0, r1, ra, rb = bufs
    before, after, far = lk.ring[axis]
    a = lk.put(part(far, 0), r0, right)
    b = lk.put(part(far, 1), r1, left)
    yield 1
    a.wait_recv()
    add_into(part(after, 0), r0)
    c = lk.put(p(after), ra, right)
    b.wait_recv()
    add_into(part(before, 1), r1)
    d = lk.put(p(before), rb, left)
    yield 1
    c.wait_recv()
    add_into(p(me), ra)
    d.wait_recv()
    add_into(p(me), rb)


def plane_reduce(lk, spot, sib_src, sib, bufs, out, first, kept=None):
    x, y, c = lk.x, lk.y, lk.c
    one, two = bufs
    got = lk.put(sib_src, sib, lk.nbr("c", 1))
    yield 1
    if kept is not None:
        kept.wait()
    got.wait_recv()

    def step(i, _):
        ref = spot(i // 4, i % 4)
        ref[...] = (ref[...].astype(F32) + sib[i // 4, i % 4].astype(F32)).astype(BF)
        return 0

    lax.fori_loop(0, 16, step, 0)
    every = slice(None)

    def pair(k):
        return pl.ds(2 * k, 2)

    def rows(ref, k):
        return ref.at[pl.ds(16 * k, 16)]

    if first == "y":
        yield from ring_reduce(lk, lambda j: spot(every, j), lambda j, k: spot(pair(k), j), one, "y", y)
        yield from ring_reduce(lk, lambda i: spot(i, y), lambda i, k: rows(spot(i, y), k), two, "x", x)
    else:
        yield from ring_reduce(lk, lambda i: spot(i, every), lambda i, k: spot(i, pair(k)), one, "x", x)
        yield from ring_reduce(lk, lambda j: spot(x, j), lambda j, k: rows(spot(x, j), k), two, "y", y)
    yield 1
    yield from line_gather(lk, spot(x, y), out, 16)


def ring_scratch(cols):
    return [
        pltpu.VMEM((4, 4, 32, cols), BF),
        pltpu.VMEM((2, 32, cols), BF),
        pltpu.VMEM((2, 32, cols), BF),
        pltpu.VMEM((4, 32, cols), BF),
        pltpu.VMEM((4, 32, cols), BF),
        pltpu.VMEM((16, cols), BF),
        pltpu.VMEM((16, cols), BF),
        pltpu.VMEM((32, cols), BF),
        pltpu.VMEM((32, cols), BF),
    ]


def down_scratch(rows):
    first = (rows // 16 + 1) // 2 * 16
    ring = [(first, 1024), (rows - first, 1024), (rows, 1024), (rows, 1024)]
    return [pltpu.VMEM(dims, BF) for dims in [(4, rows, 1024)] * 2 + ring * 2]


def down_reduce(lk, part_hbm, s, out, lo, rows):
    acc, sib, one, (x0, x1, xa, xb) = s[0], s[1], s[2:6], s[6:10]
    y, c = lk.y, lk.c
    every, cut, down_part = pl.ds(lo, rows), down_cut(lo, rows), down_cut(0, rows)
    kept = lk.keep(part_hbm.at[:, c, every], acc)
    got = lk.put(part_hbm.at[:, lk.other, every], sib, lk.nbr("c", 1))
    yield 1
    kept.wait()
    got.wait_recv()
    add_into(acc, sib)
    yield from ring_reduce(
        lk, lambda j: acc.at[j], lambda j, k: acc.at[j, down_part(k)], one, "y", y
    )
    mine = acc.at[y]
    right, left = lk.sides("x")
    place = lk.past_x
    a = lk.make(acc.at[y, down_part(0)], x0, left)
    b = lk.make(acc.at[y, down_part(1)], x1, right)
    e = lk.make(mine, xa, left)
    f = lk.make(mine, xb, right)

    @pl.when(place == 2)
    def _():
        a.start()
        b.start()

    yield 1

    @pl.when(place == 1)
    def _():
        a.wait_recv()
        add_into(acc.at[y, down_part(0)], x0)
        e.start()

    @pl.when(place == 3)
    def _():
        b.wait_recv()
        add_into(acc.at[y, down_part(1)], x1)
        f.start()

    yield 1

    @pl.when(place == 0)
    def _():
        e.wait_recv()
        add_into(mine, xa)
        f.wait_recv()
        add_into(mine, xb)

    @pl.when(place == 1)
    def _():
        e.wait_send()

    @pl.when(place == 3)
    def _():
        f.wait_send()

    @pl.when(place == 2)
    def _():
        a.wait_send()
        b.wait_send()

    yield from ring_spread(
        lk, mine, out.at[every], lambda k: out.at[cut(k)], "z", lk.past_z
    )


ANY = pl.BlockSpec(memory_space=pl.ANY)


def sems(n):
    return [pltpu.SemaphoreType.DMA((n,)), pltpu.SemaphoreType.DMA((n,)), pltpu.SemaphoreType.DMA((40,))]


def params(number):
    return pltpu.CompilerParams(collective_id=number, has_side_effects=True, vmem_limit_bytes=56 * 2**20)


def shape(*dims, dtype=BF):
    return jax.ShapeDtypeStruct(dims, dtype)


def lanes_of(shape):
    return lax.broadcasted_iota(jnp.int32, shape, len(shape) - 1)


def dot(left, right, dims=((1,), (0,)), kind=F32):
    return lax.dot_general(left, right, (dims, ((), ())), preferred_element_type=F32).astype(kind)


TOKENS = ((0,), (0,))
ROWS = ((1,), (1,))


def flat(value):
    return value.reshape(-1, value.shape[-1])


def head_ones():
    row = lax.broadcasted_iota(jnp.int32, (256, 256), 0) // 64
    col = lax.broadcasted_iota(jnp.int32, (256, 256), 1) // 64
    return jnp.where(row == col, 1.0 / 64, 0.0).astype(BF)


def head_mean(v, ones):
    high = v.astype(BF)
    low = (v - high.astype(F32)).astype(BF)
    return dot(high, ones) + dot(low, ones)


def halves_swapped(v):
    lane = lanes_of(v.shape)
    return jnp.where(lane % 64 < 32, pltpu.roll(v, 96, 1), pltpu.roll(v, 32, 1))


def angle_tables(tab):
    lane = lanes_of(tab.shape)
    other = pltpu.roll(tab, 64, 1)
    return jnp.where(lane < 64, tab, other), jnp.where(lane < 64, other, tab)


def row_scale(v):
    return lax.rsqrt(jnp.mean(v * v, axis=-1, keepdims=True) + EPS)


def gain_rows(whole, gain):
    def step(i, total):
        return total + whole[i // 8, (i // 2) % 4, i % 2, :, pl.ds(2048, 128)].astype(F32)

    total = lax.fori_loop(0, 32, step, jnp.zeros((32, 128), F32))
    for k in range(8):
        gain[0:1, pl.ds(128 * k, 128)] = total[8 + k : 9 + k]
        gain[1:2, pl.ds(128 * k, 128)] = total[16 + k : 17 + k]
        gain[2:3, pl.ds(128 * k, 128)] = total[0:1]
        gain[3:4, pl.ds(128 * k, 128)] = total[1:2]


def keys_values(whole, source, gain, normed, keys, values, lin_key, core):
    ones = head_ones()
    src = source[:, 0:1024].astype(F32)
    normed[...] = (src * row_scale(src) * gain[0:1]).astype(BF)
    cosine, sine = angle_tables(source[:, 1024:1152].astype(F32))
    kn = gain[3:4, 0:128]
    lane = lanes_of((256, 128))
    here = pl.ds(pl.multiple_of(core * 256, 256), 256)

    def put(ref, tile, r):
        turned = pltpu.roll(r, 64, 1)
        ref[2 * tile, here] = jnp.where(lane < 64, r, turned).astype(BF)
        ref[2 * tile + 1, here] = jnp.where(lane < 64, turned, r).astype(BF)

    for j in range(4):
        lin = dot(normed[...], flat(whole[:, :, :, :, pl.ds(1024 + 256 * j, 256)]))
        if j < 2:
            scale = lax.rsqrt(head_mean(lin * lin, ones) + EPS)
            lin_key[:, pl.ds(256 * j, 256)] = lin
            for h in range(2):
                cut = slice(128 * h, 128 * h + 128)
                v = lin[:, cut] * scale[:, cut] * kn
                put(keys, 2 * j + h, v * cosine + halves_swapped(v) * sine)
        else:
            for h in range(2):
                put(values, 2 * (j - 2) + h, lin[:, 128 * h : 128 * h + 128])


def own_queries(whole, source, gain, normed, lin_query, queries):
    ones = head_ones()
    cosine, sine = angle_tables(source[:, 1024:1152].astype(F32))
    qn = gain[2:3, 0:128]
    lane = lanes_of((256, 128))

    def step(j, _):
        lin = dot(normed[...], flat(whole[:, :, :, :, pl.ds(pl.multiple_of(256 * j, 256), 256)]))
        lin_query[:, pl.ds(pl.multiple_of(256 * j, 256), 256)] = lin
        scale = lax.rsqrt(head_mean(lin * lin, ones) + EPS)
        for h in range(2):
            cut = slice(128 * h, 128 * h + 128)
            v = lin[:, cut] * scale[:, cut] * qn
            r = (v * cosine + halves_swapped(v) * sine) * HEAD_SIZE ** (-0.5)
            first = jnp.where(lane < 64, r, 0.0).astype(BF)
            second = jnp.where(lane < 64, 0.0, r).astype(BF)
            for m in range(2):
                queries[m, 2 * j + h, 0:128] = first[128 * m : 128 * m + 128]
                queries[m, 2 * j + h, 128:256] = second[128 * m : 128 * m + 128]
        return 0

    lax.fori_loop(0, 4, step, 0)


def attend(m, queries, keys, values, starts, mask, probs, mixed, core):
    key_pos = lax.broadcasted_iota(jnp.int32, (512, 256), 0)
    query_pos = core * 256 + 128 * m + lax.broadcasted_iota(jnp.int32, (1, 256), 1) % 128
    lane = lanes_of((128, 128))
    row = starts[m, 0:1]
    begin = jnp.concatenate([row, row], axis=1)
    mask[...] = jnp.where((key_pos <= query_pos) & (key_pos.astype(F32) >= begin), 1.0, 0.0)

    def step(k, _):
        scores = dot(keys[k], queries[m, k], ROWS)
        raised = jnp.exp(scores) * mask[...]
        chance = (raised * (1.0 / jnp.sum(raised, axis=0, keepdims=True))).astype(BF)
        probs[8 * m + k] = chance
        got = dot(values[k], chance, TOKENS).T
        both = jnp.where(lane < 64, got[0:128], got[128:256]).astype(BF)
        mixed[128 * m : 128 * m + 128, pl.ds(pl.multiple_of(k * 128, 128), 128)] = both
        return 0

    lax.fori_loop(0, 8, step, 0, unroll=UNROLL)


UNROLL = 4


def out_project(m, whole, source, gain, mixed, middle, normed_ffn, own):
    rows = pl.ds(128 * m, 128)

    def step(j, _):
        cut = pl.ds(pl.multiple_of(256 * j, 256), 256)
        w = flat(whole[:, :, :, :, pl.ds(pl.multiple_of(2176 + 256 * j, 128), 256)])
        middle[rows, cut] = source[rows, cut].astype(F32) + dot(mixed[rows], w)
        return 0

    lax.fori_loop(0, 4, step, 0)
    mid = middle[rows]
    normed_ffn[own, rows] = (mid * row_scale(mid) * gain[1:2]).astype(BF)


def own_gains(params, dp):
    row = jnp.broadcast_to(params, (32, 128))
    line = lax.broadcasted_iota(jnp.int32, (32, 128), 0)
    lane = lanes_of((32, 128))
    spot = dp % 4 * 32
    window = (lane >= spot) & (lane < spot + 32)
    got = jnp.where((line == 8 + dp // 4) & window, pltpu.roll(row, spot, 1), 0.0)
    got = got + jnp.where((line == 16 + dp // 4) & window, pltpu.roll(row, (spot + 96) % 128, 1), 0.0)
    pair = (lane % 64 >= 2 * dp) & (lane % 64 < 2 * dp + 2)
    for k in range(2):
        low = pltpu.roll(row, (2 * dp + 64 - 2 * k) % 128, 1)
        high = pltpu.roll(row, (2 * dp + 128 - 2 * k) % 128, 1)
        got = got + jnp.where((line == k) & pair, jnp.where(lane < 64, low, high), 0.0)
    return got.astype(BF)


def feed_back_in(slots, cots, down, grad_hidden):
    tokens = jnp.concatenate([cots[i] for i in slots], axis=0) if len(slots) > 1 else cots[slots[0]]
    got = dot(tokens, flat(down[...]), ROWS, BF)
    for n, i in enumerate(slots):
        grad_hidden[i] = got[256 * n : 256 * n + 256]


def feed_chunk(slots, ffn, gate_up, down, grad_hidden, hidden, turned, ffn_turned, grad_both, grad_ffn, out_part):
    def load(ref, *cut):
        return jnp.concatenate([ref[(i, *cut)] for i in slots], axis=0) if len(slots) > 1 else ref[(slots[0], *cut)]

    def store(ref, value, *cut):
        for n, i in enumerate(slots):
            ref[(i, *cut)] = value[256 * n : 256 * n + 256]

    every = slice(None)
    size = 256 * len(slots)

    def step(j, _):
        cut = pl.ds(pl.multiple_of(384 * j, 128), 384)
        cut_up = pl.ds(pl.multiple_of(1152 + 384 * j, 128), 384)
        tokens = load(ffn, every, every)
        gated = dot(tokens, flat(gate_up[:, :, :, :, cut]))
        upward = dot(tokens, flat(gate_up[:, :, :, :, cut_up]))
        sigma = 1.0 / (1.0 + jnp.exp(-gated))
        silu = gated * sigma
        made = (silu * upward).astype(BF)
        hidden[0:size, cut] = made
        for n, i in enumerate(slots):
            turned[cut, pl.ds(pl.multiple_of(256 * i, 256), 256)] = made[256 * n : 256 * n + 256].T
        back = load(grad_hidden, every, cut).astype(F32)
        store(grad_both, (back * upward * sigma * (1.0 + gated * (1.0 - sigma))).astype(BF), every, cut)
        store(grad_both, (back * silu).astype(BF), every, cut_up)
        return 0

    lax.fori_loop(0, 3, step, 0)

    def last(j, _):
        cut = pl.ds(pl.multiple_of(256 * j, 256), 256)
        store(grad_ffn, dot(load(grad_both, every, every), flat(gate_up[j]), ROWS, BF), every, cut)
        store(out_part, dot(hidden[0:size], flat(down[:, :, :, cut]), kind=BF), every, cut)
        for i in slots:
            ffn_turned[cut, pl.ds(pl.multiple_of(256 * i, 256), 256)] = ffn[i, :, cut].T
        return 0

    lax.fori_loop(0, 4, last, 0)


def feed_grads(left, right, out, first, tiles):
    def step(j, _):
        cut = pl.ds(pl.multiple_of(256 * j, 256), 256)
        got = dot(left[...], flat(right[:, :, cut]), kind=BF)
        lead = out.shape[:-1]
        out[(slice(None),) * len(lead) + (cut,)] = got.reshape(*lead, 256)
        return 0

    lax.fori_loop(first, tiles, step, 0)


FWD_SCRATCH = [
    pltpu.VMEM((4, 4, 2, 32, WA), BF),
    pltpu.VMEM((4, 4, 2, 32, GU), BF),
    pltpu.VMEM((4, 2, DN, 1024), BF),
    pltpu.VMEM((256, 1152), BF),
    pltpu.VMEM((256, 128), F32),
    pltpu.VMEM((256, 1152), BF),
    pltpu.VMEM((4, 256, 1024), BF),
    pltpu.VMEM((4, 256, 1024), BF),
    pltpu.VMEM((256, 1024), BF),
    pltpu.VMEM((256, 1024), F32),
    pltpu.VMEM((256, 512), F32),
    pltpu.VMEM((8, 512, 128), BF),
    pltpu.VMEM((8, 512, 128), BF),
    pltpu.VMEM((2, 8, 256, 128), BF),
    pltpu.VMEM((16, 512, 256), BF),
    pltpu.VMEM((256, 1024), BF),
    pltpu.VMEM((256, 1024), F32),
    pltpu.VMEM((8, 1024), F32),
    pltpu.VMEM((4, 256, 1152), BF),
    pltpu.VMEM((512, 1152), BF),
    pltpu.VMEM((1152, 1024), BF),
    pltpu.VMEM((1024, 1024), BF),
    pltpu.VMEM((4, 256, GU), BF),
    pltpu.VMEM((4, 256, 1024), BF),
    pltpu.VMEM((4, 256, 1024), BF),
    pltpu.VMEM((256, 1024), BF),
    pltpu.VMEM((256, 1024), BF),
    pltpu.VMEM((4, 64, 1024), BF),
    pltpu.VMEM((2, 8, 128), F32),
    pltpu.VMEM((32, WA), BF),
    pltpu.VMEM((32, GU), BF),
    pltpu.VMEM((1, 128), F32),
    pltpu.VMEM((512, 256), F32),
]

FWD_OUT = (
    shape(4, 4, 2, 32, WA),
    shape(256, 1024),
    shape(256, 1024, dtype=F32),
    shape(256, 512, dtype=F32),
    shape(8, 512, 128),
    shape(8, 512, 128),
    shape(2, 8, 256, 128),
    shape(16, 512, 256),
    shape(256, 1024),
    shape(256, 1024, dtype=F32),
    shape(8, 1024, dtype=F32),
    shape(4, 4, 2, 32, GU),
    shape(4, 2, DN, 1024),
    shape(4, 256, 1024),
    shape(256, 1024, dtype=F32),
    shape(256, 1152),
    shape(256, 1024),
)


FWD_IN = 12


def go(*steps):
    for s in steps:
        next(s, None)


def fwd_kernel(*refs):
    w_query, key_weight, value_weight, w_out, w_gate, w_up, dn, x, cot, tab, starts_hbm, params_hbm = refs[:FWD_IN]
    refs = refs[FWD_IN:]
    outs, refs = refs[: len(FWD_OUT)], refs[len(FWD_OUT) :]
    lk = Links(*refs[:3])
    (
        whole, gate_up, down, source, table, at_home, cots, ffn, normed, lin_query, lin_key, keys, values, queries,
        probs, mixed, middle, gain, grad_hidden, hidden, turned, ffn_turned, grad_both, grad_ffn, out_part,
        from_right, from_left, passing, starts, wa, gu, own_params, mask,
    ) = refs[3:]
    own = lk.z
    before, after, far = lk.ring["z"]
    quarter = pl.ds(pl.multiple_of(own * 1152, 128), 1152)
    staged = [
        lk.keep(params_hbm, own_params),
        lk.keep(tab, table),
        lk.keep(x, at_home.at[:, pl.ds(0, 1024)]),
        lk.keep(w_query, wa.at[:, pl.ds(0, 1024)]),
        lk.keep(key_weight, wa.at[:, pl.ds(1024, 512)]),
        lk.keep(value_weight, wa.at[:, pl.ds(1536, 512)]),
        lk.keep(w_out, wa.at[:, pl.ds(2176, 1024)]),
        lk.keep(w_gate.at[:, quarter], gu.at[:, pl.ds(0, 1152)]),
        lk.keep(w_up.at[:, quarter], gu.at[:, pl.ds(1152, 1152)]),
    ]
    staged[0].wait()
    staged[1].wait()
    at_home[:, 1024:1152] = table[...].astype(BF)
    wa[:, 2048:2176] = own_gains(own_params[...], lax.axis_index("dp"))
    for copy in staged[2:]:
        copy.wait()
    lk.barrier()
    k1 = plane_gather(lk, wa, whole, "x", 1024, 1536)
    k2 = plane_gather(lk, wa, whole, "y", 1536, 2176)
    a1 = plane_gather(lk, wa, whole, "x", 0, 1024)
    a2 = plane_gather(lk, wa, whole, "y", 2176, WA)
    half = [pl.ds(0, 128), pl.ds(128, 128)]

    def slot(j):
        return pl.ds(128 * j, 128) if isinstance(j, int) else pl.ds(pl.multiple_of(128 * j, 128), 128)

    x1 = swap_blocks(lk, lambda m: at_home.at[half[m]], lambda j: source.at[slot(j)], True)
    s1 = swap_blocks(lk, lambda m: starts_hbm.at[m], lambda j: starts.at[j], True)
    g1 = plane_gather(lk, gu, gate_up, "x", 0, 1152)
    g2 = plane_gather(lk, gu, gate_up, "y", 1152, GU)
    d1, d2 = down_gather(lk, dn, down, 0, 80), down_gather(lk, dn, down, 80, 64)
    c1 = cots_gather(lk, cot, cots)
    go(x1, s1, c1)
    go(k1, k2)
    go(a1, a2)
    go(k1, k2)
    go(a1, a2)
    go(k1, k2)
    go(a1, a2)
    go(x1, s1)
    go(c1)
    go(k1, k2)
    go(g1, g2)
    go(k1, k2)
    go(a1, a2)
    go(d1, d2)
    drive(k1, k2, x1, s1)
    gain_rows(whole, gain)
    keys_values(whole, source, gain, normed, keys, values, lin_key, lk.c)
    mine = pl.ds(pl.multiple_of(lk.c * 256, 256), 256)
    crossed = [lk.put(ref.at[:, mine], ref.at[:, mine], lk.nbr("c", 1)) for ref in (keys, values)]
    go(g1, g2)
    drive(a1, a2)
    go(g1, g2)
    own_queries(whole, source, gain, normed, lin_query, queries)
    go(d1, d2)
    go(c1)
    for copy in crossed:
        copy.wait_recv()
    saved = [lk.keep(source, outs[15])]
    for k, ref in enumerate((normed, lin_query, lin_key, keys, values, queries)):
        saved.append(lk.keep(ref, outs[1 + k]))
    passed = []
    for m in range(2):
        attend(m, queries, keys, values, starts, mask, probs, mixed, lk.c)
        go(g1, g2)
        if m == 0:
            go(d1, d2)
            saved.append(lk.keep(whole, outs[0]))
        out_project(m, whole, source, gain, mixed, middle, ffn, own)
        rows = pl.ds(128 * m, 128)

        def part(i, k, m=m):
            return ffn.at[i, pl.ds(128 * m + 64 * k, 64)]

        passed.append(
            ring_gather(lk, ffn.at[own, rows], lambda i, rows=rows: ffn.at[i, rows], part, "z", own)
        )
        go(passed[m])
        if m == 0:
            go(c1)
    go(passed[0])
    go(d1, d2)
    drive(c1)
    saved.append(lk.keep(cots.at[own], outs[16]))
    for k, ref in enumerate((probs, mixed, middle, gain)):
        saved.append(lk.keep(ref, outs[7 + k]))
    drive(g1, g2, d1, d2)
    feed_back_in((own,), cots, down, grad_hidden)

    def chunk(*slots):
        feed_chunk(
            slots, ffn, gate_up, down, grad_hidden, hidden, turned, ffn_turned, grad_both, grad_ffn, out_part
        )

    right, left = lk.sides("z")
    chunk(own)
    go(passed[1])
    feed_back_in((before, after), cots, down, grad_hidden)
    chunk(before, after)
    low, high = pl.ds(0, 128), pl.ds(128, 128)
    sent = [
        lk.put(grad_ffn.at[after, high], from_left.at[high], right),
        lk.put(grad_ffn.at[before, low], from_right.at[low], left),
    ]
    feed_back_in((far,), cots, down, grad_hidden)
    drive(*passed)
    chunk(far)
    lk.flush()
    saved.append(lk.keep(out_part, outs[13]))
    hops = []
    for k in range(2):
        rows = pl.ds(64 * k, 64)
        hops.append((lk.put(grad_ffn.at[far, rows], passing.at[k], right), after, rows, from_left, right))
    for k in range(2):
        rows = pl.ds(128 + 64 * k, 64)
        hops.append((lk.put(grad_ffn.at[far, rows], passing.at[2 + k], left), before, rows, from_right, left))

    def hop(k):
        copy, slot, rows, landing, to = hops[k]
        copy.wait_recv()
        add_into(grad_ffn.at[slot, rows], passing.at[k])
        sent.append(lk.put(grad_ffn.at[slot, rows], landing.at[rows], to))

    feed_grads(turned, cots, down, 0, 4)
    saved.append(lk.keep(down, outs[12]))
    hop(0)
    hop(2)
    feed_grads(ffn_turned, grad_both, gate_up, 0, 4)
    hop(1)
    hop(3)
    feed_grads(ffn_turned, grad_both, gate_up, 4, 9)
    saved.append(lk.keep(gate_up, outs[11]))
    for copy in sent:
        copy.wait_recv()
    saved.pop(2).wait()
    total = grad_ffn[own].astype(F32) + from_right[...].astype(F32) + from_left[...].astype(F32)
    lin_query[...] = total
    saved.append(lk.keep(lin_query, outs[14]))
    for copy in saved:
        copy.wait()
    lk.flush()


def forward(*args):
    return pl.pallas_call(
        fwd_kernel,
        out_shape=FWD_OUT,
        in_specs=[ANY] * FWD_IN,
        out_specs=[ANY] * len(FWD_OUT),
        scratch_shapes=sems(160) + FWD_SCRATCH,
        compiler_params=pltpu.CompilerParams(
            collective_id=0, has_side_effects=True, vmem_limit_bytes=60 * 2**20
        ),
    )(*args)


BWD_IN = 17
PIECES = (1152, 1152, 512, 512, 512, 512, 512, 512, 128)
BWD_OUT = (
    shape(2, 128, 1024),
    shape(2, 128, 1024),
    shape(4, 32, WA),
    shape(4, 32, GU),
    shape(DN, 1024),
)
BWD_SCRATCH = [
    pltpu.VMEM((4, 4, 2, 32, WA), BF),
    pltpu.VMEM((256, 1024), BF),
    pltpu.VMEM((256, 1024), F32),
    pltpu.VMEM((256, 512), F32),
    pltpu.VMEM((8, 512, 128), BF),
    pltpu.VMEM((8, 512, 128), BF),
    pltpu.VMEM((2, 8, 256, 128), BF),
    pltpu.VMEM((16, 512, 256), BF),
    pltpu.VMEM((256, 1024), BF),
    pltpu.VMEM((256, 1024), F32),
    pltpu.VMEM((8, 1024), F32),
    pltpu.VMEM((4, 256, 1024), BF),
    pltpu.VMEM((256, 1024), F32),
    pltpu.VMEM((256, 1024), BF),
    pltpu.VMEM((256, 1152), BF),
]
BWD_WORK = [
    pltpu.VMEM((256, 1024), BF),
    pltpu.VMEM((2, 8, 256, 128), BF),
    pltpu.VMEM((256, 1024), F32),
    pltpu.VMEM((2, 256, 1024), BF),
    pltpu.VMEM((256, 2048), BF),
    pltpu.VMEM((1024, 256), BF),
    pltpu.VMEM((256, 1024), F32),
    pltpu.VMEM((8, 1024), F32),
    pltpu.VMEM((4, 4, 2, 32, WA), BF),
    pltpu.VMEM((4, 4, 32, 1152), BF),
    pltpu.VMEM((4, 4, 32, 1152), BF),
    pltpu.VMEM((256, 1024), BF),
    pltpu.VMEM((256, 1024), BF),
    pltpu.VMEM((256, 1024), BF),
]
Z_RING = [
    pltpu.VMEM((128, 1024), BF),
    pltpu.VMEM((128, 1024), BF),
    pltpu.VMEM((256, 1024), BF),
    pltpu.VMEM((256, 1024), BF),
]


def norm_back(v, g, dy):
    r = row_scale(v)
    gdy = g * dy
    back = r * gdy - v * (r * r * r * jnp.mean(v * gdy, axis=-1, keepdims=True))
    return back, jnp.sum(v * r * dy, axis=0, keepdims=True)


def heads_back(lin, grad, gain, cosine, sine, ones):
    parts = []
    for h in range(2):
        part = grad[:, 128 * h : 128 * h + 128]
        parts.append(part * cosine + halves_swapped(part * sine))
    dy = jnp.concatenate(parts, axis=1)
    r = lax.rsqrt(head_mean(lin * lin, ones) + EPS)
    gdy = dy * gain
    back = r * gdy - lin * (r * r * r * head_mean(lin * gdy, ones))
    return back, jnp.sum(lin * r * dy, axis=0, keepdims=True)


def turned_grads(turned, right, out, start, tiles, base=0):
    def step(j, _):
        got = dot(turned[...], right[:, pl.ds(pl.multiple_of(base + 256 * j, 256), 256)], kind=BF)
        out[:, :, :, :, pl.ds(pl.multiple_of(start + 256 * j, 128), 256)] = got.reshape(4, 4, 2, 32, 256)
        return 0

    lax.fori_loop(0, tiles, step, 0)


def attend_back(half, queries, keys, values, probs, grad_mixed, grad_queries, grad_kv):
    lane = lanes_of((128, 128))
    lane_keys = lanes_of((512, 128))

    def step(j, _):
        folded = []
        for e in range(2):
            k = 2 * j + e
            cut = pl.ds(pl.multiple_of(128 * k, 128), 128)
            key_sum = value_sum = None
            for m in range(2):
                chance = probs[8 * m + k]
                back = dot(values[k], grad_mixed[m, k], ROWS)
                p = chance.astype(F32)
                p_back = p * back
                grad_scores = (p_back - p * jnp.sum(p_back, axis=0, keepdims=True)).astype(BF)
                got = dot(keys[k], grad_scores, TOKENS).T
                grad_queries[128 * m : 128 * m + 128, cut] = jnp.where(lane < 64, got[0:128], got[128:256])
                more_keys, more_values = dot(grad_scores, queries[m, k]), dot(chance, grad_mixed[m, k])
                key_sum = more_keys if m == 0 else key_sum + more_keys
                value_sum = more_values if m == 0 else value_sum + more_values
            folded += [v + pltpu.roll(v, 64, 1) for v in (key_sum, value_sum)]
        for s in range(2):
            tile = jnp.where(lane_keys < 64, folded[s], folded[2 + s]).astype(BF)
            cut = pl.ds(pl.multiple_of(512 * s + 128 * j, 128), 128)
            grad_kv[0, :, cut] = tile[0:256]
            grad_kv[1, :, cut] = tile[256:512]
        return 0

    lax.fori_loop(2 * half, 2 * half + 2, step, 0)


def bwd_kernel(*refs):
    ins, refs = refs[:BWD_IN], refs[BWD_IN:]
    outs, refs = refs[: len(BWD_OUT)], refs[len(BWD_OUT) :]
    lk = Links(*refs[:3])
    refs = refs[3:]
    n = len(BWD_SCRATCH)
    held, refs = refs[:n], refs[n:]
    (
        whole, normed, lin_query, lin_key, keys, values, queries, probs, mixed, middle, gain, out_part, grad_middle,
        upstream, source,
    ) = held
    grad_gu, grad_down = ins[15:]
    n = len(BWD_WORK)
    work, refs = refs[:n], refs[n:]
    (
        grad_branch, grad_mixed, grad_queries, grad_kv, grad_lin, turned, grad_normed, gains_back, grad_whole, acc_a,
        acc_b, made, sent_back, kv_other,
    ) = work
    z_out, refs = refs[:4], refs[4:]
    down_refs, refs = refs[:20], refs[20:]
    rings = [refs[9 * i : 9 * i + 9] for i in range(len(PIECES))]
    outputs, grad_inputs, a_all, gu_all, down_own = outs
    own, c = lk.z, lk.c

    order = [11, 12, 9, 13, 10, 0, 8, 5, 7, 6, 4, 2, 14, 1, 3]
    loads = {}
    for k in order[:7]:
        loads[k] = lk.keep(ins[k], held[k])
    lk.barrier()

    def piece(k, spot, src, out, first, kept=None):
        ring = rings[k]
        return plane_reduce(lk, spot, src, ring[0], (ring[1:5], ring[5:9]), out, first, kept)

    def feed_piece(k, acc, lo, first):
        cols = pl.ds(lo, 1152)
        kept = lk.keep(grad_gu.at[:, :, c, :, cols], acc)
        return piece(
            k, lambda i, j: acc.at[i, j], grad_gu.at[:, :, lk.other, :, cols], gu_all.at[:, :, cols], first, kept
        )

    def whole_piece(k, lo, first):
        cols = pl.ds(lo, PIECES[k])
        return piece(
            k, lambda i, j: grad_whole.at[i, j, c, :, cols], grad_whole.at[:, :, lk.other, :, cols],
            a_all.at[:, :, cols], first,
        )

    def out_chain():
        yield from ring_reduce(
            lk, lambda i: out_part.at[i], lambda i, k: out_part.at[i, pl.ds(128 * k, 128)], z_out, "z", own
        )
        made[...] = (middle[...] + out_part[own].astype(F32)).astype(BF)
        yield from swap_blocks(
            lk, lambda j: made.at[pl.ds(128 * j, 128)], lambda m: outputs.at[m], False
        )

    def need(*names):
        for k in names:
            loads.pop(k).wait()

    f1, f2 = feed_piece(0, acc_a, 0, "y"), feed_piece(1, acc_b, 1152, "x")
    d1 = down_reduce(lk, grad_down, down_refs[:10], down_own, 0, 80)
    d2 = down_reduce(lk, grad_down, down_refs[10:], down_own, 80, 64)
    go(d1, d2, f1, f2)
    o1 = out_chain()
    need(11)
    go(o1)
    for k in order[7:]:
        loads[k] = lk.keep(ins[k], held[k])
    need(12, 9, 13, 10)
    back, row = norm_back(middle[...], gain[1:2], grad_middle[...])
    total = upstream[...].astype(F32) + back
    grad_middle[...] = total
    grad_branch[...] = total.astype(BF)
    gains_back[1:2] = row
    need(0, 8)
    go(d1, d2)
    lane = lanes_of((256, 128))

    def back_mixed(j, _):
        got = dot(grad_branch[...], flat(whole[j, :, :, :, pl.ds(2176, 1024)]), ROWS)
        for h in range(2):
            r = got[:, 128 * h : 128 * h + 128]
            first = jnp.where(lane < 64, r, 0.0).astype(BF)
            second = jnp.where(lane < 64, 0.0, r).astype(BF)
            for m in range(2):
                grad_mixed[m, 2 * j + h, 0:128] = first[128 * m : 128 * m + 128]
                grad_mixed[m, 2 * j + h, 128:256] = second[128 * m : 128 * m + 128]
        return 0

    lax.fori_loop(0, 4, back_mixed, 0)
    go(f2, f1)
    need(5, 7, 6, 4)
    attend_back(0, queries, keys, values, probs, grad_mixed, grad_queries, grad_kv)
    go(d1, d2)
    go(f2, f1)
    go(o1)
    attend_back(1, queries, keys, values, probs, grad_mixed, grad_queries, grad_kv)
    crossed = lk.put(grad_kv.at[lk.other], kv_other, lk.nbr("c", 1))
    turned[...] = mixed[...].T
    turned_grads(turned, grad_branch, grad_whole, 2176, 4)
    p2, p3 = whole_piece(2, 2176, "y"), whole_piece(3, 2688, "x")
    go(p2, p3)
    go(d1, d2)
    go(f2)
    need(2, 14, 1)
    ones = head_ones()
    cosine, sine = angle_tables(source[:, 1024:1152].astype(F32))

    def back_query(j, _):
        cut = pl.ds(pl.multiple_of(256 * j, 256), 256)
        grad = grad_queries[:, cut] * HEAD_SIZE ** (-0.5)
        got, line = heads_back(lin_query[:, cut], grad, gain[2:3, 0:256], cosine, sine, ones)
        grad_lin[:, cut] = got.astype(BF)
        gains_back[2:3, cut] = line
        return 0

    lax.fori_loop(0, 4, back_query, 0)
    turned[...] = normed[...].T
    need(3)
    crossed.wait_recv()

    def back_key(j, _):
        cut = pl.ds(pl.multiple_of(256 * j, 256), 256)
        grad = grad_kv[c, :, cut].astype(F32) + kv_other[:, cut].astype(F32)
        got, line = heads_back(lin_key[:, cut], grad, gain[3:4, 0:256], cosine, sine, ones)
        grad_lin[:, pl.ds(pl.multiple_of(1024 + 256 * j, 256), 256)] = got.astype(BF)
        gains_back[3:4, cut] = line
        return 0

    lax.fori_loop(0, 2, back_key, 0)
    value_sum = grad_kv[c, :, 512:1024].astype(F32) + kv_other[:, 512:1024].astype(F32)
    grad_lin[:, 1536:2048] = value_sum.astype(BF)

    turned_grads(turned, grad_lin, grad_whole, 1024, 4, 1024)
    p6, p7 = whole_piece(6, 1024, "y"), whole_piece(7, 1536, "x")
    go(p6, p7)
    go(d1, d2)
    go(f1, f2)
    go(p2, p3)
    turned_grads(turned, grad_lin, grad_whole, 0, 4)
    go(o1)
    p4, p5 = whole_piece(4, 0, "y"), whole_piece(5, 512, "x")
    go(p4, p5)
    go(p6, p7)
    go(d1, d2)

    def back_normed(j, _):
        grad_normed[:, pl.ds(pl.multiple_of(256 * j, 256), 256)] = dot(
            grad_lin[...], flat(whole[j, :, :, :, pl.ds(0, 2048)]), ROWS
        )
        return 0

    lax.fori_loop(0, 4, back_normed, 0)
    go(p2, p3)
    go(p6, p7)
    go(p4, p5)
    go(f2, f1)
    go(d1, d2)
    back, row = norm_back(source[:, 0:1024].astype(F32), gain[0:1], grad_normed[...])
    gains_back[0:1] = row
    sent_back[...] = (grad_middle[...] + back).astype(BF)
    i1 = swap_blocks(lk, lambda j: sent_back.at[pl.ds(128 * j, 128)], lambda m: grad_inputs.at[m], False)
    go(i1)
    small = [jnp.zeros((1, 128), F32)] * 2
    for s, tiles in ((0, 8), (1, 4)):
        for k in range(tiles):
            small[s] = small[s] + gains_back[2 + s : 3 + s, 128 * k : 128 * k + 128]
        small[s] = small[s] + pltpu.roll(jnp.broadcast_to(small[s], (8, 128)), 64, 1)[0:1]
    heads = jnp.where(lanes_of((1, 128)) < 64, small[0], small[1])
    line = lax.broadcasted_iota(jnp.int32, (32, 128), 0)
    for k in range(8):
        cut = slice(128 * k, 128 * k + 128)
        block = jnp.where(line == 8, gains_back[0:1, cut], 0.0)
        block = jnp.where(line == 16, gains_back[1:2, cut], block)
        block = jnp.where(line == 0, heads, block).astype(BF)
        for d in range(4 * k, 4 * k + 4):
            grad_whole[d // 8, (d // 2) % 4, d % 2, :, 2048:2176] = block
    p8 = whole_piece(8, 2048, "y")
    go(p8)
    go(p2, p3)
    go(p6, p7)
    go(p4, p5)
    go(p8)
    go(d1, d2)
    go(p2, p3)
    go(p6, p7)
    go(p4, p5)
    go(p8)
    go(f2, f1)
    go(p2, p3)
    go(p6, p7)
    go(p4, p5)
    go(p8)
    go(d1, d2)
    go(o1)
    go(p2, p3)
    go(p6, p7)
    go(p4, p5)
    go(p8)
    go(i1)
    go(f2, f1)
    go(d1, d2)
    drive(p6, p7, p4, p5, p8, p2, p3, f1, f2, d1, d2, o1, i1)
    lk.flush()


def backward(*args):
    return pl.pallas_call(
        bwd_kernel,
        out_shape=BWD_OUT,
        in_specs=[ANY] * BWD_IN,
        out_specs=[ANY] * len(BWD_OUT),
        scratch_shapes=sems(180) + BWD_SCRATCH + BWD_WORK + Z_RING + down_scratch(80) + down_scratch(64)
        + [v for cols in PIECES for v in ring_scratch(cols)],
        compiler_params=pltpu.CompilerParams(
            collective_id=1, has_side_effects=True, vmem_limit_bytes=62 * 2**20
        ),
    )(*args)


def finish_kernel(*refs):
    ins, outs, held, local = refs[:5], refs[5:15], refs[15:19], refs[19]
    o_out, o_in, o_query, o_key, o_value, o_wout, o_gate, o_up, o_down, o_gains = outs
    a_all, gu_all, down, grad_in = held
    pairs = [(ins[2], a_all), (ins[3], gu_all), (ins[4], down), (ins[0], o_out), (ins[1], grad_in)]
    copies = [pltpu.make_async_copy(src, dst, local.at[k]) for k, (src, dst) in enumerate(pairs)]
    for copy in copies:
        copy.start()
    copies[0].wait()
    for ref, lo, size in (
        (o_query, 0, 1024), (o_key, 1024, 512), (o_value, 1536, 512), (o_gains, 2048, 128), (o_wout, 2176, 1024),
    ):
        total = a_all[0, :, lo : lo + size].astype(F32)
        for i in range(1, 4):
            total = total + a_all[i, :, lo : lo + size].astype(F32)
        ref[...] = total
    copies[1].wait()
    for i in range(4):
        o_gate[:, 1152 * i : 1152 * i + 1152] = gu_all[i, :, 0:1152].astype(F32)
        o_up[:, 1152 * i : 1152 * i + 1152] = gu_all[i, :, 1152:2304].astype(F32)
    copies[2].wait()
    o_down[...] = down[...].astype(F32)
    copies[4].wait()
    o_in[...] = grad_in[...].astype(F32)
    copies[3].wait()


def finish(*args):
    vmem = pl.BlockSpec(memory_space=pltpu.VMEM)
    return pl.pallas_call(
        finish_kernel,
        out_shape=(
            shape(2, 128, 1024), shape(2, 128, 1024, dtype=F32), shape(32, 1024, dtype=F32), shape(32, 512, dtype=F32),
            shape(32, 512, dtype=F32), shape(32, 1024, dtype=F32), shape(32, 4608, dtype=F32),
            shape(32, 4608, dtype=F32), shape(DN, 1024, dtype=F32), shape(32, 128, dtype=F32),
        ),
        in_specs=[ANY] * 5,
        out_specs=[vmem] * 10,
        scratch_shapes=[
            pltpu.VMEM((4, 32, WA), BF), pltpu.VMEM((4, 32, GU), BF), pltpu.VMEM((DN, 1024), BF),
            pltpu.VMEM((2, 128, 1024), BF), pltpu.SemaphoreType.DMA((5,)),
        ],
        compiler_params=pltpu.CompilerParams(vmem_limit_bytes=60 * 2**20),
    )(*args)


def body(
    inputs, starts, w_query, key_weight, value_weight, w_out, w_gate, w_up, w_down,
    prenorm, midnorm, querynorm, keynorm, cotangent,
):
    z = lax.axis_index("seq")
    dp = lax.axis_index("dp")
    params = jnp.concatenate([prenorm, midnorm, querynorm, keynorm, jnp.zeros((60,), BF)])
    params = params.astype(F32).reshape(1, 128)
    pos = z * 128 + jnp.arange(128, dtype=jnp.int32)
    inside = pos - starts[:, 0]
    frequency = ROPE_BASE ** (-(jnp.arange(32, dtype=F32) * 2.0 / 64))
    angle = inside.reshape(256, 1).astype(F32) * frequency[None, :]
    cosine, sine = jnp.cos(angle), jnp.sin(angle)
    tab = jnp.concatenate([cosine, cosine, -sine, sine], axis=1)
    begin = jnp.broadcast_to(starts.astype(F32), (2, 8, 128))
    source = inputs.reshape(256, 1024)
    upstream = cotangent.reshape(256, 1024)
    (
        whole, normed, lin_query, lin_key, keys, values, queries, probs, mixed, middle, gain, grad_gu, grad_down,
        out_part, grad_ffn, row_source, row_upstream,
    ) = forward(
        w_query, key_weight, value_weight, w_out, w_gate, w_up, w_down, source, upstream, tab, begin, params
    )
    done = backward(
        whole, normed, lin_query, lin_key, keys, values, queries, probs, mixed, middle, gain, out_part, grad_ffn,
        row_upstream, row_source, grad_gu, grad_down,
    )
    outputs, grad_inputs, d_query, d_key, d_value, d_out, d_gate, d_up, d_down, d_gains = finish(*done)
    both = dp % 4 * 32
    return (
        outputs.reshape(2, 1, 128, 1024),
        grad_inputs.reshape(2, 1, 128, 1024),
        d_query,
        d_key,
        d_value,
        d_out,
        d_gate,
        d_up,
        d_down,
        lax.dynamic_slice(d_gains, (8, both), (1, 32))[0],
        lax.dynamic_slice(d_gains, (16, both), (1, 32))[0],
        lax.dynamic_slice(d_gains, (0, 2 * dp), (1, 2))[0],
        lax.dynamic_slice(d_gains, (0, 64 + 2 * dp), (1, 2))[0],
    )


def solution(mesh):
    tokens, matrix, vector = P(None, "dp", "seq", None), P("dp", None), P("dp")
    return jax.shard_map(
        body,
        mesh=mesh,
        in_specs=(tokens, P(None, "dp", "seq")) + (matrix,) * 7 + (vector,) * 4 + (tokens,),
        out_specs=(tokens, tokens) + (matrix,) * 7 + (vector,) * 4,
        check_vma=False,
    )
```
